32 devices in a mesh: dp: 16 (over z, y, x), tensor: 2 (over core).
Axes of the slice: x: 2, y: 2, z: 4, core: 2. Of those that a mesh axis runs over, the one named last changes fastest.
Arguments:
- tokens: bfloat16 [8192, 2048], P('dp'), may hold values from -8 to 8
- segments: int32 [8192], P('dp'), may hold values from 0 to 31, never falling along the last dimension, each value on 1 to 512 neighbouring positions
- ln_gain: bfloat16 [2048], replicated, may hold values from 0.099609375 to 1.8984375
- ln_shift: bfloat16 [2048], replicated, may hold values from -1.75 to 1.75
- qkv_weight: bfloat16 [2048, 3, 2048], P('dp', None, 'tensor'), may hold values from -0.125 to 0.125
- qkv_bias: bfloat16 [3, 2048], P(None, 'tensor'), may hold values from -3 to 3
- out_weight: bfloat16 [2048, 2048], P('tensor', 'dp'), may hold values from -1 to 1
- up_weight: bfloat16 [2048, 8192], P('dp', 'tensor'), may hold values from -0.125 to 0.125
- up_bias: bfloat16 [8192], P('tensor'), may hold values from -3 to 3
- down_weight: bfloat16 [8192, 2048], P('tensor', 'dp'), may hold values from -0.0625 to 0.0625
- branch_bias: bfloat16 [2048], replicated, may hold values from -3 to 3
- cotangent: bfloat16 [8192, 2048], P('dp'), may hold values from -8 to 8
Outputs:
- result: bfloat16 [8192, 2048], P('dp')
- input_grad: float32 [8192, 2048], P('dp')
- ln_gain_grad: float32 [2048], replicated
- ln_shift_grad: float32 [2048], replicated
- qkv_weight_grad: float32 [2048, 3, 2048], P('dp', None, 'tensor')
- qkv_bias_grad: float32 [3, 2048], P(None, 'tensor')
- out_weight_grad: float32 [2048, 2048], P('tensor', 'dp')
- up_weight_grad: float32 [2048, 8192], P('dp', 'tensor')
- up_bias_grad: float32 [8192], P('tensor')
- down_weight_grad: float32 [8192, 2048], P('tensor', 'dp')
- branch_bias_grad: float32 [2048], replicated
The draws below stay inside these ranges and needn't reach their ends.
Inputs may be any that keep to these rules, and one draw needn't show every extreme that they name: `segments`: document numbers never fall along the array; each document has 1 to 512 tokens and one has exactly 512.
All inputs are finite; a program needn't handle non-finite values.
Results may differ from the reference program's by a relative error of at most 0.012.
Values may be sent and summed in bfloat16 or wider, within the bound.
No kernel may reach another device: no remote copies, remote signals or barrier semaphores. Data moves between devices by JAX's collectives and lax.ppermute only.
A program may use at most 384 MiB of HBM per device.

```python
import math
import jax
import jax.numpy as jnp
import numpy as np
from jax import lax

D = 2048
HEADS = 32
HEAD_DIM = 64
ROT_DIM = 32
FF = 8192
TOK_DEV = 512
HH = 2048
TOKENS = 8192
DOCS = 32
N_DP = 16


def spiked(array, key, source, target, blocks, factor):
    def block_of(dim):
        return (jnp.arange(array.shape[dim]) // (array.shape[dim] // blocks)).reshape((-1,) + (1,) * (array.ndim - 1 - dim))

    one_side = jax.random.permutation(key, blocks)[block_of(target)]
    second = (block_of(target) + blocks // 2) % blocks
    return jnp.where((block_of(source) == one_side) | (block_of(source) == second), factor * array, array)


def steps_of(stream_key, extent, shards, smallest, high):
    def one(position, parts):
        heights = jax.random.uniform(jax.random.fold_in(jax.random.fold_in(stream_key, 6), position), (parts,), jnp.float32, smallest / len(shards), high / len(shards))
        return jnp.repeat(jnp.exp(heights), extent[position] // parts).reshape((-1,) + (1,) * (len(extent) - position - 1))

    level = one(*shards[0])
    for cut in shards[1:]:
        level = level * one(*cut)
    return level


def split_up(count, total, limit, slope):
    weights = [(1 << 20) // math.isqrt(grade ** slope) + 1 for grade in range(2, count + 1)]
    rest, counts = total - limit - (count - 1), [1] * (count - 1)
    while rest > 0:
        free = [i for i in range(count - 1) if counts[i] < limit]
        pool, remaining = sum([weights[i] for i in free]), rest
        for i in free:
            addition = min(limit - counts[i], max(1, remaining * weights[i] // pool), rest)
            counts[i] = counts[i] + addition
            rest = rest - addition
    return np.array([limit] + counts)


def ragged(rng, count, total, most, lean):
    if count == 2:
        one = jax.random.randint(rng, (), max(1, total - most), min(most, total - 1) + 1)
        return jnp.stack([one, total - one])
    sizes = jnp.asarray(split_up(count, total, most, lean), jnp.int32)
    pairs = (count - 1) // 2
    donor, receiver = sizes[1:1 + 2 * pairs:2], sizes[2:2 + 2 * pairs:2]
    room = jnp.minimum(donor - 1, most - receiver)
    shifted = jax.random.randint(jax.random.fold_in(rng, 1), (pairs,), 0, 1 << 20) % (room + 1)
    sizes = sizes.at[1:1 + 2 * pairs:2].set(donor - shifted).at[2:2 + 2 * pairs:2].set(receiver + shifted)
    return sizes[jax.random.permutation(jax.random.fold_in(rng, 2), count)]


def scatter_about(own_key, shape, spread, most, shards=(), kind=jnp.bfloat16):
    values = spread * jax.random.normal(own_key, shape, jnp.float32)
    if shards:
        values = values * steps_of(own_key, shape, shards, -0.22, 0.18)
    return jnp.clip(values, -most, most).astype(kind)


def bell_draw_with(key, shape, spread, most, pieces, heavy, held_as=jnp.bfloat16):
    array = spread * jax.random.normal(key, shape, jnp.float32)
    if pieces:
        array = array * steps_of(key, shape, pieces, -0.22, 0.18)
    return jnp.clip(spiked(array, jax.random.fold_in(key, 3), *heavy), -most, most).astype(held_as)


def setup_inputs(seed: int = 0) -> dict:
    splits = jax.random.split(jax.random.key(seed), 13)
    tokens = bell_draw_with(splits[0], (TOKENS, D), 1.0, 8.0, ((0, 16),), (0, 1, 16, 2.0))
    segments = jnp.searchsorted(jnp.cumsum(ragged(splits[1], DOCS, TOKENS, TOK_DEV, 0)), jnp.arange(TOKENS), side="right").astype(jnp.int32)
    ln_gain = jnp.clip(1.0 + 0.18 * jax.random.normal(splits[2], (D,), jnp.float32), 0.099609375, 1.8984375).astype(jnp.bfloat16)
    ln_shift = scatter_about(splits[3], (D,), 0.3, 1.75)
    qkv_weight = scatter_about(splits[4], (D, 3, HH), D ** -0.5, 0.125, ((0, 16), (2, 2)))
    qkv_bias = scatter_about(splits[5], (3, HH), 0.5, 3.0, ((1, 2),))
    out_weight = scatter_about(splits[6], (HH, D), (HH // 64) ** -0.5, 1.0, ((0, 2), (1, 16)))
    up_weight = scatter_about(splits[7], (D, FF), D ** -0.5, 0.125, ((0, 16), (1, 2)))
    up_bias = scatter_about(splits[8], (FF,), 0.5, 3.0, ((0, 2),))
    down_weight = scatter_about(splits[9], (FF, D), FF ** -0.5, 0.0625, ((0, 2), (1, 16)))
    branch_bias = scatter_about(splits[10], (D,), 0.5, 3.0)
    cotangent = bell_draw_with(splits[11], (TOKENS, D), 1.0, 8.0, ((0, 16),), (0, 1, 16, 2.0))
    return {"tokens": tokens, "segments": segments, "ln_gain": ln_gain, "ln_shift": ln_shift, "qkv_weight": qkv_weight, "qkv_bias": qkv_bias, "out_weight": out_weight, "up_weight": up_weight, "up_bias": up_bias, "down_weight": down_weight, "branch_bias": branch_bias, "cotangent": cotangent}


NEGATIVE = -1e+30
EPSILON = 1e-05
HIGHEST = lax.Precision.HIGHEST

@jax.custom_vjp
def low(v):
    return lax.optimization_barrier(v.astype(jnp.bfloat16)).astype(jnp.float32)

@jax.custom_vjp
def low_back(v):
    return v

def low_keep(v):
    return (low(v), None)

def low_pass(kept, grad):
    return (grad,)

def back_keep(v):
    return (v, None)

def back_low(kept, grad):
    return (low(grad),)
low.defvjp(low_keep, low_pass)
low_back.defvjp(back_keep, back_low)

def doc_positions(segment_ids):
    places = jnp.arange(segment_ids.shape[0], dtype=jnp.int32)
    begins = jnp.concatenate([jnp.ones((1,), dtype=bool), segment_ids[1:] != segment_ids[:-1]])
    opening = lax.cummax(jnp.where(begins, places, 0), axis=0)
    return places - opening

def rotary_tables(places):
    halfway = ROT_DIM // 2
    freqs = 10000.0 ** (-jnp.arange(halfway, dtype=jnp.float32) * 2.0 / ROT_DIM)
    angles = places.astype(jnp.float32)[:, None] * freqs[None, :]
    return (jnp.cos(angles), jnp.sin(angles))

def rotate(vectors, cosine, sine):
    halfway = ROT_DIM // 2
    first_half = vectors[..., :halfway]
    second_half = vectors[..., halfway:ROT_DIM]
    cos_b = cosine[:, None, :]
    sin_b = sine[:, None, :]
    return jnp.concatenate([first_half * cos_b - second_half * sin_b, second_half * cos_b + first_half * sin_b, vectors[..., ROT_DIM:]], axis=-1)

def attend_sequence(operands):
    queries, key_rows, value_rows, segment_ids = operands
    places = jnp.arange(TOK_DEV, dtype=jnp.int32)
    allowed = (segment_ids[:, None] == segment_ids[None, :]) & (places[:, None] >= places[None, :])
    scores = low_back(jnp.einsum('qhd,khd->hqk', queries, key_rows, precision=HIGHEST) * HEAD_DIM ** (-0.5))
    scores = jnp.where(allowed[None], scores, NEGATIVE)
    row_max = lax.optimization_barrier(jnp.max(scores, axis=-1, keepdims=True))
    exponent = jnp.exp(scores - row_max)
    probs = low(exponent / lax.optimization_barrier(jnp.sum(exponent, axis=-1, keepdims=True)))
    return jnp.einsum('hqk,khd->qhd', probs, value_rows, precision=HIGHEST)

def reference(tokens, segments, ln_gain, ln_shift, qkv_weight, qkv_bias, out_weight, up_weight, up_bias, down_weight, branch_bias, cotangent):
    seq_segments = segments.reshape(N_DP, TOK_DEV)
    places = jax.vmap(doc_positions)(seq_segments).reshape(TOKENS)
    cosine, sine = rotary_tables(places)

    def forward(inputs, gain, shift, qkv_w, qkv_b, out_w, up_w, up_b, down_w, bias_out):
        average = lax.optimization_barrier(jnp.mean(inputs, axis=-1, keepdims=True))
        centered = inputs - average
        variance = lax.optimization_barrier(jnp.mean(centered * centered, axis=-1, keepdims=True))
        normed = low(centered * lax.rsqrt(variance + EPSILON) * gain + shift)
        qkv_pre = low_back(jnp.dot(normed, qkv_w.reshape(D, 3 * HH), precision=HIGHEST) + qkv_b.reshape(3 * HH))
        qkv_pre = qkv_pre.reshape(TOKENS, 3, HEADS, HEAD_DIM)
        queries = low(rotate(qkv_pre[:, 0], cosine, sine))
        key_rows = low(rotate(qkv_pre[:, 1], cosine, sine))
        value_rows = low(qkv_pre[:, 2])
        shape_seq = (N_DP, TOK_DEV, HEADS, HEAD_DIM)
        attn_seq = lax.map(jax.checkpoint(attend_sequence), (queries.reshape(shape_seq), key_rows.reshape(shape_seq), value_rows.reshape(shape_seq), seq_segments))
        attended = low(low_back(attn_seq.reshape(TOKENS, HH)))
        up_pre = low_back(jnp.dot(normed, up_w, precision=HIGHEST) + up_b)
        activated = low(jax.nn.gelu(up_pre, approximate=True))
        branches = jnp.dot(attended, out_w, precision=HIGHEST) + jnp.dot(activated, down_w, precision=HIGHEST)
        return inputs + branches + bias_out
    floats = tuple((item.astype(jnp.float32) for item in (tokens, ln_gain, ln_shift, qkv_weight, qkv_bias, out_weight, up_weight, up_bias, down_weight, branch_bias)))
    outputs, pull = jax.vjp(forward, *floats)
    grads = pull(cotangent.astype(jnp.float32))
    return (outputs.astype(jnp.bfloat16), grads[0], grads[1], grads[2], grads[3], grads[4], grads[5], grads[6], grads[7], grads[8], grads[9])
```

```python
import jax
import jax.numpy as jnp
from jax import lax
from jax.sharding import PartitionSpec as P

HEAD_DIM = 64
ROT_DIM = 32
NEGATIVE = -1e30
EPSILON = 1e-05
GELU_A = 0.7978845608028654
GELU_B = 0.044715
X_BIT, Y_BIT, ZL_BIT = 0, 1, 2
BF = jnp.bfloat16
F32 = jnp.float32


def doc_positions(segment_ids):
    places = jnp.arange(segment_ids.shape[-1], dtype=jnp.int32)
    begins = jnp.concatenate(
        [jnp.ones(segment_ids.shape[:-1] + (1,), bool), segment_ids[:, 1:] != segment_ids[:, :-1]],
        axis=1,
    )
    opening = lax.cummax(jnp.where(begins, places, 0), axis=1)
    return places - opening


def rotary_tables(places):
    halfway = ROT_DIM // 2
    freqs = 10000.0 ** (-jnp.arange(halfway, dtype=F32) * 2.0 / ROT_DIM)
    angles = places.astype(F32)[..., None] * freqs
    return (jnp.cos(angles), jnp.sin(angles))


def rotate(vectors, cosine, sine):
    halfway = ROT_DIM // 2
    first_half = vectors[..., :halfway]
    second_half = vectors[..., halfway:ROT_DIM]
    cos_b = cosine[:, :, None, :]
    sin_b = sine[:, :, None, :]
    return jnp.concatenate(
        [
            first_half * cos_b - second_half * sin_b,
            second_half * cos_b + first_half * sin_b,
            vectors[..., ROT_DIM:],
        ],
        axis=-1,
    )


def local_part(dp_size):
    top_bits = [b for b in range(3, dp_size.bit_length() - 1)]
    gather_bits = top_bits + [Y_BIT]

    def swap(value, bit):
        return lax.ppermute(value, "dp", [(i, i ^ (1 << bit)) for i in range(dp_size)])

    def swap_core(value):
        return lax.ppermute(value, "tensor", [(0, 1), (1, 0)])

    def ordered(bit, own, other):
        return jnp.where(bit == 0, jnp.stack([own, other]), jnp.stack([other, own]))

    def pick(value, index):
        return lax.dynamic_index_in_dim(value, index, 0, keepdims=False)

    def local(
        tokens,
        segments,
        ln_gain,
        ln_shift,
        qkv_weight,
        qkv_bias,
        out_weight,
        up_weight,
        up_bias,
        down_weight,
        branch_bias,
        cotangent,
    ):
        rows, width = tokens.shape
        half = rows // 2
        share = qkv_weight.shape[0]
        me = lax.axis_index("dp")
        core = lax.axis_index("tensor")

        def my(bit):
            return (me >> bit) & 1

        x_mine, zl_mine = my(X_BIT), my(ZL_BIT)
        block = x_mine + 2 * zl_mine
        att = qkv_weight.shape[2] // 4
        hid = up_weight.shape[1] // 4
        heads = att // HEAD_DIM

        def to_mixed(value):
            lead = value.shape[:-1]
            split = value.reshape(lead + (width // (4 * share), 2, 2 * share))
            return jnp.swapaxes(split, -3, -2).reshape(lead + (width,))

        def from_mixed(value):
            lead = value.shape[:-1]
            split = value.reshape(lead + (2, width // (4 * share), 2 * share))
            return jnp.swapaxes(split, -3, -2).reshape(lead + (width,))

        def gather_weight(piece):
            cols = piece.shape[2]
            w = piece.reshape(share, 2, 2, cols).transpose(2, 1, 0, 3)
            w = ordered(x_mine, pick(w, x_mine), swap(pick(w, 1 - x_mine), X_BIT))
            w = jnp.swapaxes(w, 0, 1)
            w = ordered(zl_mine, pick(w, zl_mine), swap(pick(w, 1 - zl_mine), ZL_BIT))
            for bit in gather_bits:
                w = ordered(my(bit), w, swap(w, bit))
            return w.reshape(width, cols)

        def scatter_grad(grad):
            cols = grad.shape[1]
            for bit in reversed(gather_bits):
                grad = grad.reshape((2, -1, cols))
                got = swap(pick(grad, 1 - my(bit)), bit)
                grad = (pick(grad, my(bit)).astype(F32) + got.astype(F32)).astype(BF)
            g = grad.reshape(2, 2, share, cols)
            g = ordered(zl_mine, pick(g, zl_mine), swap(pick(g, 1 - zl_mine), ZL_BIT))
            g = jnp.swapaxes(g, 0, 1)
            g = ordered(x_mine, pick(g, x_mine), swap(pick(g, 1 - x_mine), X_BIT))
            return g.transpose(2, 1, 0, 3).reshape(share, 4, cols).astype(F32)

        def gather_act(piece):
            a = jnp.stack([piece, swap(piece, ZL_BIT)])
            a = jnp.stack([a, swap(a, X_BIT)])
            a = a.reshape(4, half, width)
            a = ordered(core, a, swap_core(a))
            return jnp.swapaxes(a, 0, 1).reshape(4 * rows, width)

        def scatter_act(part):
            p = part.reshape(4, 2, half, width).swapaxes(0, 1)
            got = swap_core(pick(p, 1 - core).astype(BF))
            p = pick(p, core) + got.astype(F32)
            p = p.reshape(2, 2, half, width)
            p = p[0] + swap(p[1].astype(BF), X_BIT).astype(F32)
            return p[0] + swap(p[1].astype(BF), ZL_BIT).astype(F32)

        def both_cores(value):
            return ordered(core, value, swap_core(value)).reshape((rows,) + value.shape[1:])

        my_tokens = pick(tokens.reshape(2, half, width), core).astype(F32)
        my_cot = pick(cotangent.reshape(2, half, width), core)
        average = jnp.mean(my_tokens, axis=-1, keepdims=True)
        centered = my_tokens - average
        inv_std = lax.rsqrt(jnp.mean(centered * centered, axis=-1, keepdims=True) + EPSILON)
        normal_x = centered * inv_std
        gain_f = ln_gain.astype(F32)
        my_normed = (normal_x * gain_f + ln_shift.astype(F32)).astype(BF)

        qkv_full = gather_weight(
            qkv_weight.reshape(share, 3, 4, att).swapaxes(1, 2).reshape(share, 4, 3 * att)
        )
        normed = gather_act(to_mixed(my_normed))
        up_full = gather_weight(up_weight.reshape(share, 4, hid))
        cot = gather_act(to_mixed(my_cot))
        out_full = gather_weight(out_weight.T.reshape(share, 4, att))
        down_full = gather_weight(down_weight.T.reshape(share, 4, hid))

        seg = jnp.stack([segments, swap(segments, ZL_BIT)])
        seg = jnp.stack([seg, swap(seg, X_BIT)]).reshape(4, rows)
        places = doc_positions(seg)
        cosine, sine = rotary_tables(places)
        order = jnp.arange(rows, dtype=jnp.int32)
        allowed = (seg[:, :, None] == seg[:, None, :]) & (order[:, None] >= order[None, :])[None]

        my_qkv_bias = lax.dynamic_slice_in_dim(qkv_bias, block * att, att, 1).astype(F32)
        my_up_bias = lax.dynamic_slice_in_dim(up_bias, block * hid, hid, 0).astype(F32)

        qkv_pre = jnp.dot(normed, qkv_full, preferred_element_type=F32) + my_qkv_bias.reshape(-1)
        qkv_pre = qkv_pre.reshape(4, rows, 3, heads, HEAD_DIM)
        queries = rotate(qkv_pre[:, :, 0], cosine, sine).astype(BF)
        key_rows = rotate(qkv_pre[:, :, 1], cosine, sine).astype(BF)
        value_rows = qkv_pre[:, :, 2].astype(BF)
        scaling = HEAD_DIM ** (-0.5)
        scores = (
            jnp.einsum("sqhd,skhd->shqk", queries, key_rows, preferred_element_type=F32) * scaling
        )
        scores = jnp.where(allowed[:, None], scores, NEGATIVE)
        row_max = jnp.max(scores, axis=-1, keepdims=True)
        exponent = jnp.exp(scores - row_max)
        summed = jnp.sum(exponent, axis=-1, keepdims=True)
        probs = exponent / summed
        prob_low = probs.astype(BF)
        attended = (
            jnp.einsum("shqk,skhd->sqhd", prob_low, value_rows, preferred_element_type=F32)
            .astype(BF)
            .reshape(4 * rows, att)
        )

        up_pre = jnp.dot(normed, up_full, preferred_element_type=F32) + my_up_bias
        squared = up_pre * up_pre
        th = jnp.tanh(GELU_A * (up_pre + GELU_B * up_pre * squared))
        act = (0.5 * up_pre * (1.0 + th)).astype(BF)
        slope = 0.5 * (1.0 + th) + 0.5 * up_pre * (1.0 - th * th) * (
            GELU_A * (1.0 + 3.0 * GELU_B * squared)
        )

        first = (((0,), (0,)), ((), ()))
        last = (((1,), (1,)), ((), ()))
        out_grad = scatter_grad(lax.dot_general(cot, attended, first, preferred_element_type=BF))
        down_grad = scatter_grad(lax.dot_general(cot, act, first, preferred_element_type=BF))

        branches = lax.dot_general(
            attended, out_full, last, preferred_element_type=F32
        ) + lax.dot_general(act, down_full, last, preferred_element_type=F32)
        branches = from_mixed(scatter_act(branches))
        result = both_cores((my_tokens + branches + branch_bias.astype(F32)).astype(BF))

        act_grad = jnp.dot(cot, down_full, preferred_element_type=F32)
        up_g = (act_grad * slope).astype(BF)
        up_grad = scatter_grad(lax.dot_general(normed, up_g, first, preferred_element_type=BF))
        attn_grad = (
            jnp.dot(cot, out_full, preferred_element_type=F32)
            .astype(BF)
            .reshape(4, rows, heads, HEAD_DIM)
        )
        value_grad = jnp.einsum("shqk,sqhd->skhd", prob_low, attn_grad, preferred_element_type=F32)
        prob_grad = jnp.einsum("sqhd,skhd->shqk", attn_grad, value_rows, preferred_element_type=F32)
        inner = jnp.sum(probs * prob_grad, axis=-1, keepdims=True)
        score_grad = (probs * (prob_grad - inner)).astype(BF)
        query_grad = (
            jnp.einsum("shqk,skhd->sqhd", score_grad, key_rows, preferred_element_type=F32)
            * scaling
        )
        key_grad = (
            jnp.einsum("shqk,sqhd->skhd", score_grad, queries, preferred_element_type=F32) * scaling
        )
        qkv_g = (
            jnp.stack(
                [rotate(query_grad, cosine, -sine), rotate(key_grad, cosine, -sine), value_grad],
                axis=2,
            )
            .astype(BF)
            .reshape(4 * rows, 3 * att)
        )
        qkv_grad = scatter_grad(lax.dot_general(normed, qkv_g, first, preferred_element_type=BF))

        normed_grad = lax.dot_general(
            qkv_g, qkv_full, last, preferred_element_type=F32
        ) + lax.dot_general(up_g, up_full, last, preferred_element_type=F32)
        normed_grad = from_mixed(scatter_act(normed_grad))
        scaled = normed_grad * gain_f
        input_grad = my_cot.astype(F32) + inv_std * (
            scaled
            - jnp.mean(scaled, axis=-1, keepdims=True)
            - normal_x * jnp.mean(scaled * normal_x, axis=-1, keepdims=True)
        )
        input_grad = both_cores(input_grad)

        def placed(value, wide):
            full = jnp.zeros(value.shape[:-1] + (wide,), F32)
            return lax.dynamic_update_slice_in_dim(
                full, value, block * value.shape[-1], value.ndim - 1
            )

        qkv_b, up_b = lax.psum(
            (
                placed(jnp.sum(qkv_g.astype(F32), axis=0).reshape(3, att), 4 * att),
                placed(jnp.sum(up_g.astype(F32), axis=0), 4 * hid),
            ),
            "dp",
        )
        gain_g, shift_g, branch_g = lax.psum(
            (
                jnp.sum(normed_grad * normal_x, axis=0),
                jnp.sum(normed_grad, axis=0),
                jnp.sum(my_cot.astype(F32), axis=0),
            ),
            ("dp", "tensor"),
        )
        return (
            result,
            input_grad,
            gain_g,
            shift_g,
            qkv_grad.reshape(share, 4, 3, att).swapaxes(1, 2).reshape(share, 3, 4 * att),
            qkv_b,
            out_grad.reshape(share, 4 * att).T,
            up_grad.reshape(share, 4 * hid),
            up_b,
            down_grad.reshape(share, 4 * hid).T,
            branch_g,
        )

    return local


def solution(mesh):
    return jax.shard_map(
        local_part(mesh.shape["dp"]),
        mesh=mesh,
        in_specs=(
            P("dp", None),
            P("dp"),
            P(),
            P(),
            P("dp", None, "tensor"),
            P(None, "tensor"),
            P("tensor", "dp"),
            P("dp", "tensor"),
            P("tensor"),
            P("tensor", "dp"),
            P(),
            P("dp", None),
        ),
        out_specs=(
            P("dp", None),
            P("dp", None),
            P(),
            P(),
            P("dp", None, "tensor"),
            P(None, "tensor"),
            P("tensor", "dp"),
            P("dp", "tensor"),
            P("tensor"),
            P("tensor", "dp"),
            P(),
        ),
        check_vma=False,
    )
```

```python
import functools

import jax
import jax.numpy as jnp
from jax import lax
from jax.experimental import pallas as pl
from jax.experimental.pallas import tpu as pltpu
from jax.sharding import PartitionSpec as P

HEAD_DIM = 64
ROT_DIM = 32
LANES = 128
NEGATIVE = -1e30
EPSILON = 1e-05
GELU_A = 0.7978845608028654
GELU_B = 0.044715
X_BIT, Y_BIT, ZL_BIT = 0, 1, 2
BF = jnp.bfloat16
F32 = jnp.float32


def doc_positions(segment_ids):
    places = jnp.arange(segment_ids.shape[-1], dtype=jnp.int32)
    begins = jnp.concatenate(
        [jnp.ones(segment_ids.shape[:-1] + (1,), bool), segment_ids[:, 1:] != segment_ids[:, :-1]],
        axis=1,
    )
    opening = lax.cummax(jnp.where(begins, places, 0), axis=1)
    return places - opening


def dot_nt(a, b):
    return lax.dot_general(a, b, (((1,), (1,)), ((), ())), preferred_element_type=F32)


def dot_tn(a, b):
    return lax.dot_general(a, b, (((0,), (0,)), ((), ())), preferred_element_type=F32)


def attention_kernel(step, pre_ref, grad_ref, cos_ref, left_ref, right_ref, seg_q_ref, seg_k_ref, out_ref, dpre_ref):
    rows, width = grad_ref.shape
    scaling = HEAD_DIM ** (-0.5)
    cos, left, right = cos_ref[...], left_ref[...], right_ref[...]
    head_of = lax.broadcasted_iota(jnp.int32, (rows, LANES), 1) // HEAD_DIM

    def turn(v, sign):
        ahead = pltpu.roll(v, LANES - ROT_DIM // 2, 1)
        behind = pltpu.roll(v, ROT_DIM // 2, 1)
        return v * cos + sign * (ahead * left + behind * right)

    for pair in range(width // LANES):
        cols = slice(pair * LANES, (pair + 1) * LANES)
        q = turn(pre_ref[:, pair * LANES : (pair + 1) * LANES], 1.0).astype(BF)
        k = turn(pre_ref[:, width + pair * LANES : width + (pair + 1) * LANES], 1.0).astype(BF)
        v = pre_ref[:, 2 * width + pair * LANES : 2 * width + (pair + 1) * LANES].astype(BF)
        g = grad_ref[:, cols]
        dk = [None] * (rows // step)
        dv = [None] * (rows // step)
        for first in range(0, rows, step):
            seen = first + step
            allowed = seg_q_ref[0, first:seen, :] == seg_k_ref[0, :, :seen]
            allowed = allowed & (
                lax.broadcasted_iota(jnp.int32, (step, seen), 0) + first
                >= lax.broadcasted_iota(jnp.int32, (step, seen), 1)
            )
            att_both = dq_both = None
            for h in range(LANES // HEAD_DIM):
                mine = head_of[first:seen] == h
                qh = jnp.where(mine, q[first:seen], 0).astype(BF)
                gh = jnp.where(mine, g[first:seen], 0).astype(BF)
                s = jnp.where(allowed, dot_nt(qh, k[:seen]) * scaling, NEGATIVE)
                e = jnp.exp(s - jnp.max(s, axis=-1, keepdims=True))
                p = e * (1.0 / jnp.sum(e, axis=-1, keepdims=True))
                low = p.astype(BF)
                att = jnp.dot(low, v[:seen], preferred_element_type=F32)
                dp = dot_nt(gh, v[:seen])
                inner = jnp.sum(p * dp, axis=-1, keepdims=True)
                ds = (p * (dp - inner)).astype(BF)
                dq = jnp.dot(ds, k[:seen], preferred_element_type=F32)
                att_both = att if h == 0 else jnp.where(mine, att, att_both)
                dq_both = dq if h == 0 else jnp.where(mine, dq, dq_both)
                dkh = dot_tn(ds, qh)
                dvh = dot_tn(low, gh)
                for part in range(seen // step):
                    sl = slice(part * step, (part + 1) * step)
                    dk[part] = dkh[sl] if dk[part] is None else dk[part] + dkh[sl]
                    dv[part] = dvh[sl] if dv[part] is None else dv[part] + dvh[sl]
            out_ref[first:seen, cols] = att_both.astype(BF)
            dpre_ref[first:seen, cols] = turn_rows(dq_both * scaling, cos, left, right, first, seen)
        dk = jnp.concatenate(dk, axis=0) * scaling
        dpre_ref[:, width + pair * LANES : width + (pair + 1) * LANES] = turn(dk, -1.0).astype(BF)
        dpre_ref[:, 2 * width + pair * LANES : 2 * width + (pair + 1) * LANES] = jnp.concatenate(dv, axis=0).astype(BF)


def turn_rows(v, cos, left, right, first, seen):
    ahead = pltpu.roll(v, LANES - ROT_DIM // 2, 1)
    behind = pltpu.roll(v, ROT_DIM // 2, 1)
    return (v * cos[first:seen] - (ahead * left[first:seen] + behind * right[first:seen])).astype(BF)


def attention(pre, grad, cos, left, right, seg, step=512):
    count, rows = seg.shape
    width = grad.shape[1]
    row_block = lambda cols: pl.BlockSpec((rows, cols), lambda s: (s, 0))
    return pl.pallas_call(
        functools.partial(attention_kernel, step),
        grid=(count,),
        out_shape=[
            jax.ShapeDtypeStruct((count * rows, width), BF),
            jax.ShapeDtypeStruct((count * rows, 3 * width), BF),
        ],
        in_specs=[
            row_block(3 * width),
            row_block(width),
            row_block(LANES),
            row_block(LANES),
            row_block(LANES),
            pl.BlockSpec((1, rows, 1), lambda s: (s, 0, 0)),
            pl.BlockSpec((1, 1, rows), lambda s: (s, 0, 0)),
        ],
        out_specs=[row_block(width), row_block(3 * width)],
        compiler_params=pltpu.CompilerParams(vmem_limit_bytes=48 * 1024 * 1024),
        cost_estimate=pl.CostEstimate(flops=40 * 10**9, bytes_accessed=16 * 10**6, transcendentals=0),
    )(pre, grad, cos, left, right, seg[:, :, None], seg[:, None, :])


def rotary_lanes(places):
    halfway = ROT_DIM // 2
    lane = jnp.arange(LANES, dtype=jnp.int32) % HEAD_DIM
    freqs = 10000.0 ** (-(lane % halfway).astype(F32) * 2.0 / ROT_DIM)
    angles = places.astype(F32)[:, None] * freqs[None, :]
    turned = lane < ROT_DIM
    cos = jnp.where(turned, jnp.cos(angles), 1.0)
    sin = jnp.where(turned, jnp.sin(angles), 0.0)
    return cos, jnp.where(lane < halfway, -sin, 0.0), jnp.where(lane >= halfway, sin, 0.0)


def local_part(dp_size):
    top_bits = [b for b in range(3, dp_size.bit_length() - 1)]
    first = (((0,), (0,)), ((), ()))
    last = (((1,), (1,)), ((), ()))

    def swap(value, bit):
        return lax.ppermute(value, "dp", [(i, i ^ (1 << bit)) for i in range(dp_size)])

    def swap_core(value):
        return lax.ppermute(value, "tensor", [(0, 1), (1, 0)])

    def ordered(bit, own, other, axis=0):
        return jnp.where(
            bit == 0, jnp.stack([own, other], axis), jnp.stack([other, own], axis)
        )

    def pick(value, index, axis=0):
        return lax.dynamic_index_in_dim(value, index, axis, keepdims=False)

    def sync(*values):
        return lax.optimization_barrier(values)

    def local(
        tokens,
        segments,
        ln_gain,
        ln_shift,
        qkv_weight,
        qkv_bias,
        out_weight,
        up_weight,
        up_bias,
        down_weight,
        branch_bias,
        cotangent,
    ):
        rows, width = tokens.shape
        half = rows // 2
        wide = width // 2
        share = qkv_weight.shape[0]
        me = lax.axis_index("dp")
        core = lax.axis_index("tensor")
        x_mine, y_mine, zl_mine = (me >> X_BIT) & 1, (me >> Y_BIT) & 1, (me >> ZL_BIT) & 1
        block = x_mine + 2 * zl_mine
        att = qkv_weight.shape[2] // 4
        hid = up_weight.shape[1] // 4

        def to_mixed(value):
            lead = value.shape[:-1]
            split = value.reshape(lead + (width // (4 * share), 2, 2 * share))
            return jnp.swapaxes(split, -3, -2).reshape(lead + (width,))

        def from_mixed(value):
            lead = value.shape[:-1]
            split = value.reshape(lead + (2, width // (4 * share), 2 * share))
            return jnp.swapaxes(split, -3, -2).reshape(lead + (width,))

        def w_parts(piece):
            return piece.reshape(share, 2, 2, piece.shape[2]).transpose(2, 1, 0, 3)

        def w_x(w):
            return ordered(x_mine, pick(w, x_mine), swap(pick(w, 1 - x_mine), X_BIT), 1)

        def w_zl(w):
            return ordered(zl_mine, pick(w, zl_mine), swap(pick(w, 1 - zl_mine), ZL_BIT))

        def w_top(w):
            for bit in top_bits:
                w = ordered((me >> bit) & 1, w, swap(w, bit))
            return w.reshape((-1,) + w.shape[-1:])

        def w_y(w):
            return ordered(y_mine, w, swap(w, Y_BIT)).reshape(width, -1)

        def fold(grad, bit):
            grad = grad.reshape((2, -1) + grad.shape[-1:])
            mine = (me >> bit) & 1
            got = swap(pick(grad, 1 - mine), bit)
            return (pick(grad, mine).astype(F32) + got.astype(F32)).astype(BF)

        def g_y(grad):
            return fold(grad, Y_BIT)

        def g_top(grad):
            for bit in reversed(top_bits):
                grad = fold(grad, bit)
            return grad.reshape(2, 2, share, -1)

        def g_zl(grad):
            return ordered(zl_mine, pick(grad, zl_mine), swap(pick(grad, 1 - zl_mine), ZL_BIT), 1)

        def g_x(grad):
            got = swap(pick(grad, 1 - x_mine), X_BIT)
            grad = ordered(x_mine, pick(grad, x_mine), got)
            return grad.transpose(2, 1, 0, 3).reshape(share, 4, -1)

        def a_first(piece):
            return (
                jnp.stack([piece[:, :wide], swap(piece[:, :wide], ZL_BIT)]),
                jnp.stack([piece[:, wide:], swap(piece[:, wide:], X_BIT)]),
            )

        def a_second(pair):
            return (
                jnp.stack([pair[0], swap(pair[0], X_BIT)]).reshape(4, half, wide),
                jnp.stack([pair[1], swap(pair[1], ZL_BIT)], 1).reshape(4, half, wide),
            )

        def a_core(pair):
            mine = jnp.concatenate(pair, axis=-1)
            return ordered(core, mine, swap_core(mine), 1).reshape(4 * rows, width)

        def s_core(part):
            part = part.reshape(4, 2, half, width)
            got = swap_core(pick(part, 1 - core, 1).astype(BF))
            return (pick(part, core, 1) + got.astype(F32)).reshape(2, 2, half, width)

        def s_first(part):
            a, b = part[..., :wide], part[..., wide:]
            return (
                a[0] + swap(a[1].astype(BF), X_BIT).astype(F32),
                b[:, 0] + swap(b[:, 1].astype(BF), ZL_BIT).astype(F32),
            )

        def s_second(pair):
            a, b = pair
            a = a[0] + swap(a[1].astype(BF), ZL_BIT).astype(F32)
            b = b[0] + swap(b[1].astype(BF), X_BIT).astype(F32)
            return from_mixed(jnp.concatenate([a, b], axis=-1))

        def both_cores(value):
            return ordered(core, value, swap_core(value)).reshape((rows,) + value.shape[1:])

        step = hid // 2
        up_p = w_parts(up_weight.reshape(share, 4, hid))
        down_p = w_parts(down_weight.T.reshape(share, 4, hid))
        qkv_p = qkv_weight.reshape(share, 3, 4, att).swapaxes(1, 2).reshape(share, 4, 3 * att)
        att_p = w_parts(
            jnp.concatenate([qkv_p, out_weight.T.reshape(share, 4, att)], axis=2)
        )

        u0 = w_x(up_p[..., :step])
        seg = jnp.stack([segments, swap(segments, ZL_BIT)])
        seg = jnp.stack([seg, swap(seg, X_BIT)]).reshape(4, rows)
        my_tokens = pick(tokens.reshape(2, half, width), core).astype(F32)
        my_cot = pick(cotangent.reshape(2, half, width), core)
        average = jnp.mean(my_tokens, axis=-1, keepdims=True)
        centered = my_tokens - average
        inv_std = lax.rsqrt(jnp.mean(centered * centered, axis=-1, keepdims=True) + EPSILON)
        normal_x = centered * inv_std
        gain_f = ln_gain.astype(F32)
        my_normed = to_mixed((normal_x * gain_f + ln_shift.astype(F32)).astype(BF))
        u0, my_normed, up_p = sync(u0, my_normed, up_p)
        u0 = w_zl(u0)
        nh = a_first(my_normed)
        u1 = w_x(up_p[..., step:])
        cot_mixed = to_mixed(my_cot)
        u0, nh, u1, down_p, att_p, cot_mixed = sync(u0, nh, u1, down_p, att_p, cot_mixed)
        u0 = w_top(u0)
        u1 = w_zl(u1)
        nh = a_second(nh)
        dd = w_x(down_p)
        places = doc_positions(seg)
        tables = rotary_lanes(places.reshape(-1))
        u0, u1, nh, dd, att_p, cot_mixed, tables = sync(
            u0, u1, nh, dd, att_p, cot_mixed, tables
        )
        u0 = w_y(u0)
        u1 = w_top(u1)
        dd = w_zl(dd)
        aa = w_x(att_p)
        ch = a_first(cot_mixed)
        normed = a_core(nh)
        u0, u1, dd, aa, ch, normed = sync(u0, u1, dd, aa, ch, normed)
        u1 = w_y(u1)
        d0 = w_top(dd[..., :step])
        ch = a_second(ch)
        u0, u1, d0, dd, aa, ch, normed = sync(u0, u1, d0, dd, aa, ch, normed)
        d0 = w_y(d0)
        d1 = w_top(dd[..., step:])
        aa = w_zl(aa)
        cot = a_core(ch)
        my_up_bias = lax.dynamic_slice_in_dim(up_bias, block * hid, hid, 0).astype(F32)
        up_full = jnp.concatenate([u0, u1], axis=1)
        up_pre = jnp.dot(normed, up_full, preferred_element_type=F32) + my_up_bias
        squared = up_pre * up_pre
        th = jnp.tanh(GELU_A * (up_pre + GELU_B * up_pre * squared))
        act = (0.5 * up_pre * (1.0 + th)).astype(BF)
        slope = (
            0.5 * (1.0 + th)
            + 0.5 * up_pre * (1.0 - th * th) * (GELU_A * (1.0 + 3.0 * GELU_B * squared))
        ).astype(BF)
        up_full, d0, d1, aa, cot, act, slope, normed = sync(
            up_full, d0, d1, aa, cot, act, slope, normed
        )
        d1 = w_y(d1)
        a0 = w_top(aa[..., : 2 * att])
        gd = lax.dot_general(cot, act, first, preferred_element_type=BF)
        d0, d1, a0, aa, gd, cot, act, slope, normed = sync(
            d0, d1, a0, aa, gd, cot, act, slope, normed
        )
        a0 = w_y(a0)
        a1 = w_top(aa[..., 2 * att :])
        down_full = jnp.concatenate([d0, d1], axis=1)
        up_g = (jnp.dot(cot, down_full, preferred_element_type=F32) * slope.astype(F32)).astype(BF)
        gu = lax.dot_general(normed, up_g, first, preferred_element_type=BF)
        a0, a1, gd, gu, up_g, normed, cot, down_full, act = sync(
            a0, a1, gd, gu, up_g, normed, cot, down_full, act
        )
        a1 = w_y(a1)
        my_qkv_bias = lax.dynamic_slice_in_dim(qkv_bias, block * att, att, 1).astype(F32)
        part_qk = jnp.dot(normed, a0, preferred_element_type=F32) + my_qkv_bias[:2].reshape(-1)
        branches = lax.dot_general(act, down_full, last, preferred_element_type=F32)
        a1, part_qk, gd, gu, normed, cot, branches = sync(
            a1, part_qk, gd, gu, normed, cot, branches
        )
        gd0 = g_y(gd[:, :step])
        part_v = jnp.dot(normed, a1[:, :att], preferred_element_type=F32) + my_qkv_bias[2]
        attn_grad = jnp.dot(cot, a1[:, att:], preferred_element_type=BF)
        attended, qkv_g = attention(
            jnp.concatenate([part_qk, part_v], axis=1), attn_grad, *tables, seg
        )
        gd0, gd, gu, attended, qkv_g, normed, cot, branches = sync(
            gd0, gd, gu, attended, qkv_g, normed, cot, branches
        )
        gd1 = g_y(gd[:, step:])
        gd0 = g_top(gd0)
        qkv_full = jnp.concatenate([a0, a1[:, :att]], axis=1)
        normed_grad = lax.dot_general(
            qkv_g, qkv_full, last, preferred_element_type=F32
        ) + lax.dot_general(up_g, up_full, last, preferred_element_type=F32)
        gq = lax.dot_general(normed, qkv_g, first, preferred_element_type=BF)
        gd0, gd1, gu, gq, normed_grad, attended, branches, cot = sync(
            gd0, gd1, gu, gq, normed_grad, attended, branches, cot
        )
        gu0 = g_y(gu[:, :step])
        gd1 = g_top(gd1)
        gd0 = g_zl(gd0)
        normed_grad = s_core(normed_grad)
        branches = branches + lax.dot_general(
            attended, a1[:, att:], last, preferred_element_type=F32
        )
        go = lax.dot_general(cot, attended, first, preferred_element_type=BF)
        gu0, gd1, gd0, normed_grad, branches, gu, gq, go = sync(
            gu0, gd1, gd0, normed_grad, branches, gu, gq, go
        )
        gu1 = g_y(gu[:, step:])
        gu0 = g_top(gu0)
        gd1 = g_zl(gd1)
        gd0 = g_x(gd0)
        normed_grad = s_first(normed_grad)
        branches = s_core(branches)
        gu1, gu0, gd1, gd0, normed_grad, branches, gq, go = sync(
            gu1, gu0, gd1, gd0, normed_grad, branches, gq, go
        )
        ga0 = g_y(gq[:, : 2 * att])
        gu1 = g_top(gu1)
        gu0 = g_zl(gu0)
        gd1 = g_x(gd1)
        normed_grad = s_second(normed_grad)
        ga0, gu1, gu0, gd1, normed_grad, branches, gq, go = sync(
            ga0, gu1, gu0, gd1, normed_grad, branches, gq, go
        )
        ga1 = g_y(jnp.concatenate([gq[:, 2 * att :], go], axis=1))
        ga0 = g_top(ga0)
        gu1 = g_zl(gu1)
        gu0 = g_x(gu0)
        branches = s_first(branches)
        scaled = normed_grad * gain_f
        input_grad = my_cot.astype(F32) + inv_std * (
            scaled
            - jnp.mean(scaled, axis=-1, keepdims=True)
            - normal_x * jnp.mean(scaled * normal_x, axis=-1, keepdims=True)
        )
        input_grad = both_cores(input_grad)
        lines = jnp.stack(
            [
                jnp.sum(normed_grad * normal_x, axis=0),
                jnp.sum(normed_grad, axis=0),
                jnp.sum(my_cot.astype(F32), axis=0),
            ]
        )
        lines = lines + swap_core(lines)
        ga1, ga0, gu1, gu0, branches, lines = sync(ga1, ga0, gu1, gu0, branches, lines)
        ga1 = g_top(ga1)
        ga0 = g_zl(ga0)
        gu1 = g_x(gu1)
        branches = s_second(branches)
        biases = jnp.concatenate(
            [jnp.sum(qkv_g.astype(F32), axis=0), jnp.sum(up_g.astype(F32), axis=0)]
        )
        for bit in top_bits + [Y_BIT]:
            lines = lines + swap(lines, bit)
            biases = biases + swap(biases, bit)
        ga1, ga0, gu1, branches, lines, biases = sync(ga1, ga0, gu1, branches, lines, biases)
        ga1 = g_zl(ga1)
        ga0 = g_x(ga0)
        result = both_cores((my_tokens + branches + branch_bias.astype(F32)).astype(BF))
        for bit in (X_BIT, ZL_BIT):
            lines = lines + swap(lines, bit)
        biases = ordered(x_mine, biases, swap(biases, X_BIT))
        ga1, ga0, result, lines, biases = sync(ga1, ga0, result, lines, biases)
        ga1 = g_x(ga1)
        biases = ordered(zl_mine, biases, swap(biases, ZL_BIT)).reshape(4, 3 * att + hid)

        gdown = jnp.concatenate([gd0, gd1], axis=2).astype(F32).reshape(share, 4 * hid).T
        gup = jnp.concatenate([gu0, gu1], axis=2).astype(F32).reshape(share, 4 * hid)
        gqkv = jnp.concatenate([ga0, ga1[..., :att]], axis=2).astype(F32)
        gqkv = gqkv.reshape(share, 4, 3, att).swapaxes(1, 2).reshape(share, 3, 4 * att)
        gout = ga1[..., att:].astype(F32).reshape(share, 4 * att).T
        qkv_b = biases[:, : 3 * att].reshape(4, 3, att).swapaxes(0, 1).reshape(3, 4 * att)
        up_b = biases[:, 3 * att :].reshape(4 * hid)
        return (
            result,
            input_grad,
            lines[0],
            lines[1],
            gqkv,
            qkv_b,
            gout,
            gup,
            up_b,
            gdown,
            lines[2],
        )

    return local


def solution(mesh):
    return jax.shard_map(
        local_part(mesh.shape["dp"]),
        mesh=mesh,
        in_specs=(
            P("dp", None),
            P("dp"),
            P(),
            P(),
            P("dp", None, "tensor"),
            P(None, "tensor"),
            P("tensor", "dp"),
            P("dp", "tensor"),
            P("tensor"),
            P("tensor", "dp"),
            P(),
            P("dp", None),
        ),
        out_specs=(
            P("dp", None),
            P("dp", None),
            P(),
            P(),
            P("dp", None, "tensor"),
            P(None, "tensor"),
            P("tensor", "dp"),
            P("dp", "tensor"),
            P("tensor"),
            P("tensor", "dp"),
            P(),
        ),
        check_vma=False,
    )
```

```python
import functools

import jax
import jax.numpy as jnp
from jax import lax
from jax.experimental import pallas as pl
from jax.experimental.pallas import tpu as pltpu
from jax.sharding import PartitionSpec as P

HEAD_DIM = 64
ROT_DIM = 32
LANES = 128
NEGATIVE = -1e30
EPSILON = 1e-05
GELU_A = 0.7978845608028654
GELU_B = 0.044715
X_BIT, Y_BIT, ZL_BIT = 0, 1, 2
BF = jnp.bfloat16
F32 = jnp.float32


def dot_nt(a, b):
    return lax.dot_general(a, b, (((1,), (1,)), ((), ())), preferred_element_type=F32)


def dot_tn(a, b):
    return lax.dot_general(a, b, (((0,), (0,)), ((), ())), preferred_element_type=F32)


def attention_kernel(
    pre_ref, grad_ref, cos_ref, left_ref, right_ref, line_ref, column_ref, out_ref, dpre_ref
):
    half, width = grad_ref.shape[2:]
    rows = 2 * half
    scaling = HEAD_DIM ** (-0.5)

    def both(ref, cols=slice(None)):
        block = ref[:, 0, :, cols]
        return block.reshape(rows, block.shape[-1])

    cos, left, right = both(cos_ref), both(left_ref), both(right_ref)
    head_of = lax.broadcasted_iota(jnp.int32, (rows, LANES), 1) // HEAD_DIM

    def turn(v, sign):
        ahead = pltpu.roll(v, LANES - ROT_DIM // 2, 1)
        behind = pltpu.roll(v, ROT_DIM // 2, 1)
        return v * cos + sign * (ahead * left + behind * right)

    line, column = line_ref[0], column_ref[0]
    allowed = (line[:, 0:1] >= column[0:1]) & (line[:, 1:2] <= column[0:1])
    for pair in range(width // LANES):
        parts = [slice(b + pair * LANES, b + (pair + 1) * LANES) for b in (0, width, 2 * width)]
        q = turn(both(pre_ref, parts[0]), 1.0).astype(BF)
        k = turn(both(pre_ref, parts[1]), 1.0).astype(BF)
        v = both(pre_ref, parts[2]).astype(BF)
        g = both(grad_ref, parts[0])
        att = dq = dk = dv = None
        for h in range(LANES // HEAD_DIM):
            mine = head_of == h
            qh = jnp.where(mine, q, 0).astype(BF)
            gh = jnp.where(mine, g, 0).astype(BF)
            s = jnp.where(allowed, dot_nt(qh, k) * scaling, NEGATIVE)
            e = jnp.exp(s - jnp.max(s, axis=-1, keepdims=True))
            p = e * (1.0 / jnp.sum(e, axis=-1, keepdims=True))
            low = p.astype(BF)
            att_h = jnp.dot(low, v, preferred_element_type=F32)
            dp = dot_nt(gh, v)
            inner = jnp.sum(p * dp, axis=-1, keepdims=True)
            ds = (p * (dp - inner)).astype(BF)
            dq_h = jnp.dot(ds, k, preferred_element_type=F32)
            dk_h = dot_tn(ds, qh)
            dv_h = dot_tn(low, gh)
            att = att_h if h == 0 else jnp.where(mine, att_h, att)
            dq = dq_h if h == 0 else jnp.where(mine, dq_h, dq)
            dk = dk_h if h == 0 else dk + dk_h
            dv = dv_h if h == 0 else dv + dv_h
        for ref, cols, value in (
            (out_ref, parts[0], att),
            (dpre_ref, parts[0], turn(dq * scaling, -1.0)),
            (dpre_ref, parts[1], turn(dk * scaling, -1.0)),
            (dpre_ref, parts[2], dv),
        ):
            ref[:, 0, :, cols] = value.astype(BF).reshape(2, half, LANES)


def attention(pre, grad, tables, line, column):
    count, rows = column.shape[0], column.shape[2]
    half, width = rows // 2, grad.shape[1]

    def split(value):
        return value.reshape(2, count, half, value.shape[1])

    def block(cols):
        return pl.BlockSpec((2, 1, half, cols), lambda s: (0, s, 0, 0))

    attended, dpre = pl.pallas_call(
        attention_kernel,
        grid=(count,),
        out_shape=[
            jax.ShapeDtypeStruct((2, count, half, width), BF),
            jax.ShapeDtypeStruct((2, count, half, 3 * width), BF),
        ],
        in_specs=[
            block(3 * width),
            block(width),
            block(LANES),
            block(LANES),
            block(LANES),
            pl.BlockSpec((1, rows, LANES), lambda s: (s, 0, 0)),
            pl.BlockSpec((1, 8, rows), lambda s: (s, 0, 0)),
        ],
        out_specs=[block(width), block(3 * width)],
        compiler_params=pltpu.CompilerParams(vmem_limit_bytes=48 * 1024 * 1024),
        cost_estimate=pl.CostEstimate(
            flops=20 * 10**9, bytes_accessed=16 * 10**6, transcendentals=4 * 10**6
        ),
    )(split(pre), split(grad), *[split(t) for t in tables], line, column)
    return attended.reshape(2 * count * half, width), dpre.reshape(2 * count * half, 3 * width)


def rotary_lanes(places):
    halfway = ROT_DIM // 2
    lane = jnp.arange(LANES, dtype=jnp.int32) % HEAD_DIM
    freqs = 10000.0 ** (-(lane % halfway).astype(F32) * 2.0 / ROT_DIM)
    angles = places.astype(F32)[:, None] * freqs[None, :]
    turned = lane < ROT_DIM
    cos = jnp.where(turned, jnp.cos(angles), 1.0)
    sin = jnp.where(turned, jnp.sin(angles), 0.0)
    return cos, jnp.where(lane < halfway, -sin, 0.0), jnp.where(lane >= halfway, sin, 0.0)


def join_kernel(plan, *refs):
    count = len(plan)
    out_ref, sems = refs[-2], refs[-1]
    copies = [
        pltpu.make_async_copy(
            refs[which].at[pl.ds(source, size)], out_ref.at[pl.ds(target, size)], sems.at[i]
        )
        for i, (which, source, size, target) in enumerate(plan)
    ]
    for copy in copies:
        copy.start()
    for copy in copies:
        copy.wait()


def join_rows(arrays, plan):
    rows = sum(size for _, _, size, _ in plan)
    first = arrays[0]
    anywhere = pl.BlockSpec(memory_space=pl.ANY)
    return pl.pallas_call(
        functools.partial(join_kernel, plan),
        out_shape=jax.ShapeDtypeStruct((rows,) + first.shape[1:], first.dtype),
        in_specs=[anywhere] * len(arrays),
        out_specs=anywhere,
        scratch_shapes=[pltpu.SemaphoreType.DMA((len(plan),))],
        cost_estimate=pl.CostEstimate(
            flops=0, bytes_accessed=2 * rows * first.shape[1] * first.dtype.itemsize, transcendentals=0
        ),
    )(*arrays)


def place_kernel(core_ref, own_ref, other_ref, out_ref, sems):
    half = own_ref.shape[0]
    core = core_ref[0]
    copies = [
        pltpu.make_async_copy(
            ref, out_ref.at[pl.ds(pl.multiple_of(which * half, half), half)], sems.at[i]
        )
        for i, (ref, which) in enumerate(((own_ref, core), (other_ref, 1 - core)))
    ]
    for copy in copies:
        copy.start()
    for copy in copies:
        copy.wait()


def place_halves(core, own, other):
    anywhere = pl.BlockSpec(memory_space=pl.ANY)
    return pl.pallas_call(
        place_kernel,
        out_shape=jax.ShapeDtypeStruct((2 * own.shape[0],) + own.shape[1:], own.dtype),
        grid_spec=pltpu.PrefetchScalarGridSpec(
            num_scalar_prefetch=1,
            grid=(1,),
            in_specs=[anywhere] * 2,
            out_specs=anywhere,
            scratch_shapes=[pltpu.SemaphoreType.DMA((2,))],
        ),
        cost_estimate=pl.CostEstimate(
            flops=0, bytes_accessed=4 * own.size * own.dtype.itemsize, transcendentals=0
        ),
    )(core.reshape(1).astype(jnp.int32), own, other)


def pair_kernel(a_ref, b_ref, c_ref, d_ref, out_ref):
    total = dot_nt(a_ref[...], b_ref[...]) + dot_nt(c_ref[...], d_ref[...])
    out_ref[...] = total.astype(out_ref.dtype)


def pair_dot(part, parts, a, b, c, d, tile=256):
    rows, width = a.shape[0] // parts, b.shape[0]
    return pl.pallas_call(
        pair_kernel,
        grid=(width // tile,),
        out_shape=jax.ShapeDtypeStruct((rows, width), BF),
        in_specs=[
            pl.BlockSpec((rows, a.shape[1]), lambda i: (part, 0)),
            pl.BlockSpec((tile, b.shape[1]), lambda i: (i, 0)),
            pl.BlockSpec((rows, c.shape[1]), lambda i: (part, 0)),
            pl.BlockSpec((tile, d.shape[1]), lambda i: (i, 0)),
        ],
        out_specs=pl.BlockSpec((rows, tile), lambda i: (0, i)),
        compiler_params=pltpu.CompilerParams(vmem_limit_bytes=48 * 1024 * 1024),
        cost_estimate=pl.CostEstimate(
            flops=2 * rows * width * (a.shape[1] + c.shape[1]),
            bytes_accessed=2 * (rows + width) * (a.shape[1] + c.shape[1]) + 2 * rows * width,
            transcendentals=0,
        ),
    )(a, b, c, d)


def standardize(inputs):
    average = jnp.mean(inputs, axis=-1, keepdims=True)
    centered = inputs - average
    inv_std = lax.rsqrt(jnp.mean(centered * centered, axis=-1, keepdims=True) + EPSILON)
    return centered * inv_std, inv_std


def input_gradient(normed_grad, cot, normal_x, inv_std, gain):
    scaled = normed_grad * gain
    return cot + inv_std * (
        scaled
        - jnp.mean(scaled, axis=-1, keepdims=True)
        - normal_x * jnp.mean(scaled * normal_x, axis=-1, keepdims=True)
    )


def norm_kernel(table_ref, tok_ref, cot_ref, gain_ref, shift_ref, normed_ref, mixed_ref, *, cols):
    normal_x, _ = standardize(tok_ref[...].astype(F32))
    normed = (normal_x * gain_ref[...].astype(F32) + shift_ref[...].astype(F32)).astype(BF)
    for n in range(tok_ref.shape[1] // cols):
        target = pl.ds(pl.multiple_of(table_ref[n], cols), cols)
        normed_ref[:, target] = normed[:, n * cols : (n + 1) * cols]
        mixed_ref[:, target] = cot_ref[:, n * cols : (n + 1) * cols]


def natural(table_ref, kept_ref, got_ref, cols):
    parts = []
    for n in range(kept_ref.shape[1] // cols):
        source = pl.ds(pl.multiple_of(table_ref[n], cols), cols)
        parts.append(kept_ref[:, source].astype(F32) + got_ref[:, source].astype(F32))
    return jnp.concatenate(parts, axis=1)


def norm_back_kernel(
    table_ref, tok_ref, cot_ref, gain_ref, kept_ref, got_ref, grad_ref, lines_ref, *, cols
):
    normal_x, inv_std = standardize(tok_ref[...].astype(F32))
    cot = cot_ref[...].astype(F32)
    normed_grad = natural(table_ref, kept_ref, got_ref, cols)
    grad_ref[...] = input_gradient(
        normed_grad, cot, normal_x, inv_std, gain_ref[...].astype(F32)
    )

    @pl.when(pl.program_id(0) == 0)
    def _():
        lines_ref[...] = jnp.zeros_like(lines_ref)

    for row, value in enumerate((normed_grad * normal_x, normed_grad, cot)):
        lines_ref[row : row + 1, :] += jnp.sum(value, axis=0, keepdims=True)


def result_kernel(table_ref, tok_ref, bias_ref, kept_ref, got_ref, out_ref, *, cols):
    branches = natural(table_ref, kept_ref, got_ref, cols)
    out_ref[...] = (tok_ref[...].astype(F32) + branches + bias_ref[...].astype(F32)).astype(BF)


def on_half(kernel, table, cols, whole, lines, mine, outs, tile=64):
    half, width = whole[0].shape[0] // 2, whole[0].shape[1]
    steps = half // tile
    last_entry = table.shape[0] - 1
    block = pl.BlockSpec((tile, width), lambda i, t: (i, 0))
    return pl.pallas_call(
        functools.partial(kernel, cols=cols),
        out_shape=outs,
        grid_spec=pltpu.PrefetchScalarGridSpec(
            num_scalar_prefetch=1,
            grid=(steps,),
            in_specs=[pl.BlockSpec((tile, width), lambda i, t: (t[last_entry] * steps + i, 0))]
            * len(whole)
            + [pl.BlockSpec((1, width), lambda i, t: (0, 0))] * len(lines)
            + [block] * len(mine),
            out_specs=[
                block if out.shape[0] == half else pl.BlockSpec(out.shape, lambda i, t: (0, 0))
                for out in outs
            ],
        ),
        compiler_params=pltpu.CompilerParams(vmem_limit_bytes=32 * 1024 * 1024),
        cost_estimate=pl.CostEstimate(
            flops=20 * half * width, bytes_accessed=12 * half * width, transcendentals=0
        ),
    )(table, *whole, *[line.reshape(1, width) for line in lines], *mine)


def local_part(dp_size):
    top_bits = [b for b in range(3, dp_size.bit_length() - 1)]
    first = (((0,), (0,)), ((), ()))

    def swap(value, bit):
        return lax.ppermute(value, "dp", [(i, i ^ (1 << bit)) for i in range(dp_size)])

    def swap_core(value):
        return lax.ppermute(value, "tensor", [(0, 1), (1, 0)])

    def swap_mixed(value, bits):
        pairs = [(2 * i + c, 2 * (i ^ (1 << bits[c])) + c) for i in range(dp_size) for c in (0, 1)]
        return lax.ppermute(value, ("dp", "tensor"), pairs)

    def swap_first(value):
        return swap_mixed(value, (ZL_BIT, X_BIT))

    def swap_second(value):
        return swap_mixed(value, (X_BIT, ZL_BIT))

    def ordered(bit, own, other, axis):
        return jnp.where(
            bit == 0,
            jnp.concatenate([own, other], axis),
            jnp.concatenate([other, own], axis),
        )

    def part_of(value, index, axis):
        size = value.shape[axis] // 2
        return lax.dynamic_slice_in_dim(value, index * size, size, axis)

    def sync(*values):
        return lax.optimization_barrier(values)

    def local(
        tokens,
        segments,
        ln_gain,
        ln_shift,
        qkv_weight,
        qkv_bias,
        out_weight,
        up_weight,
        up_bias,
        down_weight,
        branch_bias,
        cotangent,
    ):
        rows, width = tokens.shape
        half = rows // 2
        wide = width // 2
        share = qkv_weight.shape[0]
        unit = 4 * share
        cols = 2 * share
        me = lax.axis_index("dp")
        core = lax.axis_index("tensor")
        x_mine, y_mine, zl_mine = (me >> X_BIT) & 1, (me >> Y_BIT) & 1, (me >> ZL_BIT) & 1
        block = 2 * x_mine + zl_mine
        att = qkv_weight.shape[2] // 4
        hid = up_weight.shape[1] // 4
        tops = 2 ** len(top_bits)

        n = jnp.arange(4 * tops, dtype=jnp.int32)
        table = ((((n & 1) ^ y_mine) * tops + ((n >> 2) ^ (me >> 3))) * 2 + ((n >> 1) & 1)) * cols
        table = jnp.concatenate([table, core.reshape(1)]).astype(jnp.int32)
        aligned = cols % LANES == 0

        def relative(split):
            for axis, bit in enumerate([Y_BIT] + top_bits[::-1]):
                split = jnp.where((me >> bit) & 1 == 1, jnp.flip(split, axis + 1), split)
            return split

        def to_mixed(value):
            count = value.shape[0]
            split = value.reshape(count, tops, 2, 2, cols).transpose(0, 3, 1, 2, 4)
            split = relative(split.reshape((count, 2) + (2,) * len(top_bits) + (unit,)))
            return split.reshape(count, width)

        def from_mixed(value):
            count = value.shape[0]
            split = relative(value.reshape((count, 2) + (2,) * len(top_bits) + (unit,)))
            split = split.reshape(count, 2, tops, 2, cols).transpose(0, 2, 3, 1, 4)
            return split.reshape(count, width)

        def my_rows(value):
            return lax.dynamic_slice_in_dim(value, core * half, half, 0)

        def norm_forward():
            shape = jax.ShapeDtypeStruct((half, width), BF)
            if aligned:
                return on_half(
                    norm_kernel,
                    table,
                    cols,
                    [tokens, cotangent],
                    [ln_gain, ln_shift],
                    [],
                    [shape, shape],
                )
            normal_x, _ = standardize(my_rows(tokens).astype(F32))
            normed = normal_x * ln_gain.astype(F32) + ln_shift.astype(F32)
            return to_mixed(normed.astype(BF)), to_mixed(my_rows(cotangent))

        def norm_backward(kept, got):
            if aligned:
                return on_half(
                    norm_back_kernel,
                    table,
                    cols,
                    [tokens, cotangent],
                    [ln_gain],
                    [kept, got],
                    [
                        jax.ShapeDtypeStruct((half, width), F32),
                        jax.ShapeDtypeStruct((8, width), F32),
                    ],
                )
            normal_x, inv_std = standardize(my_rows(tokens).astype(F32))
            cot = my_rows(cotangent).astype(F32)
            grad = from_mixed(add(kept, got))
            lines = jnp.stack(
                [jnp.sum(v, axis=0) for v in (grad * normal_x, grad, cot)]
                + [jnp.zeros((width,), F32)] * 5
            )
            return input_gradient(grad, cot, normal_x, inv_std, ln_gain.astype(F32)), lines

        def finish(kept, got):
            if aligned:
                return on_half(
                    result_kernel,
                    table,
                    cols,
                    [tokens],
                    [branch_bias],
                    [kept, got],
                    [jax.ShapeDtypeStruct((half, width), BF)],
                )[0]
            branches = from_mixed(add(kept, got))
            return (my_rows(tokens).astype(F32) + branches + branch_bias.astype(F32)).astype(BF)

        def w_x(piece):
            got = swap(part_of(piece, 1 - x_mine, 1), X_BIT)
            return ordered(x_mine, part_of(piece, x_mine, 1), got, 0)

        def w_zl(w):
            got = swap(part_of(w, 1 - zl_mine, 1), ZL_BIT)
            return ordered(zl_mine, part_of(w, zl_mine, 1), got, 0)

        def w_top(w):
            rest = None
            for bit in top_bits:
                mine = w if rest is None else jnp.concatenate([w, rest])
                got = swap(mine, bit)
                rest = got if rest is None else jnp.concatenate([rest, got])
            return rest

        def w_join(own, rest, far, far_rest):
            return jnp.concatenate([own, rest, far, far_rest])

        def add(*values):
            total = values[0].astype(F32)
            for value in values[1:]:
                total = total + value.astype(F32)
            return total

        def g_y(grad):
            return add(grad[:wide], swap(grad[wide:], Y_BIT)).astype(BF)

        def g_top(grad):
            for bit in reversed(top_bits):
                cut = grad.shape[0] // 2
                grad = add(grad[:cut], swap(grad[cut:], bit)).astype(BF)
            return grad

        def g_zl(grad):
            got = swap(part_of(grad, 1 - zl_mine, 0), ZL_BIT)
            return ordered(zl_mine, part_of(grad, zl_mine, 0), got, 1)

        def g_x(grad):
            got = swap(part_of(grad, 1 - x_mine, 0), X_BIT)
            return ordered(x_mine, part_of(grad, x_mine, 0), got, 1)

        def a_join(pair, second, got_pair, got_second):
            return join_rows(
                [pair, second, got_pair, got_second],
                (
                    (0, 0, 2 * half, 0),
                    (1, 0, 2 * half, 2 * half),
                    (2, 0, half, 4 * half),
                    (3, 0, half, 5 * half),
                    (2, half, half, 6 * half),
                    (3, half, half, 7 * half),
                ),
            )

        def s_join(kept, got):
            got = got.reshape(4, half, width)
            kept = kept.reshape(4, half, width)
            pair = add(kept[:2], jnp.stack([got[0], got[2]])).reshape(2 * half, width)
            send = add(kept[2:], jnp.stack([got[1], got[3]])).astype(BF).reshape(2 * half, width)
            return pair, send

        uu = w_x(up_weight)
        n_own, c_own = norm_forward()
        seg = segments.reshape(1, rows)
        seg = jnp.concatenate([seg, swap_first(seg)])
        uu, n_own, c_own, seg, qkv_weight, out_weight, down_weight = sync(
            uu, n_own, c_own, seg, qkv_weight, out_weight, down_weight
        )
        uu = w_zl(uu)
        seg = jnp.concatenate([seg, swap_second(seg)])
        n_pair = jnp.concatenate([n_own, swap_first(n_own)])
        qkv_piece = qkv_weight.reshape(share, 3, 4, att).swapaxes(1, 2).reshape(share, 4, 3 * att)
        out_piece = out_weight.T.reshape(share, 4, att)
        aa = w_x(jnp.concatenate([qkv_piece, out_piece], axis=2).reshape(share, 16 * att))
        uu, n_pair, aa, c_own, seg, down_weight = sync(uu, n_pair, aa, c_own, seg, down_weight)
        u_rest = w_top(uu)
        u_far = swap(uu, Y_BIT)
        n_second = swap_second(n_pair)
        n_got_pair = swap_core(n_pair)
        aa = w_zl(aa)
        dd = w_x(down_weight.T)
        uu, u_rest, u_far, n_pair, n_second, n_got_pair, aa, dd, c_own, seg = sync(
            uu, u_rest, u_far, n_pair, n_second, n_got_pair, aa, dd, c_own, seg
        )
        a_rest = w_top(aa)
        a_far = swap(aa, Y_BIT)
        u_far_rest = swap(u_rest, Y_BIT)
        n_got_second = swap_core(n_second)
        dd = w_zl(dd)
        c_pair = jnp.concatenate([c_own, swap_first(c_own)])
        order = jnp.broadcast_to(jnp.arange(rows, dtype=jnp.int32), (4, rows))
        begins = jnp.concatenate([jnp.ones((4, 1), bool), seg[:, 1:] != seg[:, :-1]], axis=1)
        opening = lax.cummax(jnp.where(begins, order, 0), axis=1)

        def halves(value):
            return jnp.where(core == 0, value, jnp.roll(value, half, axis=1))

        order, opening = halves(order), halves(opening)
        tables = rotary_lanes(
            (order - opening).reshape(4, 2, half).swapaxes(0, 1).reshape(4 * rows)
        )
        line = jnp.stack([order, opening], axis=2)
        line = jnp.pad(line, ((0, 0), (0, 0), (0, LANES - 2)))
        column = jnp.broadcast_to(order[:, None, :], (4, 8, rows))
        (
            uu,
            u_rest,
            u_far,
            u_far_rest,
            aa,
            a_rest,
            a_far,
            dd,
            c_pair,
            n_pair,
            n_second,
            n_got_pair,
            n_got_second,
            tables,
            line,
            column,
        ) = sync(
            uu,
            u_rest,
            u_far,
            u_far_rest,
            aa,
            a_rest,
            a_far,
            dd,
            c_pair,
            n_pair,
            n_second,
            n_got_pair,
            n_got_second,
            tables,
            line,
            column,
        )
        d_rest = w_top(dd)
        d_far = swap(dd, Y_BIT)
        a_far_rest = swap(a_rest, Y_BIT)
        c_second = swap_second(c_pair)
        c_got_pair = swap_core(c_pair)
        normed = a_join(n_pair, n_second, n_got_pair, n_got_second)
        my_up_bias = lax.dynamic_slice_in_dim(up_bias, block * hid, hid, 0).astype(F32)
        up_full = w_join(uu, u_rest, u_far, u_far_rest)
        up_pre = jnp.dot(normed, up_full, preferred_element_type=F32) + my_up_bias
        squared = up_pre * up_pre
        gate = 0.5 + 0.5 * jnp.tanh(up_pre * (GELU_A + GELU_A * GELU_B * squared))
        act_f = up_pre * gate
        act = act_f.astype(BF)
        slope = gate + act_f * (1.0 - gate) * (2.0 * GELU_A + 6.0 * GELU_A * GELU_B * squared)
        slope = slope.astype(BF)
        (
            dd,
            d_rest,
            d_far,
            aa,
            a_rest,
            a_far,
            a_far_rest,
            c_pair,
            c_second,
            c_got_pair,
            normed,
            up_full,
            act,
            slope,
        ) = sync(
            dd,
            d_rest,
            d_far,
            aa,
            a_rest,
            a_far,
            a_far_rest,
            c_pair,
            c_second,
            c_got_pair,
            normed,
            up_full,
            act,
            slope,
        )
        d_far_rest = swap(d_rest, Y_BIT)
        c_got_second = swap_core(c_second)
        a_full = w_join(aa, a_rest, a_far, a_far_rest)
        my_qkv_bias = lax.dynamic_slice_in_dim(qkv_bias, block * att, att, 1).astype(F32)
        qkv_full, out_full = a_full[:, : 3 * att], a_full[:, 3 * att :]
        pre = jnp.dot(normed, qkv_full, preferred_element_type=F32) + my_qkv_bias.reshape(-1)
        cot = a_join(c_pair, c_second, c_got_pair, c_got_second)

        def weight_grad(left, right):
            return lax.dot_general(left, right, first, preferred_element_type=F32).astype(BF)

        gd = weight_grad(cot, act)
        d_far_rest, pre, cot, gd, qkv_full, out_full = sync(
            d_far_rest, pre, cot, gd, qkv_full, out_full
        )
        gd = g_y(gd)
        attn_grad = jnp.dot(cot, out_full, preferred_element_type=F32).astype(BF)
        attended, qkv_g = attention(pre, attn_grad, tables, line, column)
        ga = jnp.concatenate([weight_grad(normed, qkv_g), weight_grad(cot, attended)], axis=1)
        gd, attended, qkv_g, ga, d_far_rest = sync(gd, attended, qkv_g, ga, d_far_rest)
        gd = g_top(gd)
        ga = g_y(ga)
        down_full = w_join(dd, d_rest, d_far, d_far_rest)
        up_g = (jnp.dot(cot, down_full, preferred_element_type=F32) * slope.astype(F32)).astype(BF)
        n_send = pair_dot(1, 2, up_g, up_full, qkv_g, qkv_full)
        n_got = swap_core(n_send)
        n_keep = pair_dot(0, 2, up_g, up_full, qkv_g, qkv_full)
        gu = weight_grad(normed, up_g)
        n_pair, n_send = s_join(n_keep, n_got)
        gd, ga, gu, n_pair, n_send, up_g, down_full = sync(
            gd, ga, gu, n_pair, n_send, up_g, down_full
        )
        ga = g_top(ga)
        gu = g_y(gu)
        gd = g_zl(gd)
        n_got = swap_second(n_send)
        b_send = pair_dot(1, 2, act, down_full, attended, out_full)
        b_got = swap_core(b_send)
        b_keep = pair_dot(0, 2, act, down_full, attended, out_full)
        biases = jnp.concatenate(
            [jnp.sum(qkv_g.astype(F32), axis=0), jnp.sum(up_g.astype(F32), axis=0)]
        )
        b_pair, b_send = s_join(b_keep, b_got)
        n_send = add(n_pair[half:], n_got[half:]).astype(BF)
        n_keep = add(n_pair[:half], n_got[:half])
        ga, gd, gu, n_send, n_keep, b_pair, b_send, biases = sync(
            ga, gd, gu, n_send, n_keep, b_pair, b_send, biases
        )
        gu = g_top(gu)
        ga = g_zl(ga)
        gd = g_x(gd)
        n_got = swap_first(n_send)
        b_got = swap_second(b_send)
        input_grad, lines = norm_backward(n_keep, n_got)
        b_send = add(b_pair[half:], b_got[half:]).astype(BF)
        b_keep = add(b_pair[:half], b_got[:half])
        gu, ga, gd, b_send, b_keep, input_grad, lines, biases = sync(
            gu, ga, gd, b_send, b_keep, input_grad, lines, biases
        )
        gu = g_zl(gu)
        ga = g_x(ga)
        b_got = swap_first(b_send)
        input_other = swap_core(input_grad)
        lines = lines[:3].reshape(-1)
        lines = lines + swap_core(lines)
        spread = lax.dynamic_update_slice_in_dim(
            jnp.zeros((4, biases.shape[0]), F32), biases[None], block, 0
        )
        lines = jnp.concatenate([lines, spread.reshape(-1)])
        for bit in top_bits + [Y_BIT]:
            lines = lines + swap(lines, bit)
        result = finish(b_keep, b_got)
        gu, ga, result, lines, input_other = sync(gu, ga, result, lines, input_other)
        gu = g_x(gu)
        result = place_halves(core, result, swap_core(result))
        input_grad = place_halves(core, input_grad, input_other)
        for bit in (X_BIT, ZL_BIT):
            lines = lines + swap(lines, bit)

        gdown = gd.astype(F32).T
        gup = gu.astype(F32)
        ga = ga.reshape(share, 4, 4 * att)
        gqkv = ga[..., : 3 * att].astype(F32)
        gqkv = gqkv.reshape(share, 4, 3, att).swapaxes(1, 2).reshape(share, 3, 4 * att)
        gout = ga[..., 3 * att :].astype(F32).reshape(share, 4 * att).T
        biases = lines[3 * width :].reshape(4, 3 * att + hid)
        qkv_b = biases[:, : 3 * att].reshape(4, 3, att).swapaxes(0, 1).reshape(3, 4 * att)
        up_b = biases[:, 3 * att :].reshape(4 * hid)
        return (
            result,
            input_grad,
            lines[:width],
            lines[width : 2 * width],
            gqkv,
            qkv_b,
            gout,
            gup,
            up_b,
            gdown,
            lines[2 * width : 3 * width],
        )

    return local


def solution(mesh):
    return jax.shard_map(
        local_part(mesh.shape["dp"]),
        mesh=mesh,
        in_specs=(
            P("dp", None),
            P("dp"),
            P(),
            P(),
            P("dp", None, "tensor"),
            P(None, "tensor"),
            P("tensor", "dp"),
            P("dp", "tensor"),
            P("tensor"),
            P("tensor", "dp"),
            P(),
            P("dp", None),
        ),
        out_specs=(
            P("dp", None),
            P("dp", None),
            P(),
            P(),
            P("dp", None, "tensor"),
            P(None, "tensor"),
            P("tensor", "dp"),
            P("dp", "tensor"),
            P("tensor"),
            P("tensor", "dp"),
            P(),
        ),
        check_vma=False,
    )
```

```python
import functools

import jax
import jax.numpy as jnp
from jax import lax
from jax.experimental import pallas as pl
from jax.experimental.pallas import tpu as pltpu
from jax.sharding import PartitionSpec as P

HEAD_DIM = 64
ROT_DIM = 32
LANES = 128
NEGATIVE = -1e30
EPSILON = 1e-05
GELU_A = 0.7978845608028654
GELU_B = 0.044715
X_BIT, Y_BIT, ZL_BIT = 0, 1, 2
BF = jnp.bfloat16
F32 = jnp.float32


def dot_nn(a, b):
    return jnp.dot(a, b, preferred_element_type=F32)


def dot_nt(a, b):
    return lax.dot_general(a, b, (((1,), (1,)), ((), ())), preferred_element_type=F32)


def dot_tn(a, b):
    return lax.dot_general(a, b, (((0,), (0,)), ((), ())), preferred_element_type=F32)


def call(kernel, outs, grid, in_specs, out_specs, *operands, prefetch=0):
    return pl.pallas_call(
        kernel,
        out_shape=outs,
        grid_spec=pltpu.PrefetchScalarGridSpec(
            num_scalar_prefetch=prefetch, grid=grid, in_specs=in_specs, out_specs=out_specs
        ),
        compiler_params=pltpu.CompilerParams(vmem_limit_bytes=54 * 1024 * 1024),
        cost_estimate=pl.CostEstimate(flops=1000, bytes_accessed=1000, transcendentals=0),
    )(*operands)


def resident(value):
    return pl.BlockSpec(value.shape, lambda *_: (0,) * value.ndim)


def wide_dot(rows, refs, cols):
    total, low = None, 0
    for ref in refs:
        high = low + ref.shape[0]
        term = dot_nn(rows[:, low:high], ref[:, cols])
        total = term if total is None else total + term
        low = high
    return total


def join_kernel(flags_ref, pair_ref, second_ref, got_pair_ref, got_second_ref, out_ref):
    i = pl.program_id(0)
    place = lax.rem(i, 4)
    for own, (p_ref, s_ref) in enumerate(
        ((pair_ref, second_ref), (got_pair_ref, got_second_ref))
    ):
        here = (i // 4) == own
        crossed = flags_ref[own] == 1
        from_pair = (place == 0) | ((place == 1) & jnp.logical_not(crossed))
        from_pair = from_pair | ((place == 2) & crossed)

        @pl.when(here & from_pair)
        def _(ref=p_ref):
            out_ref[...] = ref[...]

        @pl.when(here & jnp.logical_not(from_pair))
        def _(ref=s_ref):
            out_ref[...] = ref[...]


def join(flags, pair, second, got_pair, got_second):
    half, width = pair.shape[0] // 2, pair.shape[1]

    def spec(low, edge):
        return pl.BlockSpec((half, width), lambda i, f: (jnp.where(i - low > edge, 1, 0), 0))

    return call(
        join_kernel,
        jax.ShapeDtypeStruct((8 * half, width), pair.dtype),
        (8,),
        [spec(0, 0), spec(0, 2), spec(4, 0), spec(4, 2)],
        pl.BlockSpec((half, width), lambda i, f: (i, 0)),
        flags,
        pair,
        second,
        got_pair,
        got_second,
        prefetch=1,
    )


def place_kernel(core_ref, own_ref, other_ref, out_ref):
    steps = pl.num_programs(0) // 2

    @pl.when(pl.program_id(0) < steps)
    def _():
        out_ref[...] = own_ref[...]

    @pl.when(pl.program_id(0) >= steps)
    def _():
        out_ref[...] = other_ref[...]


def place_halves(core, own, other, steps=2):
    tile, width = own.shape[0] // steps, own.shape[1]
    return call(
        place_kernel,
        jax.ShapeDtypeStruct((2 * own.shape[0], width), own.dtype),
        (2 * steps,),
        [
            pl.BlockSpec((tile, width), lambda i, c: (jnp.minimum(i, steps - 1), 0)),
            pl.BlockSpec((tile, width), lambda i, c: (jnp.maximum(i - steps, 0), 0)),
        ],
        pl.BlockSpec((tile, width), lambda i, c: (lax.rem(i + steps * c[0], 2 * steps), 0)),
        core.reshape(1).astype(jnp.int32),
        own,
        other,
        prefetch=1,
    )


def up_kernel(rows_ref, bias_ref, *refs, chunk):
    weights, act_ref, slope_ref = refs[:-2], refs[-2], refs[-1]
    rows = rows_ref[...]
    for low in range(0, act_ref.shape[1], chunk):
        cols = slice(low, low + chunk)
        u = wide_dot(rows, weights, cols) + bias_ref[:, cols]
        squared = u * u
        gate = 0.5 + 0.5 * jnp.tanh(u * (GELU_A + GELU_A * GELU_B * squared))
        act = u * gate
        act_ref[:, cols] = act.astype(BF)
        slope = gate + act * (1.0 - gate) * (2.0 * GELU_A + 6.0 * GELU_A * GELU_B * squared)
        slope_ref[:, cols] = slope.astype(BF)


def up_project(rows, bias, weights, tile=256):
    count, hid = rows.shape[0], weights[0].shape[1]
    out = jax.ShapeDtypeStruct((count, hid), BF)
    block = pl.BlockSpec((tile, hid), lambda i: (i, 0))
    return call(
        functools.partial(up_kernel, chunk=256),
        [out, out],
        (count // tile,),
        [pl.BlockSpec((tile, rows.shape[1]), lambda i: (i, 0)), pl.BlockSpec((1, hid), lambda i: (0, 0))]
        + [resident(w) for w in weights],
        [block, block],
        rows,
        bias.reshape(1, hid),
        *weights,
    )


def add_row_sum(sum_ref, value):
    @pl.when(pl.program_id(0) == 0)
    def _():
        sum_ref[...] = jnp.zeros_like(sum_ref)

    sum_ref[0:1, :] += jnp.sum(value.astype(F32), axis=0, keepdims=True)


def up_grad_kernel(rows_ref, slope_ref, *refs):
    weights, grad_ref, sum_ref = refs[:-2], refs[-2], refs[-1]
    grad = wide_dot(rows_ref[...], weights, slice(None)) * slope_ref[...].astype(F32)
    grad = grad.astype(BF)
    grad_ref[...] = grad
    add_row_sum(sum_ref, grad)


def up_gradient(rows, slope, weights, tile=256):
    count, hid = slope.shape
    block = pl.BlockSpec((tile, hid), lambda i: (i, 0))
    return call(
        up_grad_kernel,
        [jax.ShapeDtypeStruct((count, hid), BF), jax.ShapeDtypeStruct((8, hid), F32)],
        (count // tile,),
        [pl.BlockSpec((tile, rows.shape[1]), lambda i: (i, 0)), block]
        + [resident(w) for w in weights],
        [block, pl.BlockSpec((8, hid), lambda i: (0, 0))],
        rows,
        slope,
        *weights,
    )


def weight_grad_kernel(terms, starts, *refs):
    outs = refs[2 * terms :]
    for n, out_ref in enumerate(outs):

        @pl.when((pl.program_id(0) >= starts[n]) & (pl.program_id(0) < starts[n + 1]))
        def _(out_ref=out_ref):
            low = 0
            for t in range(terms):
                value = dot_tn(refs[2 * t][...], refs[2 * t + 1][...])
                out_ref[:, low : low + value.shape[1]] = value.astype(BF)
                low = low + value.shape[1]


def weight_grads(unit, *pairs):
    width = pairs[0][0].shape[1]
    cols = sum(right.shape[1] for _, right in pairs)
    steps = width // unit
    rest = steps // 2 - 1
    sizes = [size for size in (rest, 1, rest, 1) if size]
    starts = [sum(sizes[:n]) for n in range(len(sizes) + 1)]

    def left_block(i):
        lower = i <= rest
        place = jnp.where(lower, i, i - rest - 1)
        return 0, jnp.where(place == rest, 0, place + 1) + jnp.where(lower, rest + 1, 0)

    in_specs, operands = [], []
    for left, right in pairs:
        in_specs.append(pl.BlockSpec((left.shape[0], unit), left_block))
        in_specs.append(resident(right))
        operands += [left, right]

    def out_block(n):
        return lambda i: (jnp.clip(i - starts[n], 0, sizes[n] - 1), 0)

    outs = call(
        functools.partial(weight_grad_kernel, len(pairs), starts),
        [jax.ShapeDtypeStruct((size * unit, cols), BF) for size in sizes],
        (steps,),
        in_specs,
        [pl.BlockSpec((unit, cols), out_block(n)) for n in range(len(sizes))],
        *operands,
    )
    return outs if rest else [None, outs[0], None, outs[1]]


def pair_kernel(pieces, cut, _, a_ref, c_ref, *refs):
    out_ref = refs[-1]
    a, c = a_ref[...], c_ref[...]
    low = 0
    for b_ref, d_ref in zip(refs[:pieces], refs[pieces : 2 * pieces]):
        high = low + b_ref.shape[0]
        total = dot_nt(a, b_ref[...]) + dot_nt(c, d_ref[:, cut : cut + c.shape[1]])
        out_ref[:, low:high] = total.astype(BF)
        low = high


def pair_dot(part, crossed, a, b, c, d, cut):
    rows, width = a.shape[0] // 2, sum(piece.shape[0] for piece in b)
    tile = rows // 4

    def out_block(i, f):
        return jnp.where((f[0] == 1) & (i > 0) & (i < 3), 3 - i, i), 0

    return call(
        functools.partial(pair_kernel, len(b), cut),
        jax.ShapeDtypeStruct((rows, width), BF),
        (4,),
        [
            pl.BlockSpec((tile, a.shape[1]), lambda i, f: (part * 4 + i, 0)),
            pl.BlockSpec((tile, c.shape[1]), lambda i, f: (part * 4 + i, 0)),
        ]
        + [resident(w) for w in b]
        + [resident(w) for w in d],
        pl.BlockSpec((tile, width), out_block),
        crossed.reshape(1).astype(jnp.int32),
        a,
        c,
        *b,
        *d,
        prefetch=1,
    )


def attention_kernel(
    rows_ref, cot_ref, bias_ref, cos_ref, left_ref, right_ref, line_ref, column_ref, *refs
):
    weights, (out_ref, dpre_ref, sum_ref) = refs[:-3], refs[-3:]
    half, width = out_ref.shape[2:]
    rows = 2 * half
    scaling = HEAD_DIM ** (-0.5)

    def both(ref):
        return ref[:, 0].reshape(rows, ref.shape[3])

    cos, left, right = both(cos_ref), both(left_ref), both(right_ref)
    normed, cot = both(rows_ref), both(cot_ref)
    head_of = lax.broadcasted_iota(jnp.int32, (rows, LANES), 1) // HEAD_DIM

    def turn(v, sign):
        ahead = pltpu.roll(v, LANES - ROT_DIM // 2, 1)
        behind = pltpu.roll(v, ROT_DIM // 2, 1)
        return v * cos + sign * (ahead * left + behind * right)

    line, column = line_ref[0], column_ref[0]
    allowed = (line[:, 0:1] >= column[0:1]) & (line[:, 1:2] <= column[0:1])
    pre = wide_dot(normed, weights, slice(0, 3 * width)) + bias_ref[...]
    grads = wide_dot(cot, weights, slice(3 * width, 4 * width)).astype(BF)
    dpre_all = [None] * (3 * width // LANES)
    for pair in range(width // LANES):
        parts = [slice(b + pair * LANES, b + (pair + 1) * LANES) for b in (0, width, 2 * width)]
        q = turn(pre[:, parts[0]], 1.0).astype(BF)
        k = turn(pre[:, parts[1]], 1.0).astype(BF)
        v = pre[:, parts[2]].astype(BF)
        g = grads[:, parts[0]]
        att = dq = dk = dv = None
        for h in range(LANES // HEAD_DIM):
            mine = head_of == h
            qh = jnp.where(mine, q, 0).astype(BF)
            gh = jnp.where(mine, g, 0).astype(BF)
            s = jnp.where(allowed, dot_nt(qh, k) * scaling, NEGATIVE)
            e = jnp.exp(s - jnp.max(s, axis=-1, keepdims=True))
            p = e * (1.0 / jnp.sum(e, axis=-1, keepdims=True))
            low = p.astype(BF)
            att_h = dot_nn(low, v)
            dp = dot_nt(gh, v)
            inner = jnp.sum(p * dp, axis=-1, keepdims=True)
            ds = (p * (dp - inner)).astype(BF)
            dq_h = dot_nn(ds, k)
            dk_h = dot_tn(ds, qh)
            dv_h = dot_tn(low, gh)
            att = att_h if h == 0 else jnp.where(mine, att_h, att)
            dq = dq_h if h == 0 else jnp.where(mine, dq_h, dq)
            dk = dk_h if h == 0 else dk + dk_h
            dv = dv_h if h == 0 else dv + dv_h
        out_ref[:, 0, :, parts[0]] = att.astype(BF).reshape(2, half, LANES)
        for n, value in enumerate((turn(dq * scaling, -1.0), turn(dk * scaling, -1.0), dv)):
            value = value.astype(BF)
            dpre_ref[:, 0, :, parts[n]] = value.reshape(2, half, LANES)
            dpre_all[parts[n].start // LANES] = value
    add_row_sum(sum_ref, jnp.concatenate(dpre_all, axis=1))


def attention(normed, cot, bias, tables, line, column, weights):
    count, rows = column.shape[0], column.shape[2]
    half, width = rows // 2, weights[0].shape[1] // 4

    def split(value):
        return value.reshape(2, count, half, value.shape[1])

    def block(cols):
        return pl.BlockSpec((2, 1, half, cols), lambda s: (0, s, 0, 0))

    attended, dpre, sums = call(
        attention_kernel,
        [
            jax.ShapeDtypeStruct((2, count, half, width), BF),
            jax.ShapeDtypeStruct((2, count, half, 3 * width), BF),
            jax.ShapeDtypeStruct((8, 3 * width), F32),
        ],
        (count,),
        [
            block(normed.shape[1]),
            block(cot.shape[1]),
            pl.BlockSpec((1, 3 * width), lambda s: (0, 0)),
            block(LANES),
            block(LANES),
            block(LANES),
            pl.BlockSpec((1, rows, LANES), lambda s: (s, 0, 0)),
            pl.BlockSpec((1, 8, rows), lambda s: (s, 0, 0)),
        ]
        + [resident(w) for w in weights],
        [block(width), block(3 * width), pl.BlockSpec((8, 3 * width), lambda s: (0, 0))],
        split(normed),
        split(cot),
        bias.reshape(1, 3 * width),
        *[split(t) for t in tables],
        line,
        column,
        *weights,
    )
    tokens = 2 * count * half
    return attended.reshape(tokens, width), dpre.reshape(tokens, 3 * width), sums


def rotary_lanes(places):
    halfway = ROT_DIM // 2
    lane = jnp.arange(LANES, dtype=jnp.int32) % HEAD_DIM
    freqs = 10000.0 ** (-(lane % halfway).astype(F32) * 2.0 / ROT_DIM)
    angles = places.astype(F32)[:, None] * freqs[None, :]
    turned = lane < ROT_DIM
    cos = jnp.where(turned, jnp.cos(angles), 1.0)
    sin = jnp.where(turned, jnp.sin(angles), 0.0)
    return cos, jnp.where(lane < halfway, -sin, 0.0), jnp.where(lane >= halfway, sin, 0.0)


def standardize(inputs):
    average = jnp.mean(inputs, axis=-1, keepdims=True)
    centered = inputs - average
    inv_std = lax.rsqrt(jnp.mean(centered * centered, axis=-1, keepdims=True) + EPSILON)
    return centered * inv_std, inv_std


def input_gradient(normed_grad, cot, normal_x, inv_std, gain):
    scaled = normed_grad * gain
    return cot + inv_std * (
        scaled
        - jnp.mean(scaled, axis=-1, keepdims=True)
        - normal_x * jnp.mean(scaled * normal_x, axis=-1, keepdims=True)
    )


def norm_kernel(table_ref, tok_ref, cot_ref, gain_ref, shift_ref, normed_ref, mixed_ref, *, cols):
    normal_x, _ = standardize(tok_ref[...].astype(F32))
    normed = (normal_x * gain_ref[...].astype(F32) + shift_ref[...].astype(F32)).astype(BF)
    for n in range(tok_ref.shape[1] // cols):
        target = pl.ds(pl.multiple_of(table_ref[n], cols), cols)
        normed_ref[:, target] = normed[:, n * cols : (n + 1) * cols]
        mixed_ref[:, target] = cot_ref[:, n * cols : (n + 1) * cols]


def natural(table_ref, kept_ref, got_ref, cols):
    parts = []
    for n in range(kept_ref.shape[1] // cols):
        source = pl.ds(pl.multiple_of(table_ref[n], cols), cols)
        parts.append(kept_ref[:, source].astype(F32) + got_ref[:, source].astype(F32))
    return jnp.concatenate(parts, axis=1)


def norm_back_kernel(
    table_ref, tok_ref, cot_ref, gain_ref, kept_ref, got_ref, grad_ref, lines_ref, *, cols
):
    normal_x, inv_std = standardize(tok_ref[...].astype(F32))
    cot = cot_ref[...].astype(F32)
    normed_grad = natural(table_ref, kept_ref, got_ref, cols)
    grad_ref[...] = input_gradient(
        normed_grad, cot, normal_x, inv_std, gain_ref[...].astype(F32)
    )

    @pl.when(pl.program_id(0) == 0)
    def _():
        lines_ref[...] = jnp.zeros_like(lines_ref)

    for row, value in enumerate((normed_grad * normal_x, normed_grad, cot)):
        lines_ref[row : row + 1, :] += jnp.sum(value, axis=0, keepdims=True)


def result_kernel(table_ref, tok_ref, bias_ref, kept_ref, got_ref, out_ref, *, cols):
    branches = natural(table_ref, kept_ref, got_ref, cols)
    out_ref[...] = (tok_ref[...].astype(F32) + branches + bias_ref[...].astype(F32)).astype(BF)


def on_half(kernel, table, cols, whole, lines, mine, outs, tile=64):
    half, width = whole[0].shape[0] // 2, whole[0].shape[1]
    steps = half // tile
    last_entry = table.shape[0] - 1
    block = pl.BlockSpec((tile, width), lambda i, t: (i, 0))
    return pl.pallas_call(
        functools.partial(kernel, cols=cols),
        out_shape=outs,
        grid_spec=pltpu.PrefetchScalarGridSpec(
            num_scalar_prefetch=1,
            grid=(steps,),
            in_specs=[pl.BlockSpec((tile, width), lambda i, t: (t[last_entry] * steps + i, 0))]
            * len(whole)
            + [pl.BlockSpec((1, width), lambda i, t: (0, 0))] * len(lines)
            + [block] * len(mine),
            out_specs=[
                block if out.shape[0] == half else pl.BlockSpec(out.shape, lambda i, t: (0, 0))
                for out in outs
            ],
        ),
        compiler_params=pltpu.CompilerParams(vmem_limit_bytes=32 * 1024 * 1024),
        cost_estimate=pl.CostEstimate(
            flops=1000, bytes_accessed=1000, transcendentals=0
        ),
    )(table, *whole, *[line.reshape(1, width) for line in lines], *mine)


def local_part(dp_size):
    top_bits = [b for b in range(3, dp_size.bit_length() - 1)]

    def swap(value, bit):
        return lax.ppermute(value, "dp", [(i, i ^ (1 << bit)) for i in range(dp_size)])

    def swap_core(value):
        return lax.ppermute(value, "tensor", [(0, 1), (1, 0)])

    def swap_mixed(value, bits):
        pairs = [(2 * i + c, 2 * (i ^ (1 << bits[c])) + c) for i in range(dp_size) for c in (0, 1)]
        return lax.ppermute(value, ("dp", "tensor"), pairs)

    def ordered(bit, own, other, axis):
        return jnp.where(
            bit == 0,
            jnp.concatenate([own, other], axis),
            jnp.concatenate([other, own], axis),
        )

    def part_of(value, index, axis):
        size = value.shape[axis] // 2
        return lax.dynamic_slice_in_dim(value, index * size, size, axis)

    def sync(*values):
        return lax.optimization_barrier(values)

    def local(
        tokens,
        segments,
        ln_gain,
        ln_shift,
        qkv_weight,
        qkv_bias,
        out_weight,
        up_weight,
        up_bias,
        down_weight,
        branch_bias,
        cotangent,
    ):
        rows, width = tokens.shape
        half = rows // 2
        wide = width // 2
        share = qkv_weight.shape[0]
        unit = 4 * share
        cols = 2 * share
        me = lax.axis_index("dp")
        core = lax.axis_index("tensor")
        x_mine, y_mine, zl_mine = (me >> X_BIT) & 1, (me >> Y_BIT) & 1, (me >> ZL_BIT) & 1
        block = 2 * x_mine + zl_mine
        att = qkv_weight.shape[2] // 4
        hid = up_weight.shape[1] // 4
        tops = 2 ** len(top_bits)

        n = jnp.arange(4 * tops, dtype=jnp.int32)
        table = ((((n & 1) ^ y_mine) * tops + ((n >> 2) ^ (me >> 3))) * 2 + ((n >> 1) & 1)) * cols
        table = jnp.concatenate([table, core.reshape(1)]).astype(jnp.int32)
        aligned = cols % LANES == 0

        def relative(split):
            for axis, bit in enumerate([Y_BIT] + top_bits[::-1]):
                split = jnp.where((me >> bit) & 1 == 1, jnp.flip(split, axis + 1), split)
            return split

        def to_mixed(value):
            count = value.shape[0]
            split = value.reshape(count, tops, 2, 2, cols).transpose(0, 3, 1, 2, 4)
            split = relative(split.reshape((count, 2) + (2,) * len(top_bits) + (unit,)))
            return split.reshape(count, width)

        def from_mixed(value):
            count = value.shape[0]
            split = relative(value.reshape((count, 2) + (2,) * len(top_bits) + (unit,)))
            split = split.reshape(count, 2, tops, 2, cols).transpose(0, 2, 3, 1, 4)
            return split.reshape(count, width)

        def my_rows(value):
            return lax.dynamic_slice_in_dim(value, core * half, half, 0)

        def norm_forward():
            shape = jax.ShapeDtypeStruct((half, width), BF)
            if aligned:
                return on_half(
                    norm_kernel,
                    table,
                    cols,
                    [tokens, cotangent],
                    [ln_gain, ln_shift],
                    [],
                    [shape, shape],
                )
            normal_x, _ = standardize(my_rows(tokens).astype(F32))
            normed = normal_x * ln_gain.astype(F32) + ln_shift.astype(F32)
            return to_mixed(normed.astype(BF)), to_mixed(my_rows(cotangent))

        def norm_backward(kept, got):
            if aligned:
                return on_half(
                    norm_back_kernel,
                    table,
                    cols,
                    [tokens, cotangent],
                    [ln_gain],
                    [kept, got],
                    [
                        jax.ShapeDtypeStruct((half, width), F32),
                        jax.ShapeDtypeStruct((8, width), F32),
                    ],
                )
            normal_x, inv_std = standardize(my_rows(tokens).astype(F32))
            cot = my_rows(cotangent).astype(F32)
            grad = from_mixed(add(kept, got))
            lines = jnp.stack(
                [jnp.sum(v, axis=0) for v in (grad * normal_x, grad, cot)]
                + [jnp.zeros((width,), F32)] * 5
            )
            return input_gradient(grad, cot, normal_x, inv_std, ln_gain.astype(F32)), lines

        def finish(kept, got):
            if aligned:
                return on_half(
                    result_kernel,
                    table,
                    cols,
                    [tokens],
                    [branch_bias],
                    [kept, got],
                    [jax.ShapeDtypeStruct((half, width), BF)],
                )[0]
            branches = from_mixed(add(kept, got))
            return (my_rows(tokens).astype(F32) + branches + branch_bias.astype(F32)).astype(BF)

        def w_x(piece):
            return part_of(piece, x_mine, 1), swap(part_of(piece, 1 - x_mine, 1), X_BIT)

        def w_zl(w):
            return part_of(w, zl_mine, 1), swap(part_of(w, 1 - zl_mine, 1), ZL_BIT)

        def w_top(w):
            rest = None
            for bit in top_bits:
                mine = w if rest is None else jnp.concatenate([w, rest])
                got = swap(mine, bit)
                rest = got if rest is None else jnp.concatenate([rest, got])
            return rest

        def add(*values):
            total = values[0].astype(F32)
            for value in values[1:]:
                total = total + value.astype(F32)
            return total

        def top_send(kept, got):
            if kept is None:
                return None, None
            if tops > 2:
                return add(kept, got).astype(BF), None
            cut = kept.shape[0] // 2
            return add(kept[:cut], got[:cut]).astype(BF), add(kept[cut:], got[cut:]).astype(BF)

        def g_top(rest):
            if rest is None or tops == 2:
                return None if rest is None else swap(rest, top_bits[0])
            own = jnp.zeros((unit,) + rest.shape[1:], rest.dtype)
            grad = jnp.concatenate([own, rest])
            for bit in reversed(top_bits):
                cut = grad.shape[0] // 2
                grad = add(grad[:cut], swap(grad[cut:], bit)).astype(BF)
            return grad

        def g_own(kept, got, *tops_got):
            tops_got = [value for value in tops_got if value is not None]
            if len(tops_got) > 1:
                tops_got = [jnp.concatenate(tops_got)]
            return add(kept, got, *tops_got).astype(BF)

        def g_zl(grad):
            return part_of(grad, zl_mine, 0), swap(part_of(grad, 1 - zl_mine, 0), ZL_BIT)

        def g_x(grad):
            return part_of(grad, x_mine, 0), swap(part_of(grad, 1 - x_mine, 0), X_BIT)

        def g_swap_y(value):
            return None if value is None else swap(value, Y_BIT)

        straight = jnp.zeros((2,), jnp.int32)
        crossed = jnp.stack([core, 1 - core]).astype(jnp.int32)

        u_x = w_x(up_weight)
        n_own, c_own = norm_forward()
        seg = segments.reshape(1, rows)
        u_x, c_own, qkv_weight, out_weight, down_weight = sync(
            u_x, c_own, qkv_weight, out_weight, down_weight
        )
        uu = w_zl(ordered(x_mine, *u_x, 0))
        n_got = swap(n_own, ZL_BIT)
        seg = jnp.concatenate([seg, swap(seg, ZL_BIT)])
        qkv_piece = qkv_weight.reshape(share, 3, 4, att).swapaxes(1, 2).reshape(share, 4, 3 * att)
        out_piece = out_weight.T.reshape(share, 4, att)
        a_x = w_x(jnp.concatenate([qkv_piece, out_piece], axis=2).reshape(share, 16 * att))
        d_x = w_x(down_weight.T)
        uu, n_own, n_got, a_x, d_x, c_own, seg = sync(uu, n_own, n_got, a_x, d_x, c_own, seg)
        uu = ordered(zl_mine, *uu, 0)
        u_rest = w_top(uu)
        u_far = swap(uu, Y_BIT)
        n_pair = jnp.concatenate([n_own, n_got])
        n_second = swap(n_pair, X_BIT)
        n_got_pair = swap_core(n_pair)
        aa = w_zl(ordered(x_mine, *a_x, 0))
        seg = jnp.concatenate([seg, swap(seg, X_BIT)])
        dd = ordered(x_mine, *d_x, 0)
        u_rest, u_far, n_second, n_got_pair, aa, dd, c_own, seg = sync(
            u_rest, u_far, n_second, n_got_pair, aa, dd, c_own, seg
        )
        aa = ordered(zl_mine, *aa, 0)
        a_rest = w_top(aa)
        a_far = swap(aa, Y_BIT)
        u_far_rest = g_swap_y(u_rest)
        n_got_second = swap_core(n_second)
        dd = w_zl(dd)
        c_got = swap_mixed(c_own, (ZL_BIT, X_BIT))
        order = jnp.broadcast_to(jnp.arange(rows, dtype=jnp.int32), (4, rows))
        begins = jnp.concatenate([jnp.ones((4, 1), bool), seg[:, 1:] != seg[:, :-1]], axis=1)
        opening = lax.cummax(jnp.where(begins, order, 0), axis=1)

        def halves(value):
            return jnp.where(core == 0, value, jnp.roll(value, half, axis=1))

        order, opening = halves(order), halves(opening)
        tables = rotary_lanes(
            (order - opening).reshape(4, 2, half).swapaxes(0, 1).reshape(4 * rows)
        )
        line = jnp.stack([order, opening], axis=2)
        line = jnp.pad(line, ((0, 0), (0, 0), (0, LANES - 2)))
        column = jnp.broadcast_to(order[:, None, :], (4, 8, rows))
        u_far_rest, a_rest, a_far, dd, c_own, c_got, n_got_second, tables, line, column = sync(
            u_far_rest, a_rest, a_far, dd, c_own, c_got, n_got_second, tables, line, column
        )
        dd = ordered(zl_mine, *dd, 0)
        d_rest = w_top(dd)
        d_far = swap(dd, Y_BIT)
        a_far_rest = g_swap_y(a_rest)
        c_pair = jnp.concatenate([c_own, c_got])
        c_second = swap_mixed(c_pair, (X_BIT, ZL_BIT))
        c_got_pair = swap_core(c_pair)
        normed = join(straight, n_pair, n_second, n_got_pair, n_got_second)
        my_up_bias = lax.dynamic_slice_in_dim(up_bias, block * hid, hid, 0).astype(F32)
        up_w = [w for w in (uu, u_rest, u_far, u_far_rest) if w is not None]
        act, slope = up_project(normed, my_up_bias, up_w)
        d_rest, d_far, a_far_rest, c_second, c_got_pair, normed, act, slope = sync(
            d_rest, d_far, a_far_rest, c_second, c_got_pair, normed, act, slope
        )
        d_far_rest = g_swap_y(d_rest)
        c_got_second = swap_core(c_second)
        cot = join(crossed, c_pair, c_second, c_got_pair, c_got_second)
        gd = weight_grads(unit, (cot, act))
        d_far_rest, cot, gd = sync(d_far_rest, cot, gd)
        d_a = g_swap_y(gd[0])
        my_qkv_bias = lax.dynamic_slice_in_dim(qkv_bias, block * att, att, 1).astype(F32)
        att_w = [w for w in (aa, a_rest, a_far, a_far_rest) if w is not None]
        attended, qkv_g, qkv_sums = attention(
            normed, cot, my_qkv_bias, tables, line, column, att_w
        )
        d_a, gd, attended, qkv_g, d_far_rest = sync(d_a, gd, attended, qkv_g, d_far_rest)
        d_z1, d_z2 = top_send(gd[2], d_a)
        d_z1 = g_top(d_z1)
        d_b = swap(gd[1], Y_BIT)
        ga = weight_grads(unit, (normed, qkv_g), (cot, attended))
        d_z1, d_z2, d_b, ga, cot, slope = sync(d_z1, d_z2, d_b, ga, cot, slope)
        d_z2 = g_top(d_z2)
        a_a = g_swap_y(ga[0])
        down_w = [w for w in (dd, d_rest, d_far, d_far_rest) if w is not None]
        up_g, up_sums = up_gradient(cot, slope, down_w)
        n_send = pair_dot(1, 1 - core, up_g, up_w, qkv_g, att_w, 0)
        d_z2, a_a, ga, up_g, n_send = sync(d_z2, a_a, ga, up_g, n_send)
        d_l = g_zl(g_own(gd[3], d_b, d_z1, d_z2))
        a_z1, a_z2 = top_send(ga[2], a_a)
        a_z1 = g_top(a_z1)
        a_b = swap(ga[1], Y_BIT)
        n_got = swap_core(n_send)
        gu = weight_grads(unit, (normed, up_g))
        n_kept = pair_dot(0, core, up_g, up_w, qkv_g, att_w, 0)
        d_l, a_z1, a_z2, a_b, gu, n_got, n_kept, act, attended = sync(
            d_l, a_z1, a_z2, a_b, gu, n_got, n_kept, act, attended
        )
        n_second = swap_mixed(add(n_kept[2 * half :], n_got[2 * half :]).astype(BF), (X_BIT, ZL_BIT))
        a_z2 = g_top(a_z2)
        u_a = g_swap_y(gu[0])
        d_x = g_x(ordered(zl_mine, *d_l, 1))
        b_send = pair_dot(1, 1 - core, act, down_w, attended, att_w, 3 * att)
        a_z2, u_a, gu, d_x, n_second, b_send, act, attended = sync(
            a_z2, u_a, gu, d_x, n_second, b_send, act, attended
        )
        n_first = add(n_kept[half : 2 * half], n_got[half : 2 * half], n_second[half:])
        n_first = swap_mixed(n_first.astype(BF), (ZL_BIT, X_BIT))
        u_z1, u_z2 = top_send(gu[2], u_a)
        u_z1 = g_top(u_z1)
        u_b = swap(gu[1], Y_BIT)
        a_l = g_zl(g_own(ga[3], a_b, a_z1, a_z2))
        b_got = swap_core(b_send)
        b_kept = pair_dot(0, core, act, down_w, attended, att_w, 3 * att)
        n_keep = add(n_kept[:half], n_got[:half], n_second[:half])
        u_z1, u_z2, u_b, a_l, n_first, n_keep, b_got, b_kept = sync(
            u_z1, u_z2, u_b, a_l, n_first, n_keep, b_got, b_kept
        )
        b_second = swap_mixed(add(b_kept[2 * half :], b_got[2 * half :]).astype(BF), (X_BIT, ZL_BIT))
        u_z2 = g_top(u_z2)
        a_x = g_x(ordered(zl_mine, *a_l, 1))
        input_grad, lines = norm_backward(n_keep, n_first)
        input_other = swap_core(input_grad)
        lines = lines[:3].reshape(-1)
        lines = lines + swap_core(lines)
        biases = jnp.concatenate([qkv_sums[0], up_sums[0]])
        spread = lax.dynamic_update_slice_in_dim(
            jnp.zeros((4, biases.shape[0]), F32), biases[None], block, 0
        )
        lines = jnp.concatenate([lines, spread.reshape(-1)])
        for bit in top_bits + [Y_BIT]:
            lines = lines + swap(lines, bit)
        u_z2, a_x, b_second, input_grad, input_other, lines = sync(
            u_z2, a_x, b_second, input_grad, input_other, lines
        )
        b_first = add(b_kept[half : 2 * half], b_got[half : 2 * half], b_second[half:])
        b_first = swap_mixed(b_first.astype(BF), (ZL_BIT, X_BIT))
        u_l = g_zl(g_own(gu[3], u_b, u_z1, u_z2))
        b_keep = add(b_kept[:half], b_got[:half], b_second[:half])
        input_grad = place_halves(core, input_grad, input_other)
        lines = lines + swap(lines, X_BIT)
        lines = lines + swap(lines, ZL_BIT)
        ga = ordered(x_mine, *a_x, 1)
        gd = ordered(x_mine, *d_x, 1)
        u_l, b_first, b_keep, lines = sync(u_l, b_first, b_keep, lines)
        gu = g_x(ordered(zl_mine, *u_l, 1))
        result = finish(b_keep, b_first)
        result = place_halves(core, result, swap_core(result))
        gu = ordered(x_mine, *gu, 1)

        gdown = gd.astype(F32).T
        gup = gu.astype(F32)
        ga = ga.reshape(share, 4, 4 * att)
        gqkv = ga[..., : 3 * att].astype(F32)
        gqkv = gqkv.reshape(share, 4, 3, att).swapaxes(1, 2).reshape(share, 3, 4 * att)
        gout = ga[..., 3 * att :].astype(F32).reshape(share, 4 * att).T
        biases = lines[3 * width :].reshape(4, 3 * att + hid)
        qkv_b = biases[:, : 3 * att].reshape(4, 3, att).swapaxes(0, 1).reshape(3, 4 * att)
        up_b = biases[:, 3 * att :].reshape(4 * hid)
        return (
            result,
            input_grad,
            lines[:width],
            lines[width : 2 * width],
            gqkv,
            qkv_b,
            gout,
            gup,
            up_b,
            gdown,
            lines[2 * width : 3 * width],
        )

    return local


def solution(mesh):
    return jax.shard_map(
        local_part(mesh.shape["dp"]),
        mesh=mesh,
        in_specs=(
            P("dp", None),
            P("dp"),
            P(),
            P(),
            P("dp", None, "tensor"),
            P(None, "tensor"),
            P("tensor", "dp"),
            P("dp", "tensor"),
            P("tensor"),
            P("tensor", "dp"),
            P(),
            P("dp", None),
        ),
        out_specs=(
            P("dp", None),
            P("dp", None),
            P(),
            P(),
            P("dp", None, "tensor"),
            P(None, "tensor"),
            P("tensor", "dp"),
            P("dp", "tensor"),
            P("tensor"),
            P("tensor", "dp"),
            P(),
        ),
        check_vma=False,
    )
```

```python
import functools

import jax
import jax.numpy as jnp
from jax import lax
from jax.experimental import pallas as pl
from jax.experimental.pallas import tpu as pltpu
from jax.sharding import PartitionSpec as P

HEAD_DIM = 64
ROT_DIM = 32
LANES = 128
NEGATIVE = -1e30
EPSILON = 1e-05
GELU_A = 0.7978845608028654
GELU_B = 0.044715
X_BIT, Y_BIT, ZL_BIT = 0, 1, 2
BF = jnp.bfloat16
F32 = jnp.float32


def dot_nn(a, b):
    return jnp.dot(a, b, preferred_element_type=F32)


def dot_nt(a, b):
    return lax.dot_general(a, b, (((1,), (1,)), ((), ())), preferred_element_type=F32)


def dot_tn(a, b):
    return lax.dot_general(a, b, (((0,), (0,)), ((), ())), preferred_element_type=F32)


def call(kernel, outs, grid, in_specs, out_specs, *operands, prefetch=0):
    return pl.pallas_call(
        kernel,
        out_shape=outs,
        grid_spec=pltpu.PrefetchScalarGridSpec(
            num_scalar_prefetch=prefetch, grid=grid, in_specs=in_specs, out_specs=out_specs
        ),
        compiler_params=pltpu.CompilerParams(vmem_limit_bytes=54 * 1024 * 1024),
        cost_estimate=pl.CostEstimate(flops=1000, bytes_accessed=1000, transcendentals=0),
    )(*operands)


def resident(value):
    return pl.BlockSpec(value.shape, lambda *_: (0,) * value.ndim)


def wide_dot(rows, refs, cols):
    total, low = None, 0
    for ref in refs:
        high = low + ref.shape[0]
        term = dot_nn(rows[:, low:high], ref[:, cols])
        total = term if total is None else total + term
        low = high
    return total


def sum_kernel(*refs):
    total = refs[0][...].astype(F32)
    for ref in refs[1:-1]:
        total = total + ref[...].astype(F32)
    refs[-1][...] = total.astype(BF)


def sum_rows(rows, *terms, tile=128):
    width = terms[0][0].shape[1]
    tile = min(tile, rows)

    def spec(start):
        return pl.BlockSpec((tile, width), lambda i: (start // tile + i, 0))

    return call(
        sum_kernel,
        jax.ShapeDtypeStruct((rows, width), BF),
        (rows // tile,),
        [spec(start) for _, start in terms],
        spec(0),
        *[value for value, _ in terms],
    )


def split_kernel(flag_ref, kept_ref, got_ref, one_ref, two_ref, send_ref, own_ref):
    sending = pl.program_id(0) == 0
    upper = (flag_ref[0] == 1) != sending
    total = kept_ref[...].astype(F32) + got_ref[...].astype(F32)
    total = total + jnp.where(upper, two_ref[...], one_ref[...]).astype(F32)

    @pl.when(sending)
    def _():
        send_ref[...] = total.astype(BF)

    @pl.when(jnp.logical_not(sending))
    def _():
        own_ref[...] = total.astype(BF)


def split_sum(flag, kept, got, one, two):
    rows, cols = one.shape
    out = jax.ShapeDtypeStruct((rows, cols), BF)
    picked = pl.BlockSpec((rows, cols), lambda i, f: (jnp.where(i == 0, 1 - f[0], f[0]), 0))
    return call(
        split_kernel,
        [out, out],
        (2,),
        [picked, picked, resident(one), resident(two)],
        [pl.BlockSpec((rows, cols), lambda i, f: (0, 0))] * 2,
        flag.reshape(1).astype(jnp.int32),
        kept,
        got,
        one,
        two,
        prefetch=1,
    )


def cross_kernel(flags_ref, own_ref, got_ref, send_ref, kept_ref):
    cols = own_ref.shape[1]
    for n, out_ref in enumerate((send_ref, kept_ref)):

        @pl.when(pl.program_id(0) == n)
        def _(out_ref=out_ref):
            for ref, place in ((own_ref, flags_ref[0]), (got_ref, 1 - flags_ref[0])):
                out_ref[:, pl.ds(pl.multiple_of(place * cols, cols), cols)] = ref[...]


def cross(zl, x, own, got):
    rows, cols = own.shape[0] // 2, own.shape[1]
    out = jax.ShapeDtypeStruct((rows, 2 * cols), BF)
    picked = pl.BlockSpec((rows, cols), lambda i, f: (jnp.where(i == 0, 1 - f[1], f[1]), 0))
    return call(
        cross_kernel,
        [out, out],
        (2,),
        [picked, picked],
        [pl.BlockSpec((rows, 2 * cols), lambda i, f: (0, 0))] * 2,
        jnp.stack([zl, x]).astype(jnp.int32),
        own,
        got,
        prefetch=1,
    )


def join_kernel(flags_ref, pair_ref, second_ref, got_pair_ref, got_second_ref, out_ref):
    i = pl.program_id(0)
    place = lax.rem(i, 4)
    for own, (p_ref, s_ref) in enumerate(
        ((pair_ref, second_ref), (got_pair_ref, got_second_ref))
    ):
        here = (i // 4) == own
        crossed = flags_ref[own] == 1
        from_pair = (place == 0) | ((place == 1) & jnp.logical_not(crossed))
        from_pair = from_pair | ((place == 2) & crossed)

        @pl.when(here & from_pair)
        def _(ref=p_ref):
            out_ref[...] = ref[...]

        @pl.when(here & jnp.logical_not(from_pair))
        def _(ref=s_ref):
            out_ref[...] = ref[...]


def join(flags, pair, second, got_pair, got_second):
    half, width = pair.shape[0] // 2, pair.shape[1]

    def spec(low, edge):
        return pl.BlockSpec((half, width), lambda i, f: (jnp.where(i - low > edge, 1, 0), 0))

    return call(
        join_kernel,
        jax.ShapeDtypeStruct((8 * half, width), pair.dtype),
        (8,),
        [spec(0, 0), spec(0, 2), spec(4, 0), spec(4, 2)],
        pl.BlockSpec((half, width), lambda i, f: (i, 0)),
        flags,
        pair,
        second,
        got_pair,
        got_second,
        prefetch=1,
    )


def place_kernel(core_ref, own_ref, other_ref, out_ref):
    steps = pl.num_programs(0) // 2

    @pl.when(pl.program_id(0) < steps)
    def _():
        out_ref[...] = own_ref[...]

    @pl.when(pl.program_id(0) >= steps)
    def _():
        out_ref[...] = other_ref[...]


def place_halves(core, own, other, steps=2, rows=None):
    rows, width = rows or own.shape[0], own.shape[1]
    tile = rows // steps
    return call(
        place_kernel,
        jax.ShapeDtypeStruct((2 * rows, width), own.dtype),
        (2 * steps,),
        [
            pl.BlockSpec((tile, width), lambda i, c: (jnp.minimum(i, steps - 1), 0)),
            pl.BlockSpec((tile, width), lambda i, c: (jnp.maximum(i - steps, 0), 0)),
        ],
        pl.BlockSpec((tile, width), lambda i, c: (lax.rem(i + steps * c[0], 2 * steps), 0)),
        core.reshape(1).astype(jnp.int32),
        own,
        other,
        prefetch=1,
    )


def up_kernel(rows_ref, bias_ref, *refs, chunk):
    weights, act_ref, slope_ref = refs[:-2], refs[-2], refs[-1]
    rows = rows_ref[...]
    for low in range(0, act_ref.shape[1], chunk):
        cols = slice(low, low + chunk)
        u = wide_dot(rows, weights, cols) + bias_ref[:, cols]
        squared = u * u
        gate = 0.5 + 0.5 * jnp.tanh(u * (GELU_A + GELU_A * GELU_B * squared))
        act = u * gate
        act_ref[:, cols] = act.astype(BF)
        slope = gate + act * (1.0 - gate) * (2.0 * GELU_A + 6.0 * GELU_A * GELU_B * squared)
        slope_ref[:, cols] = slope.astype(BF)


def up_project(rows, bias, weights, tile=256):
    count, hid = rows.shape[0], weights[0].shape[1]
    out = jax.ShapeDtypeStruct((count, hid), BF)
    block = pl.BlockSpec((tile, hid), lambda i: (i, 0))
    return call(
        functools.partial(up_kernel, chunk=256),
        [out, out],
        (count // tile,),
        [pl.BlockSpec((tile, rows.shape[1]), lambda i: (i, 0)), pl.BlockSpec((1, hid), lambda i: (0, 0))]
        + [resident(w) for w in weights],
        [block, block],
        rows,
        bias.reshape(1, hid),
        *weights,
    )


def add_row_sum(sum_ref, value):
    @pl.when(pl.program_id(0) == 0)
    def _():
        sum_ref[...] = jnp.zeros_like(sum_ref)

    sum_ref[0:1, :] += jnp.sum(value.astype(F32), axis=0, keepdims=True)


def up_grad_kernel(rows_ref, slope_ref, *refs):
    weights, grad_ref, sum_ref = refs[:-2], refs[-2], refs[-1]
    grad = wide_dot(rows_ref[...], weights, slice(None)) * slope_ref[...].astype(F32)
    grad = grad.astype(BF)
    grad_ref[...] = grad
    add_row_sum(sum_ref, grad)


def up_gradient(rows, slope, weights, tile=256):
    count, hid = slope.shape
    block = pl.BlockSpec((tile, hid), lambda i: (i, 0))
    return call(
        up_grad_kernel,
        [jax.ShapeDtypeStruct((count, hid), BF), jax.ShapeDtypeStruct((8, hid), F32)],
        (count // tile,),
        [pl.BlockSpec((tile, rows.shape[1]), lambda i: (i, 0)), block]
        + [resident(w) for w in weights],
        [block, pl.BlockSpec((8, hid), lambda i: (0, 0))],
        rows,
        slope,
        *weights,
    )


def weight_grad_kernel(terms, starts, *refs):
    outs = refs[2 * terms :]
    for n, out_ref in enumerate(outs):

        @pl.when((pl.program_id(0) >= starts[n]) & (pl.program_id(0) < starts[n + 1]))
        def _(out_ref=out_ref):
            low = 0
            for t in range(terms):
                value = dot_tn(refs[2 * t][...], refs[2 * t + 1][...])
                out_ref[:, low : low + value.shape[1]] = value.astype(BF)
                low = low + value.shape[1]


def weight_grads(unit, parts, *pairs):
    width = pairs[0][0].shape[1]
    cols = sum(right.shape[1] for _, right in pairs)
    tops = width // unit // 2
    every = ((tops + 1, tops - 1), (tops, 1), (1, tops - 1), (0, 1))
    sizes = [every[part][1] for part in parts]
    starts = [sum(sizes[:n]) for n in range(len(sizes) + 1)]

    def left_block(i):
        place = i
        for n, part in enumerate(parts):
            place = jnp.where(i >= starts[n], i - starts[n] + every[part][0], place)
        return 0, place

    in_specs, operands = [], []
    for left, right in pairs:
        in_specs.append(pl.BlockSpec((left.shape[0], unit), left_block))
        in_specs.append(resident(right))
        operands += [left, right]

    def out_block(n):
        return lambda i: (jnp.clip(i - starts[n], 0, sizes[n] - 1), 0)

    return call(
        functools.partial(weight_grad_kernel, len(pairs), starts),
        [jax.ShapeDtypeStruct((size * unit, cols), BF) for size in sizes],
        (starts[-1],),
        in_specs,
        [pl.BlockSpec((unit, cols), out_block(n)) for n in range(len(sizes))],
        *operands,
    )


def pair_kernel(pieces, adding, _, a_ref, c_ref, *refs):
    a, c = a_ref[...], c_ref[...]
    outs = refs[2 * pieces + adding :]

    def into(out_ref):
        low = 0
        for b_ref, d_ref in zip(refs[:pieces], refs[pieces : 2 * pieces]):
            high = low + b_ref.shape[0]
            total = dot_nt(a, b_ref[...]) + dot_nt(c, d_ref[...])
            if adding:
                total = total + refs[2 * pieces][:, low:high].astype(F32)
            out_ref[:, low:high] = total.astype(BF)
            low = high

    steps = 4 // len(outs)
    for n, out_ref in enumerate(outs):
        pl.when(pl.program_id(0) // steps == n)(functools.partial(into, out_ref))


def pair_dot(part, crossed, a, b, c, d, cut, got=None):
    rows, width = a.shape[0] // 2, sum(piece.shape[0] for piece in b)
    tile = rows // 4
    adding = got is not None

    def row_block(i, f):
        return part * 4 + jnp.where((f[0] == 1) & (i > 0) & (i < 3), 3 - i, i), 0

    count = 2 if adding else 1
    steps = 4 // count

    def out_block(n):
        return lambda i, f: (jnp.clip(i - n * steps, 0, steps - 1), 0)

    outs = call(
        functools.partial(pair_kernel, len(b), int(adding)),
        [jax.ShapeDtypeStruct((rows // count, width), BF)] * count,
        (4,),
        [pl.BlockSpec((tile, a.shape[1]), row_block), pl.BlockSpec((tile, c.shape[1]), row_block)]
        + [resident(w) for w in b]
        + [pl.BlockSpec((w.shape[0], c.shape[1]), lambda i, f: (0, cut // c.shape[1])) for w in d]
        + [pl.BlockSpec((tile, width), lambda i, f: (i, 0))] * int(adding),
        [pl.BlockSpec((tile, width), out_block(n)) for n in range(count)],
        crossed.reshape(1).astype(jnp.int32),
        a,
        c,
        *b,
        *d,
        *([got] if adding else []),
        prefetch=1,
    )
    return outs if adding else outs[0]


def attention_kernel(
    rows_ref, cot_ref, bias_ref, cos_ref, left_ref, right_ref, line_ref, column_ref, *refs
):
    weights, (out_ref, dpre_ref, sum_ref) = refs[:-3], refs[-3:]
    half, width = out_ref.shape[2:]
    rows = 2 * half
    scaling = HEAD_DIM ** (-0.5)

    def both(ref):
        return ref[:, 0].reshape(rows, ref.shape[3])

    cos, left, right = both(cos_ref), both(left_ref), both(right_ref)
    normed, cot = both(rows_ref), both(cot_ref)
    head_of = lax.broadcasted_iota(jnp.int32, (rows, LANES), 1) // HEAD_DIM

    def turn(v, sign):
        ahead = pltpu.roll(v, LANES - ROT_DIM // 2, 1)
        behind = pltpu.roll(v, ROT_DIM // 2, 1)
        return v * cos + sign * (ahead * left + behind * right)

    line, column = line_ref[0], column_ref[0]
    allowed = (line[:, 0:1] >= column[0:1]) & (line[:, 1:2] <= column[0:1])
    pre = wide_dot(normed, weights, slice(0, 3 * width)) + bias_ref[...]
    grads = wide_dot(cot, weights, slice(3 * width, 4 * width)).astype(BF)
    dpre_all = [None] * (3 * width // LANES)
    for pair in range(width // LANES):
        parts = [slice(b + pair * LANES, b + (pair + 1) * LANES) for b in (0, width, 2 * width)]
        q = turn(pre[:, parts[0]], 1.0).astype(BF)
        k = turn(pre[:, parts[1]], 1.0).astype(BF)
        v = pre[:, parts[2]].astype(BF)
        g = grads[:, parts[0]]
        att = dq = dk = dv = None
        for h in range(LANES // HEAD_DIM):
            mine = head_of == h
            qh = jnp.where(mine, q, 0).astype(BF)
            gh = jnp.where(mine, g, 0).astype(BF)
            s = jnp.where(allowed, dot_nt(qh, k) * scaling, NEGATIVE)
            e = jnp.exp(s - jnp.max(s, axis=-1, keepdims=True))
            p = e * (1.0 / jnp.sum(e, axis=-1, keepdims=True))
            low = p.astype(BF)
            att_h = dot_nn(low, v)
            dp = dot_nt(gh, v)
            inner = jnp.sum(p * dp, axis=-1, keepdims=True)
            ds = (p * (dp - inner)).astype(BF)
            dq_h = dot_nn(ds, k)
            dk_h = dot_tn(ds, qh)
            dv_h = dot_tn(low, gh)
            att = att_h if h == 0 else jnp.where(mine, att_h, att)
            dq = dq_h if h == 0 else jnp.where(mine, dq_h, dq)
            dk = dk_h if h == 0 else dk + dk_h
            dv = dv_h if h == 0 else dv + dv_h
        out_ref[:, 0, :, parts[0]] = att.astype(BF).reshape(2, half, LANES)
        for n, value in enumerate((turn(dq * scaling, -1.0), turn(dk * scaling, -1.0), dv)):
            value = value.astype(BF)
            dpre_ref[:, 0, :, parts[n]] = value.reshape(2, half, LANES)
            dpre_all[parts[n].start // LANES] = value
    add_row_sum(sum_ref, jnp.concatenate(dpre_all, axis=1))


def attention(normed, cot, bias, tables, line, column, weights):
    count, rows = column.shape[0], column.shape[2]
    half, width = rows // 2, weights[0].shape[1] // 4

    def split(value):
        return value.reshape(2, count, half, value.shape[1])

    def block(cols):
        return pl.BlockSpec((2, 1, half, cols), lambda s: (0, s, 0, 0))

    attended, dpre, sums = call(
        attention_kernel,
        [
            jax.ShapeDtypeStruct((2, count, half, width), BF),
            jax.ShapeDtypeStruct((2, count, half, 3 * width), BF),
            jax.ShapeDtypeStruct((8, 3 * width), F32),
        ],
        (count,),
        [
            block(normed.shape[1]),
            block(cot.shape[1]),
            pl.BlockSpec((1, 3 * width), lambda s: (0, 0)),
            block(LANES),
            block(LANES),
            block(LANES),
            pl.BlockSpec((1, rows, LANES), lambda s: (s, 0, 0)),
            pl.BlockSpec((1, 8, rows), lambda s: (s, 0, 0)),
        ]
        + [resident(w) for w in weights],
        [block(width), block(3 * width), pl.BlockSpec((8, 3 * width), lambda s: (0, 0))],
        split(normed),
        split(cot),
        bias.reshape(1, 3 * width),
        *[split(t) for t in tables],
        line,
        column,
        *weights,
    )
    tokens = 2 * count * half
    return attended.reshape(tokens, width), dpre.reshape(tokens, 3 * width), sums


def rotary_lanes(places):
    halfway = ROT_DIM // 2
    lane = jnp.arange(LANES, dtype=jnp.int32) % HEAD_DIM
    freqs = 10000.0 ** (-(lane % halfway).astype(F32) * 2.0 / ROT_DIM)
    angles = places.astype(F32)[:, None] * freqs[None, :]
    turned = lane < ROT_DIM
    cos = jnp.where(turned, jnp.cos(angles), 1.0)
    sin = jnp.where(turned, jnp.sin(angles), 0.0)
    return cos, jnp.where(lane < halfway, -sin, 0.0), jnp.where(lane >= halfway, sin, 0.0)


def standardize(inputs):
    average = jnp.mean(inputs, axis=-1, keepdims=True)
    centered = inputs - average
    inv_std = lax.rsqrt(jnp.mean(centered * centered, axis=-1, keepdims=True) + EPSILON)
    return centered * inv_std, inv_std


def input_gradient(normed_grad, cot, normal_x, inv_std, gain):
    scaled = normed_grad * gain
    return cot + inv_std * (
        scaled
        - jnp.mean(scaled, axis=-1, keepdims=True)
        - normal_x * jnp.mean(scaled * normal_x, axis=-1, keepdims=True)
    )


def norm_kernel(table_ref, tok_ref, cot_ref, gain_ref, shift_ref, normed_ref, mixed_ref, *, cols):
    normal_x, _ = standardize(tok_ref[...].astype(F32))
    normed = (normal_x * gain_ref[...].astype(F32) + shift_ref[...].astype(F32)).astype(BF)
    for n in range(tok_ref.shape[1] // cols):
        target = pl.ds(pl.multiple_of(table_ref[n], cols), cols)
        normed_ref[:, target] = normed[:, n * cols : (n + 1) * cols]
        mixed_ref[:, target] = cot_ref[:, n * cols : (n + 1) * cols]


def natural(table_ref, refs, cols):
    parts = []
    for n in range(refs[0].shape[1] // cols):
        source = pl.ds(pl.multiple_of(table_ref[n], cols), cols)
        total = refs[0][:, source].astype(F32)
        for ref in refs[1:]:
            total = total + ref[:, source].astype(F32)
        parts.append(total)
    return jnp.concatenate(parts, axis=1)


def norm_back_kernel(table_ref, tok_ref, cot_ref, gain_ref, *refs, cols):
    pieces, (grad_ref, lines_ref) = refs[:-2], refs[-2:]
    i, last_tile = pl.program_id(0), pl.num_programs(0) - 1

    @pl.when(i == 0)
    def _():
        lines_ref[...] = jnp.zeros_like(lines_ref)

    @pl.when(i == last_tile)
    def _():
        grad_ref[...] = jnp.zeros_like(grad_ref)
        grad_ref[0:8, :] = lines_ref[...]

    @pl.when(i < last_tile)
    def _():
        normal_x, inv_std = standardize(tok_ref[...].astype(F32))
        cot = cot_ref[...].astype(F32)
        normed_grad = natural(table_ref, pieces, cols)
        grad_ref[...] = input_gradient(
            normed_grad, cot, normal_x, inv_std, gain_ref[...].astype(F32)
        )
        for row, value in enumerate((normed_grad * normal_x, normed_grad, cot)):
            lines_ref[row : row + 1, :] += jnp.sum(value, axis=0, keepdims=True)


def result_kernel(table_ref, tok_ref, bias_ref, *refs, cols):
    pieces, out_ref = refs[:-1], refs[-1]
    branches = natural(table_ref, pieces, cols)
    out_ref[...] = (tok_ref[...].astype(F32) + branches + bias_ref[...].astype(F32)).astype(BF)


def on_half(kernel, table, cols, whole, lines, mine, outs, extra=0, scratch=(), tile=64):
    half, width = whole[0].shape[0] // 2, whole[0].shape[1]
    steps = half // tile
    last_entry = table.shape[0] - 1

    def row(i):
        return jnp.minimum(i, steps - 1)

    return pl.pallas_call(
        functools.partial(kernel, cols=cols),
        out_shape=outs,
        grid_spec=pltpu.PrefetchScalarGridSpec(
            num_scalar_prefetch=1,
            grid=(steps + extra,),
            in_specs=[pl.BlockSpec((tile, width), lambda i, t: (t[last_entry] * steps + row(i), 0))]
            * len(whole)
            + [pl.BlockSpec((1, width), lambda i, t: (0, 0))] * len(lines)
            + [pl.BlockSpec((tile, width), lambda i, t: (row(i), 0))] * len(mine),
            out_specs=[pl.BlockSpec((tile, width), lambda i, t: (i, 0))] * len(outs),
            scratch_shapes=list(scratch),
        ),
        compiler_params=pltpu.CompilerParams(vmem_limit_bytes=32 * 1024 * 1024),
        cost_estimate=pl.CostEstimate(flops=1000, bytes_accessed=1000, transcendentals=0),
    )(table, *whole, *[line.reshape(1, width) for line in lines], *mine)


def local_part(dp_size):
    top_bits = [b for b in range(3, dp_size.bit_length() - 1)]

    def swap(value, *bits):
        flip = sum(1 << bit for bit in bits)
        return lax.ppermute(value, "dp", [(i, i ^ flip) for i in range(dp_size)])

    def swap_core(value):
        return lax.ppermute(value, "tensor", [(0, 1), (1, 0)])

    def swap_mixed(value, bits):
        pairs = [(2 * i + c, 2 * (i ^ (1 << bits[c])) + c) for i in range(dp_size) for c in (0, 1)]
        return lax.ppermute(value, ("dp", "tensor"), pairs)

    def ordered(bit, own, other, axis):
        return jnp.where(
            bit == 0,
            jnp.concatenate([own, other], axis),
            jnp.concatenate([other, own], axis),
        )

    def part_of(value, index, axis):
        size = value.shape[axis] // 2
        return lax.dynamic_slice_in_dim(value, index * size, size, axis)

    def sync(*values):
        return lax.optimization_barrier(values)

    def local(
        tokens,
        segments,
        ln_gain,
        ln_shift,
        qkv_weight,
        qkv_bias,
        out_weight,
        up_weight,
        up_bias,
        down_weight,
        branch_bias,
        cotangent,
    ):
        rows, width = tokens.shape
        half = rows // 2
        wide = width // 2
        share = qkv_weight.shape[0]
        unit = 4 * share
        cols = 2 * share
        me = lax.axis_index("dp")
        core = lax.axis_index("tensor")
        x_mine, y_mine, zl_mine = (me >> X_BIT) & 1, (me >> Y_BIT) & 1, (me >> ZL_BIT) & 1
        block = 2 * x_mine + zl_mine
        att = qkv_weight.shape[2] // 4
        hid = up_weight.shape[1] // 4
        tops = 2 ** len(top_bits)

        n = jnp.arange(4 * tops, dtype=jnp.int32)
        table = ((((n & 1) ^ y_mine) * tops + ((n >> 2) ^ (me >> 3))) * 2 + ((n >> 1) & 1)) * cols
        table = jnp.concatenate([table, core.reshape(1)]).astype(jnp.int32)
        aligned = cols % LANES == 0

        def relative(split):
            for axis, bit in enumerate([Y_BIT] + top_bits[::-1]):
                split = jnp.where((me >> bit) & 1 == 1, jnp.flip(split, axis + 1), split)
            return split

        def to_mixed(value):
            count = value.shape[0]
            split = value.reshape(count, tops, 2, 2, cols).transpose(0, 3, 1, 2, 4)
            split = relative(split.reshape((count, 2) + (2,) * len(top_bits) + (unit,)))
            return split.reshape(count, width)

        def from_mixed(value):
            count = value.shape[0]
            split = relative(value.reshape((count, 2) + (2,) * len(top_bits) + (unit,)))
            split = split.reshape(count, 2, tops, 2, cols).transpose(0, 2, 3, 1, 4)
            return split.reshape(count, width)

        def my_rows(value):
            return lax.dynamic_slice_in_dim(value, core * half, half, 0)

        def norm_forward():
            shape = jax.ShapeDtypeStruct((half, width), BF)
            if aligned:
                return on_half(
                    norm_kernel,
                    table,
                    cols,
                    [tokens, cotangent],
                    [ln_gain, ln_shift],
                    [],
                    [shape, shape],
                )
            normal_x, _ = standardize(my_rows(tokens).astype(F32))
            normed = normal_x * ln_gain.astype(F32) + ln_shift.astype(F32)
            return to_mixed(normed.astype(BF)), to_mixed(my_rows(cotangent))

        def norm_backward(*pieces):
            if aligned:
                return on_half(
                    norm_back_kernel,
                    table,
                    cols,
                    [tokens, cotangent],
                    [ln_gain],
                    list(pieces),
                    [jax.ShapeDtypeStruct((half + 64, width), F32)],
                    extra=1,
                    scratch=[pltpu.VMEM((8, width), F32)],
                )[0]
            normal_x, inv_std = standardize(my_rows(tokens).astype(F32))
            cot = my_rows(cotangent).astype(F32)
            grad = from_mixed(add(*[piece[:half] for piece in pieces]))
            lines = [jnp.sum(v, axis=0, keepdims=True) for v in (grad * normal_x, grad, cot)]
            result = input_gradient(grad, cot, normal_x, inv_std, ln_gain.astype(F32))
            return jnp.concatenate([result] + lines + [jnp.zeros((61, width), F32)])

        def finish(*pieces):
            if aligned:
                return on_half(
                    result_kernel,
                    table,
                    cols,
                    [tokens],
                    [branch_bias],
                    list(pieces),
                    [jax.ShapeDtypeStruct((half, width), BF)],
                )[0]
            branches = from_mixed(add(*[piece[:half] for piece in pieces]))
            return (my_rows(tokens).astype(F32) + branches + branch_bias.astype(F32)).astype(BF)

        def w_x(piece):
            return part_of(piece, x_mine, 1), swap(part_of(piece, 1 - x_mine, 1), X_BIT)

        def w_zl(w):
            return part_of(w, zl_mine, 1), swap(part_of(w, 1 - zl_mine, 1), ZL_BIT)

        def w_place(pair):
            return place_halves(zl_mine, *pair, steps=1)

        def w_top(w):
            rest = None
            for bit in top_bits:
                mine = w if rest is None else jnp.concatenate([w, rest])
                got = swap(mine, bit)
                rest = got if rest is None else jnp.concatenate([rest, got])
            return rest

        def add(*values):
            total = values[0].astype(F32)
            for value in values[1:]:
                total = total + value.astype(F32)
            return total

        def top_send(kept, got):
            if kept is None:
                return None, None
            if tops > 2:
                return add(kept, got).astype(BF), None
            cut = kept.shape[0] // 2
            return sum_rows(cut, (kept, 0), (got, 0)), sum_rows(cut, (kept, cut), (got, cut))

        def g_top(rest):
            if rest is None or tops == 2:
                return None if rest is None else swap(rest, top_bits[0])
            own = jnp.zeros((unit,) + rest.shape[1:], rest.dtype)
            grad = jnp.concatenate([own, rest])
            for bit in reversed(top_bits):
                cut = grad.shape[0] // 2
                grad = add(grad[:cut], swap(grad[cut:], bit)).astype(BF)
            return grad

        def g_split(kept, got, one, two):
            if two is not None:
                return split_sum(zl_mine, kept, got, one, two)
            total = add(kept, got, one[:unit]).astype(BF)
            return part_of(total, 1 - zl_mine, 0), part_of(total, zl_mine, 0)

        def g_zl(split):
            return split[1], swap(split[0], ZL_BIT)

        def g_cross(pair):
            return cross(zl_mine, x_mine, *pair)

        def g_x(split):
            return split[1], swap(split[0], X_BIT)

        def g_swap_y(value):
            return None if value is None else swap(value, Y_BIT)

        straight = jnp.zeros((2,), jnp.int32)
        crossed = jnp.stack([core, 1 - core]).astype(jnp.int32)

        def far_side(far):
            return swap_mixed(far, (X_BIT, ZL_BIT))

        def near_side(near, second):
            return swap_mixed(sum_rows(half, (near, half), (second, half)), (ZL_BIT, X_BIT))

        u_x = w_x(up_weight)
        n_own, c_own = norm_forward()
        seg = jnp.stack(
            [segments, swap(segments, ZL_BIT), swap(segments, X_BIT), swap(segments, X_BIT, ZL_BIT)]
        )
        u_x, c_own, seg, qkv_weight, out_weight, down_weight = sync(
            u_x, c_own, seg, qkv_weight, out_weight, down_weight
        )
        uu = w_place(w_zl(ordered(x_mine, *u_x, 0)))
        n_got = swap(n_own, ZL_BIT)
        qkv_piece = qkv_weight.reshape(share, 3, 4, att).swapaxes(1, 2).reshape(share, 4, 3 * att)
        out_piece = out_weight.T.reshape(share, 4, att)
        a_x = w_x(jnp.concatenate([qkv_piece, out_piece], axis=2).reshape(share, 16 * att))
        d_x = w_x(down_weight.T)
        uu, n_own, n_got, a_x, d_x, c_own, seg = sync(uu, n_own, n_got, a_x, d_x, c_own, seg)
        u_rest = w_top(uu)
        u_far = swap(uu, Y_BIT)
        n_pair = jnp.concatenate([n_own, n_got])
        n_second = swap(n_pair, X_BIT)
        n_got_pair = swap_core(n_pair)
        aa = w_place(w_zl(ordered(x_mine, *a_x, 0)))
        dd = ordered(x_mine, *d_x, 0)
        u_rest, u_far, n_second, n_got_pair, aa, dd, c_own, seg = sync(
            u_rest, u_far, n_second, n_got_pair, aa, dd, c_own, seg
        )
        a_rest = w_top(aa)
        a_far = swap(aa, Y_BIT)
        u_far_rest = g_swap_y(u_rest)
        n_got_second = swap_core(n_second)
        dd = w_place(w_zl(dd))
        c_got = swap_mixed(c_own, (ZL_BIT, X_BIT))
        order = jnp.broadcast_to(jnp.arange(rows, dtype=jnp.int32), (4, rows))
        begins = jnp.concatenate([jnp.ones((4, 1), bool), seg[:, 1:] != seg[:, :-1]], axis=1)
        opening = lax.cummax(jnp.where(begins, order, 0), axis=1)

        def halves(value):
            return jnp.where(core == 0, value, jnp.roll(value, half, axis=1))

        order, opening = halves(order), halves(opening)
        tables = rotary_lanes(
            (order - opening).reshape(4, 2, half).swapaxes(0, 1).reshape(4 * rows)
        )
        line = jnp.stack([order, opening], axis=2)
        line = jnp.pad(line, ((0, 0), (0, 0), (0, LANES - 2)))
        column = jnp.broadcast_to(order[:, None, :], (4, 8, rows))
        u_far_rest, a_rest, a_far, dd, c_own, c_got, n_got_second, tables, line, column = sync(
            u_far_rest, a_rest, a_far, dd, c_own, c_got, n_got_second, tables, line, column
        )
        d_rest = w_top(dd)
        d_far = swap(dd, Y_BIT)
        a_far_rest = g_swap_y(a_rest)
        c_pair = jnp.concatenate([c_own, c_got])
        c_second = swap_mixed(c_pair, (X_BIT, ZL_BIT))
        c_got_pair = swap_core(c_pair)
        normed = join(straight, n_pair, n_second, n_got_pair, n_got_second)
        my_up_bias = lax.dynamic_slice_in_dim(up_bias, block * hid, hid, 0).astype(F32)
        up_w = [w for w in (uu, u_rest, u_far, u_far_rest) if w is not None]
        act, slope = up_project(normed, my_up_bias, up_w)
        d_rest, d_far, a_far_rest, c_second, c_got_pair, normed, act, slope = sync(
            d_rest, d_far, a_far_rest, c_second, c_got_pair, normed, act, slope
        )
        d_far_rest = g_swap_y(d_rest)
        c_got_second = swap_core(c_second)
        cot = join(crossed, c_pair, c_second, c_got_pair, c_got_second)
        gd = weight_grads(unit, (0, 1, 2), (cot, act))
        d_far_rest, cot, gd = sync(d_far_rest, cot, gd)
        d_a = g_swap_y(gd[0])
        my_qkv_bias = lax.dynamic_slice_in_dim(qkv_bias, block * att, att, 1).astype(F32)
        att_w = [w for w in (aa, a_rest, a_far, a_far_rest) if w is not None]
        attended, qkv_g, qkv_sums = attention(
            normed, cot, my_qkv_bias, tables, line, column, att_w
        )
        d_a, gd, attended, qkv_g, d_far_rest = sync(d_a, gd, attended, qkv_g, d_far_rest)
        d_z1, d_z2 = top_send(gd[2], d_a)
        d_z1 = g_top(d_z1)
        d_b = swap(gd[1], Y_BIT)
        ga = weight_grads(unit, (0, 1, 2), (normed, qkv_g), (cot, attended))
        down_w = [w for w in (dd, d_rest, d_far, d_far_rest) if w is not None]
        b_send = pair_dot(1, 1 - core, act, down_w, attended, att_w, 3 * att)
        d_z1, d_z2, d_b, ga, b_send, cot, slope, act, attended = sync(
            d_z1, d_z2, d_b, ga, b_send, cot, slope, act, attended
        )
        d_z2 = g_top(d_z2)
        a_a = g_swap_y(ga[0])
        b_got = swap_core(b_send)
        up_g, up_sums = up_gradient(cot, slope, down_w)
        n_send = pair_dot(1, 1 - core, up_g, up_w, qkv_g, att_w, 0)
        b_near, b_far = pair_dot(0, core, act, down_w, attended, att_w, 3 * att, b_got)
        d_z2, a_a, ga, b_near, b_far, up_g, n_send = sync(
            d_z2, a_a, ga, b_near, b_far, up_g, n_send
        )
        a_z1, a_z2 = top_send(ga[2], a_a)
        a_z1 = g_top(a_z1)
        a_b = swap(ga[1], Y_BIT)
        n_got = swap_core(n_send)
        b_second = far_side(b_far)
        gu = weight_grads(unit, (0,), (normed, up_g))
        n_near, n_far = pair_dot(0, core, up_g, up_w, qkv_g, att_w, 0, n_got)
        a_z1, a_z2, a_b, gu, n_near, n_far, b_second = sync(
            a_z1, a_z2, a_b, gu, n_near, n_far, b_second
        )
        a_z2 = g_top(a_z2)
        u_a = g_swap_y(gu[0])
        n_second = far_side(n_far)
        gu = weight_grads(unit, (1, 2), (normed, up_g))
        (gd_own,) = weight_grads(unit, (3,), (cot, act))
        d_l = g_split(gd_own, d_b, d_z1, d_z2)
        a_z2, u_a, gu, d_l, n_second, b_near, b_second, up_g, qkv_g, attended, normed, cot = sync(
            a_z2, u_a, gu, d_l, n_second, b_near, b_second, up_g, qkv_g, attended, normed, cot
        )
        u_z1, u_z2 = top_send(gu[1], u_a)
        u_z1 = g_top(u_z1)
        u_b = swap(gu[0], Y_BIT)
        n_first = near_side(n_near, n_second)
        b_first = near_side(b_near, b_second)
        d_l = g_zl(d_l)
        (ga_own,) = weight_grads(unit, (3,), (normed, qkv_g), (cot, attended))
        a_l = g_split(ga_own, a_b, a_z1, a_z2)
        (gu_own,) = weight_grads(unit, (3,), (normed, up_g))
        u_z1, u_z2, u_b, n_first, b_first, d_l, a_l, gu_own = sync(
            u_z1, u_z2, u_b, n_first, b_first, d_l, a_l, gu_own
        )
        u_z2 = g_top(u_z2)
        a_l = g_zl(a_l)
        d_x = g_x(g_cross(d_l))
        input_grad = norm_backward(n_near, n_second, n_first)
        result = finish(b_near, b_second, b_first)
        biases = jnp.concatenate([qkv_sums[0], up_sums[0]])
        spread = lax.dynamic_update_slice(
            jnp.zeros((4, biases.shape[0]), F32), biases[None], (block, 0)
        )
        u_z2, a_l, d_x, input_grad, result, spread = sync(
            u_z2, a_l, d_x, input_grad, result, spread
        )
        u_l = g_zl(g_split(gu_own, u_b, u_z1, u_z2))
        a_x = g_x(g_cross(a_l))
        input_other = swap_core(input_grad)
        result_other = swap_core(result)
        lines = input_grad[half : half + 3] + input_other[half : half + 3]
        lines = jnp.concatenate([lines.reshape(-1), spread.reshape(-1)])
        for bit in [Y_BIT] + top_bits + [X_BIT]:
            lines = lines + swap(lines, bit)
        u_l, a_x, input_other, result_other, lines = sync(
            u_l, a_x, input_other, result_other, lines
        )
        gu = g_x(g_cross(u_l))
        lines = lines + swap(lines, ZL_BIT)
        result = place_halves(core, result, result_other)
        input_grad = place_halves(core, input_grad, input_other, rows=half)
        ga = ordered(x_mine, *a_x, 1)
        gd = ordered(x_mine, *d_x, 1)
        gu = ordered(x_mine, *gu, 1)

        gdown = gd.astype(F32).T
        gup = gu.astype(F32)
        ga = ga.reshape(share, 4, 4 * att)
        gqkv = ga[..., : 3 * att].astype(F32)
        gqkv = gqkv.reshape(share, 4, 3, att).swapaxes(1, 2).reshape(share, 3, 4 * att)
        gout = ga[..., 3 * att :].astype(F32).reshape(share, 4 * att).T
        biases = lines[3 * width :].reshape(4, 3 * att + hid)
        qkv_b = biases[:, : 3 * att].reshape(4, 3, att).swapaxes(0, 1).reshape(3, 4 * att)
        up_b = biases[:, 3 * att :].reshape(4 * hid)
        return (
            result,
            input_grad,
            lines[:width],
            lines[width : 2 * width],
            gqkv,
            qkv_b,
            gout,
            gup,
            up_b,
            gdown,
            lines[2 * width : 3 * width],
        )

    return local


def solution(mesh):
    return jax.shard_map(
        local_part(mesh.shape["dp"]),
        mesh=mesh,
        in_specs=(
            P("dp", None),
            P("dp"),
            P(),
            P(),
            P("dp", None, "tensor"),
            P(None, "tensor"),
            P("tensor", "dp"),
            P("dp", "tensor"),
            P("tensor"),
            P("tensor", "dp"),
            P(),
            P("dp", None),
        ),
        out_specs=(
            P("dp", None),
            P("dp", None),
            P(),
            P(),
            P("dp", None, "tensor"),
            P(None, "tensor"),
            P("tensor", "dp"),
            P("dp", "tensor"),
            P("tensor"),
            P("tensor", "dp"),
            P(),
        ),
        check_vma=False,
    )
```

```python
import functools

import jax
import jax.numpy as jnp
from jax import lax
from jax.experimental import pallas as pl
from jax.experimental.pallas import tpu as pltpu
from jax.sharding import PartitionSpec as P

HEAD_DIM = 64
ROT_DIM = 32
LANES = 128
NEGATIVE = -1e30
EPSILON = 1e-05
GELU_A = 0.7978845608028654
GELU_B = 0.044715
X_BIT, Y_BIT, ZL_BIT = 0, 1, 2
BF = jnp.bfloat16
F32 = jnp.float32


def dot_nn(a, b):
    return jnp.dot(a, b, preferred_element_type=F32)


def dot_nt(a, b):
    return lax.dot_general(a, b, (((1,), (1,)), ((), ())), preferred_element_type=F32)


def dot_tn(a, b):
    return lax.dot_general(a, b, (((0,), (0,)), ((), ())), preferred_element_type=F32)


def call(kernel, outs, grid, in_specs, out_specs, *operands, prefetch=0, cost=1000):
    return pl.pallas_call(
        kernel,
        out_shape=outs,
        grid_spec=pltpu.PrefetchScalarGridSpec(
            num_scalar_prefetch=prefetch, grid=grid, in_specs=in_specs, out_specs=out_specs
        ),
        compiler_params=pltpu.CompilerParams(vmem_limit_bytes=54 * 1024 * 1024),
        cost_estimate=pl.CostEstimate(flops=1000, bytes_accessed=cost, transcendentals=0),
    )(*operands)


def resident(value):
    return pl.BlockSpec(value.shape, lambda *_: (0,) * value.ndim)


def wide_dot(rows, refs, cols):
    total, low = None, 0
    for ref in refs:
        high = low + ref.shape[0]
        term = dot_nn(rows[:, low:high], ref[:, cols])
        total = term if total is None else total + term
        low = high
    return total


def sum_kernel(*refs):
    total = refs[0][...].astype(F32)
    for ref in refs[1:-1]:
        total = total + ref[...].astype(F32)
    refs[-1][...] = total.astype(BF)


def sum_rows(rows, *terms, tile=128):
    width = terms[0][0].shape[1]
    tile = min(tile, rows)

    def spec(start):
        return pl.BlockSpec((tile, width), lambda i: (start // tile + i, 0))

    return call(
        sum_kernel,
        jax.ShapeDtypeStruct((rows, width), BF),
        (rows // tile,),
        [spec(start) for _, start in terms],
        spec(0),
        *[value for value, _ in terms],
    )


def half_kernel(_, *refs):
    sum_kernel(*refs)


def half_sum(which, wholes, halves=(), steps=2):
    rows, cols = wholes[0].shape[0] // 2, wholes[0].shape[1]
    tile = rows // steps
    plain = pl.BlockSpec((tile, cols), lambda i, f: (i, 0))
    picked = pl.BlockSpec((tile, cols), lambda i, f: (f[0] * steps + i, 0))
    return call(
        half_kernel,
        jax.ShapeDtypeStruct((rows, cols), BF),
        (steps,),
        [picked] * len(wholes) + [plain] * len(halves),
        plain,
        which.reshape(1).astype(jnp.int32),
        *wholes,
        *halves,
        prefetch=1,
    )


def cross_kernel(flags_ref, own_ref, got_ref, send_ref, kept_ref):
    cols = own_ref.shape[1]
    for n, out_ref in enumerate((send_ref, kept_ref)):

        @pl.when(pl.program_id(0) == n)
        def _(out_ref=out_ref):
            for ref, place in ((own_ref, flags_ref[0]), (got_ref, 1 - flags_ref[0])):
                out_ref[:, pl.ds(pl.multiple_of(place * cols, cols), cols)] = ref[...]


def cross(zl, x, own, got):
    rows, cols = own.shape[0] // 2, own.shape[1]
    out = jax.ShapeDtypeStruct((rows, 2 * cols), BF)
    picked = pl.BlockSpec((rows, cols), lambda i, f: (jnp.where(i == 0, 1 - f[1], f[1]), 0))
    return call(
        cross_kernel,
        [out, out],
        (2,),
        [picked, picked],
        [pl.BlockSpec((rows, 2 * cols), lambda i, f: (0, 0))] * 2,
        jnp.stack([zl, x]).astype(jnp.int32),
        own,
        got,
        prefetch=1,
    )


def join_kernel(flags_ref, pair_ref, second_ref, got_pair_ref, got_second_ref, out_ref):
    i = pl.program_id(0)
    place = lax.rem(i, 4)
    for own, (p_ref, s_ref) in enumerate(
        ((pair_ref, second_ref), (got_pair_ref, got_second_ref))
    ):
        here = (i // 4) == own
        crossed = flags_ref[own] == 1
        from_pair = (place == 0) | ((place == 1) & jnp.logical_not(crossed))
        from_pair = from_pair | ((place == 2) & crossed)

        @pl.when(here & from_pair)
        def _(ref=p_ref):
            out_ref[...] = ref[...]

        @pl.when(here & jnp.logical_not(from_pair))
        def _(ref=s_ref):
            out_ref[...] = ref[...]


def join(flags, pair, second, got_pair, got_second):
    half, width = pair.shape[0] // 2, pair.shape[1]

    def spec(low, edge):
        return pl.BlockSpec((half, width), lambda i, f: (jnp.where(i - low > edge, 1, 0), 0))

    return call(
        join_kernel,
        jax.ShapeDtypeStruct((8 * half, width), pair.dtype),
        (8,),
        [spec(0, 0), spec(0, 2), spec(4, 0), spec(4, 2)],
        pl.BlockSpec((half, width), lambda i, f: (i, 0)),
        flags,
        pair,
        second,
        got_pair,
        got_second,
        prefetch=1,
    )


def place_kernel(core_ref, own_ref, other_ref, out_ref):
    steps = pl.num_programs(0) // 2

    @pl.when(pl.program_id(0) < steps)
    def _():
        out_ref[...] = own_ref[...]

    @pl.when(pl.program_id(0) >= steps)
    def _():
        out_ref[...] = other_ref[...]


def place_halves(core, own, other, steps=2, rows=None, cost=1000):
    rows, width = rows or own.shape[0], own.shape[1]
    tile = rows // steps
    return call(
        place_kernel,
        jax.ShapeDtypeStruct((2 * rows, width), own.dtype),
        (2 * steps,),
        [
            pl.BlockSpec((tile, width), lambda i, c: (jnp.minimum(i, steps - 1), 0)),
            pl.BlockSpec((tile, width), lambda i, c: (jnp.maximum(i - steps, 0), 0)),
        ],
        pl.BlockSpec((tile, width), lambda i, c: (lax.rem(i + steps * c[0], 2 * steps), 0)),
        core.reshape(1).astype(jnp.int32),
        own,
        other,
        prefetch=1,
        cost=cost,
    )


def up_kernel(rows_ref, bias_ref, *refs, chunk):
    weights, act_ref, slope_ref = refs[:-2], refs[-2], refs[-1]
    rows = rows_ref[...]
    for low in range(0, act_ref.shape[1], chunk):
        cols = slice(low, low + chunk)
        u = wide_dot(rows, weights, cols) + bias_ref[:, cols]
        squared = u * u
        gate = 0.5 + 0.5 * jnp.tanh(u * (GELU_A + GELU_A * GELU_B * squared))
        act = u * gate
        act_ref[:, cols] = act.astype(BF)
        slope = gate + act * (1.0 - gate) * (2.0 * GELU_A + 6.0 * GELU_A * GELU_B * squared)
        slope_ref[:, cols] = slope.astype(BF)


def up_project(rows, bias, weights, tile=256):
    count, hid = rows.shape[0], weights[0].shape[1]
    out = jax.ShapeDtypeStruct((count, hid), BF)
    block = pl.BlockSpec((tile, hid), lambda i: (i, 0))
    return call(
        functools.partial(up_kernel, chunk=256),
        [out, out],
        (count // tile,),
        [pl.BlockSpec((tile, rows.shape[1]), lambda i: (i, 0)), pl.BlockSpec((1, hid), lambda i: (0, 0))]
        + [resident(w) for w in weights],
        [block, block],
        rows,
        bias.reshape(1, hid),
        *weights,
    )


def add_row_sum(sum_ref, value):
    @pl.when(pl.program_id(0) == 0)
    def _():
        sum_ref[...] = jnp.zeros_like(sum_ref)

    sum_ref[0:1, :] += jnp.sum(value.astype(F32), axis=0, keepdims=True)


def up_grad_kernel(rows_ref, slope_ref, *refs):
    weights, grad_ref, sum_ref = refs[:-2], refs[-2], refs[-1]
    grad = wide_dot(rows_ref[...], weights, slice(None)) * slope_ref[...].astype(F32)
    grad = grad.astype(BF)
    grad_ref[...] = grad
    add_row_sum(sum_ref, grad)


def up_gradient(rows, slope, weights, tile=256):
    count, hid = slope.shape
    block = pl.BlockSpec((tile, hid), lambda i: (i, 0))
    return call(
        up_grad_kernel,
        [jax.ShapeDtypeStruct((count, hid), BF), jax.ShapeDtypeStruct((8, hid), F32)],
        (count // tile,),
        [pl.BlockSpec((tile, rows.shape[1]), lambda i: (i, 0)), block]
        + [resident(w) for w in weights],
        [block, pl.BlockSpec((8, hid), lambda i: (0, 0))],
        rows,
        slope,
        *weights,
    )


def weight_grad_kernel(terms, starts, *refs):
    outs = refs[2 * terms :]
    for n, out_ref in enumerate(outs):

        @pl.when((pl.program_id(0) >= starts[n]) & (pl.program_id(0) < starts[n + 1]))
        def _(out_ref=out_ref):
            low = 0
            for t in range(terms):
                value = dot_tn(refs[2 * t][...], refs[2 * t + 1][...])
                out_ref[:, low : low + value.shape[1]] = value.astype(BF)
                low = low + value.shape[1]


def weight_grads(unit, parts, *pairs):
    width = pairs[0][0].shape[1]
    cols = sum(right.shape[1] for _, right in pairs)
    tops = width // unit // 2
    every = ((tops + 1, tops - 1), (tops, 1), (1, tops - 1), (0, 1))
    sizes = [every[part][1] for part in parts]
    starts = [sum(sizes[:n]) for n in range(len(sizes) + 1)]

    def left_block(i):
        place = i
        for n, part in enumerate(parts):
            place = jnp.where(i >= starts[n], i - starts[n] + every[part][0], place)
        return 0, place

    in_specs, operands = [], []
    for left, right in pairs:
        in_specs.append(pl.BlockSpec((left.shape[0], unit), left_block))
        in_specs.append(resident(right))
        operands += [left, right]

    def out_block(n):
        return lambda i: (jnp.clip(i - starts[n], 0, sizes[n] - 1), 0)

    return call(
        functools.partial(weight_grad_kernel, len(pairs), starts),
        [jax.ShapeDtypeStruct((size * unit, cols), BF) for size in sizes],
        (starts[-1],),
        in_specs,
        [pl.BlockSpec((unit, cols), out_block(n)) for n in range(len(sizes))],
        *operands,
    )


def pair_kernel(pieces, adding, _, a_ref, c_ref, *refs):
    a, c, out_ref = a_ref[...], c_ref[...], refs[-1]
    low = 0
    for b_ref, d_ref in zip(refs[:pieces], refs[pieces : 2 * pieces]):
        high = low + b_ref.shape[0]
        total = dot_nt(a, b_ref[...]) + dot_nt(c, d_ref[...])
        if adding:
            total = total + refs[2 * pieces][:, low:high].astype(F32)
        out_ref[:, low:high] = total.astype(BF)
        low = high


def pair_dot(part, crossed, a, b, c, d, cut, got=None, begin=0, count=4):
    tile, width = a.shape[0] // 8, sum(piece.shape[0] for piece in b)
    extra = [] if got is None else [got]

    def row_block(i, f):
        i = i + begin
        return part * 4 + jnp.where((f[0] == 1) & (i > 0) & (i < 3), 3 - i, i), 0

    return call(
        functools.partial(pair_kernel, len(b), len(extra)),
        jax.ShapeDtypeStruct((count * tile, width), BF),
        (count,),
        [pl.BlockSpec((tile, a.shape[1]), row_block), pl.BlockSpec((tile, c.shape[1]), row_block)]
        + [resident(w) for w in b]
        + [pl.BlockSpec((w.shape[0], c.shape[1]), lambda i, f: (0, cut // c.shape[1])) for w in d]
        + [pl.BlockSpec((tile, width), lambda i, f: (i + begin, 0))] * len(extra),
        pl.BlockSpec((tile, width), lambda i, f: (i, 0)),
        crossed.reshape(1).astype(jnp.int32),
        a,
        c,
        *b,
        *d,
        *extra,
        prefetch=1,
    )


def attention_kernel(
    rows_ref, cot_ref, bias_ref, cos_ref, left_ref, right_ref, line_ref, column_ref, *refs
):
    weights, (out_ref, dpre_ref, sum_ref) = refs[:-3], refs[-3:]
    half, width = out_ref.shape[2:]
    rows = 2 * half
    scaling = HEAD_DIM ** (-0.5)

    def both(ref):
        return ref[:, 0].reshape(rows, ref.shape[3])

    cos, left, right = both(cos_ref), both(left_ref), both(right_ref)
    normed, cot = both(rows_ref), both(cot_ref)
    head_of = lax.broadcasted_iota(jnp.int32, (rows, LANES), 1) // HEAD_DIM

    def turn(v, sign):
        ahead = pltpu.roll(v, LANES - ROT_DIM // 2, 1)
        behind = pltpu.roll(v, ROT_DIM // 2, 1)
        return v * cos + sign * (ahead * left + behind * right)

    line, column = line_ref[0], column_ref[0]
    allowed = (line[:, 0:1] >= column[0:1]) & (line[:, 1:2] <= column[0:1])
    pre = wide_dot(normed, weights, slice(0, 3 * width)) + bias_ref[...]
    grads = wide_dot(cot, weights, slice(3 * width, 4 * width)).astype(BF)
    dpre_all = [None] * (3 * width // LANES)
    for pair in range(width // LANES):
        parts = [slice(b + pair * LANES, b + (pair + 1) * LANES) for b in (0, width, 2 * width)]
        q = turn(pre[:, parts[0]], 1.0).astype(BF)
        k = turn(pre[:, parts[1]], 1.0).astype(BF)
        v = pre[:, parts[2]].astype(BF)
        g = grads[:, parts[0]]
        att = dq = dk = dv = None
        for h in range(LANES // HEAD_DIM):
            mine = head_of == h
            qh = jnp.where(mine, q, 0).astype(BF)
            gh = jnp.where(mine, g, 0).astype(BF)
            s = jnp.where(allowed, dot_nt(qh, k) * scaling, NEGATIVE)
            e = jnp.exp(s - jnp.max(s, axis=-1, keepdims=True))
            p = e * (1.0 / jnp.sum(e, axis=-1, keepdims=True))
            low = p.astype(BF)
            att_h = dot_nn(low, v)
            dp = dot_nt(gh, v)
            inner = jnp.sum(p * dp, axis=-1, keepdims=True)
            ds = (p * (dp - inner)).astype(BF)
            dq_h = dot_nn(ds, k)
            dk_h = dot_tn(ds, qh)
            dv_h = dot_tn(low, gh)
            att = att_h if h == 0 else jnp.where(mine, att_h, att)
            dq = dq_h if h == 0 else jnp.where(mine, dq_h, dq)
            dk = dk_h if h == 0 else dk + dk_h
            dv = dv_h if h == 0 else dv + dv_h
        out_ref[:, 0, :, parts[0]] = att.astype(BF).reshape(2, half, LANES)
        for n, value in enumerate((turn(dq * scaling, -1.0), turn(dk * scaling, -1.0), dv)):
            value = value.astype(BF)
            dpre_ref[:, 0, :, parts[n]] = value.reshape(2, half, LANES)
            dpre_all[parts[n].start // LANES] = value
    add_row_sum(sum_ref, jnp.concatenate(dpre_all, axis=1))


def attention(normed, cot, bias, tables, line, column, weights):
    count, rows = column.shape[0], column.shape[2]
    half, width = rows // 2, weights[0].shape[1] // 4

    def split(value):
        return value.reshape(2, count, half, value.shape[1])

    def block(cols):
        return pl.BlockSpec((2, 1, half, cols), lambda s: (0, s, 0, 0))

    attended, dpre, sums = call(
        attention_kernel,
        [
            jax.ShapeDtypeStruct((2, count, half, width), BF),
            jax.ShapeDtypeStruct((2, count, half, 3 * width), BF),
            jax.ShapeDtypeStruct((8, 3 * width), F32),
        ],
        (count,),
        [
            block(normed.shape[1]),
            block(cot.shape[1]),
            pl.BlockSpec((1, 3 * width), lambda s: (0, 0)),
            block(LANES),
            block(LANES),
            block(LANES),
            pl.BlockSpec((1, rows, LANES), lambda s: (s, 0, 0)),
            pl.BlockSpec((1, 8, rows), lambda s: (s, 0, 0)),
        ]
        + [resident(w) for w in weights],
        [block(width), block(3 * width), pl.BlockSpec((8, 3 * width), lambda s: (0, 0))],
        split(normed),
        split(cot),
        bias.reshape(1, 3 * width),
        *[split(t) for t in tables],
        line,
        column,
        *weights,
    )
    tokens = 2 * count * half
    return attended.reshape(tokens, width), dpre.reshape(tokens, 3 * width), sums


def rotary_lanes(places):
    halfway = ROT_DIM // 2
    lane = jnp.arange(LANES, dtype=jnp.int32) % HEAD_DIM
    freqs = 10000.0 ** (-(lane % halfway).astype(F32) * 2.0 / ROT_DIM)
    angles = places.astype(F32)[:, None] * freqs[None, :]
    turned = lane < ROT_DIM
    cos = jnp.where(turned, jnp.cos(angles), 1.0)
    sin = jnp.where(turned, jnp.sin(angles), 0.0)
    return cos, jnp.where(lane < halfway, -sin, 0.0), jnp.where(lane >= halfway, sin, 0.0)


def standardize(inputs):
    average = jnp.mean(inputs, axis=-1, keepdims=True)
    centered = inputs - average
    inv_std = lax.rsqrt(jnp.mean(centered * centered, axis=-1, keepdims=True) + EPSILON)
    return centered * inv_std, inv_std


def input_gradient(normed_grad, cot, normal_x, inv_std, gain):
    scaled = normed_grad * gain
    return cot + inv_std * (
        scaled
        - jnp.mean(scaled, axis=-1, keepdims=True)
        - normal_x * jnp.mean(scaled * normal_x, axis=-1, keepdims=True)
    )


def norm_kernel(table_ref, tok_ref, cot_ref, gain_ref, shift_ref, normed_ref, mixed_ref, *, cols):
    normal_x, _ = standardize(tok_ref[...].astype(F32))
    normed = (normal_x * gain_ref[...].astype(F32) + shift_ref[...].astype(F32)).astype(BF)
    for n in range(tok_ref.shape[1] // cols):
        target = pl.ds(pl.multiple_of(table_ref[n], cols), cols)
        normed_ref[:, target] = normed[:, n * cols : (n + 1) * cols]
        mixed_ref[:, target] = cot_ref[:, n * cols : (n + 1) * cols]


def natural(table_ref, refs, cols):
    parts = []
    for n in range(refs[0].shape[1] // cols):
        source = pl.ds(pl.multiple_of(table_ref[n], cols), cols)
        total = refs[0][:, source].astype(F32)
        for ref in refs[1:]:
            total = total + ref[:, source].astype(F32)
        parts.append(total)
    return jnp.concatenate(parts, axis=1)


def norm_back_kernel(table_ref, tok_ref, cot_ref, gain_ref, *refs, cols):
    pieces, (grad_ref, lines_ref) = refs[:-2], refs[-2:]
    i, last_tile = pl.program_id(0), pl.num_programs(0) - 1

    @pl.when(i == 0)
    def _():
        lines_ref[...] = jnp.zeros_like(lines_ref)

    @pl.when(i == last_tile)
    def _():
        grad_ref[...] = jnp.zeros_like(grad_ref)
        grad_ref[0:8, :] = lines_ref[...]

    @pl.when(i < last_tile)
    def _():
        normal_x, inv_std = standardize(tok_ref[...].astype(F32))
        cot = cot_ref[...].astype(F32)
        normed_grad = natural(table_ref, pieces, cols)
        grad_ref[...] = input_gradient(
            normed_grad, cot, normal_x, inv_std, gain_ref[...].astype(F32)
        )
        for row, value in enumerate((normed_grad * normal_x, normed_grad, cot)):
            lines_ref[row : row + 1, :] += jnp.sum(value, axis=0, keepdims=True)


def result_kernel(table_ref, tok_ref, bias_ref, *refs, cols):
    pieces, out_ref = refs[:-1], refs[-1]
    branches = natural(table_ref, pieces, cols)
    out_ref[...] = (tok_ref[...].astype(F32) + branches + bias_ref[...].astype(F32)).astype(BF)


def on_half(kernel, table, cols, whole, lines, mine, outs, extra=0, scratch=(), tile=64):
    half, width = whole[0].shape[0] // 2, whole[0].shape[1]
    steps = half // tile
    last_entry = table.shape[0] - 1

    def row(i):
        return jnp.minimum(i, steps - 1)

    return pl.pallas_call(
        functools.partial(kernel, cols=cols),
        out_shape=outs,
        grid_spec=pltpu.PrefetchScalarGridSpec(
            num_scalar_prefetch=1,
            grid=(steps + extra,),
            in_specs=[pl.BlockSpec((tile, width), lambda i, t: (t[last_entry] * steps + row(i), 0))]
            * len(whole)
            + [pl.BlockSpec((1, width), lambda i, t: (0, 0))] * len(lines)
            + [pl.BlockSpec((tile, width), lambda i, t: (row(i), 0))] * len(mine),
            out_specs=[pl.BlockSpec((tile, width), lambda i, t: (i, 0))] * len(outs),
            scratch_shapes=list(scratch),
        ),
        compiler_params=pltpu.CompilerParams(vmem_limit_bytes=32 * 1024 * 1024),
        cost_estimate=pl.CostEstimate(flops=1000, bytes_accessed=1000, transcendentals=0),
    )(table, *whole, *[line.reshape(1, width) for line in lines], *mine)


def local_part(dp_size):
    top_bits = [b for b in range(3, dp_size.bit_length() - 1)]

    def swap(value, *bits):
        flip = sum(1 << bit for bit in bits)
        return lax.ppermute(value, "dp", [(i, i ^ flip) for i in range(dp_size)])

    def swap_core(value):
        return lax.ppermute(value, "tensor", [(0, 1), (1, 0)])

    def swap_mixed(value, bits):
        pairs = [(2 * i + c, 2 * (i ^ (1 << bits[c])) + c) for i in range(dp_size) for c in (0, 1)]
        return lax.ppermute(value, ("dp", "tensor"), pairs)

    def ordered(bit, own, other, axis):
        return jnp.where(
            bit == 0,
            jnp.concatenate([own, other], axis),
            jnp.concatenate([other, own], axis),
        )

    def part_of(value, index, axis):
        size = value.shape[axis] // 2
        return lax.dynamic_slice_in_dim(value, index * size, size, axis)

    def sync(*values):
        return lax.optimization_barrier(values)

    def local(
        tokens,
        segments,
        ln_gain,
        ln_shift,
        qkv_weight,
        qkv_bias,
        out_weight,
        up_weight,
        up_bias,
        down_weight,
        branch_bias,
        cotangent,
    ):
        rows, width = tokens.shape
        half = rows // 2
        wide = width // 2
        share = qkv_weight.shape[0]
        unit = 4 * share
        cols = 2 * share
        me = lax.axis_index("dp")
        core = lax.axis_index("tensor")
        x_mine, y_mine, zl_mine = (me >> X_BIT) & 1, (me >> Y_BIT) & 1, (me >> ZL_BIT) & 1
        block = 2 * x_mine + zl_mine
        att = qkv_weight.shape[2] // 4
        hid = up_weight.shape[1] // 4
        tops = 2 ** len(top_bits)

        n = jnp.arange(4 * tops, dtype=jnp.int32)
        table = ((((n & 1) ^ y_mine) * tops + ((n >> 2) ^ (me >> 3))) * 2 + ((n >> 1) & 1)) * cols
        table = jnp.concatenate([table, core.reshape(1)]).astype(jnp.int32)
        aligned = cols % LANES == 0

        def relative(split):
            for axis, bit in enumerate([Y_BIT] + top_bits[::-1]):
                split = jnp.where((me >> bit) & 1 == 1, jnp.flip(split, axis + 1), split)
            return split

        def to_mixed(value):
            count = value.shape[0]
            split = value.reshape(count, tops, 2, 2, cols).transpose(0, 3, 1, 2, 4)
            split = relative(split.reshape((count, 2) + (2,) * len(top_bits) + (unit,)))
            return split.reshape(count, width)

        def from_mixed(value):
            count = value.shape[0]
            split = relative(value.reshape((count, 2) + (2,) * len(top_bits) + (unit,)))
            split = split.reshape(count, 2, tops, 2, cols).transpose(0, 2, 3, 1, 4)
            return split.reshape(count, width)

        def my_rows(value):
            return lax.dynamic_slice_in_dim(value, core * half, half, 0)

        def norm_forward():
            shape = jax.ShapeDtypeStruct((half, width), BF)
            if aligned:
                return on_half(
                    norm_kernel,
                    table,
                    cols,
                    [tokens, cotangent],
                    [ln_gain, ln_shift],
                    [],
                    [shape, shape],
                )
            normal_x, _ = standardize(my_rows(tokens).astype(F32))
            normed = normal_x * ln_gain.astype(F32) + ln_shift.astype(F32)
            return to_mixed(normed.astype(BF)), to_mixed(my_rows(cotangent))

        def norm_backward(*pieces):
            if aligned:
                return on_half(
                    norm_back_kernel,
                    table,
                    cols,
                    [tokens, cotangent],
                    [ln_gain],
                    list(pieces),
                    [jax.ShapeDtypeStruct((half + 64, width), F32)],
                    extra=1,
                    scratch=[pltpu.VMEM((8, width), F32)],
                )[0]
            normal_x, inv_std = standardize(my_rows(tokens).astype(F32))
            cot = my_rows(cotangent).astype(F32)
            grad = from_mixed(add(*[piece[:half] for piece in pieces]))
            lines = [jnp.sum(v, axis=0, keepdims=True) for v in (grad * normal_x, grad, cot)]
            result = input_gradient(grad, cot, normal_x, inv_std, ln_gain.astype(F32))
            return jnp.concatenate([result] + lines + [jnp.zeros((61, width), F32)])

        def finish(*pieces):
            if aligned:
                return on_half(
                    result_kernel,
                    table,
                    cols,
                    [tokens],
                    [branch_bias],
                    list(pieces),
                    [jax.ShapeDtypeStruct((half, width), BF)],
                )[0]
            branches = from_mixed(add(*[piece[:half] for piece in pieces]))
            return (my_rows(tokens).astype(F32) + branches + branch_bias.astype(F32)).astype(BF)

        def w_x(piece):
            return part_of(piece, x_mine, 1), swap(part_of(piece, 1 - x_mine, 1), X_BIT)

        def w_zl(w):
            return part_of(w, zl_mine, 1), swap(part_of(w, 1 - zl_mine, 1), ZL_BIT)

        def w_place(pair):
            return place_halves(zl_mine, *pair, steps=1)

        def w_top(w):
            rest = None
            for bit in top_bits:
                mine = w if rest is None else jnp.concatenate([w, rest])
                got = swap(mine, bit)
                rest = got if rest is None else jnp.concatenate([rest, got])
            return rest

        def add(*values):
            total = values[0].astype(F32)
            for value in values[1:]:
                total = total + value.astype(F32)
            return total

        def top_send(kept, got):
            if tops > 2:
                return add(kept, got).astype(BF), None
            return half_sum(1 - zl_mine, (kept, got)), half_sum(zl_mine, (kept, got))

        def g_top(rest):
            if rest is None or tops == 2:
                return None if rest is None else swap(rest, top_bits[0])
            own = jnp.zeros((unit,) + rest.shape[1:], rest.dtype)
            grad = jnp.concatenate([own, rest])
            for bit in reversed(top_bits):
                cut = grad.shape[0] // 2
                grad = add(grad[:cut], swap(grad[cut:], bit)).astype(BF)
            return grad

        def g_far(kept, got, one):
            if tops > 2:
                return part_of(add(kept, got, one[:unit]).astype(BF), 1 - zl_mine, 0)
            return half_sum(1 - zl_mine, (kept, got), (one,))

        def g_near(kept, got, one, two):
            if tops > 2:
                return part_of(add(kept, got, one[:unit]).astype(BF), zl_mine, 0)
            return half_sum(zl_mine, (kept, got), (two,))

        def g_cross(own, got):
            return cross(zl_mine, x_mine, own, got)

        def g_x(split):
            return split[1], swap(split[0], X_BIT)

        def g_swap_y(value):
            return None if value is None else swap(value, Y_BIT)

        straight = jnp.zeros((2,), jnp.int32)
        crossed = jnp.stack([core, 1 - core]).astype(jnp.int32)

        first_way, second_way = (ZL_BIT, X_BIT), (X_BIT, ZL_BIT)

        def near_side(near, second, way):
            return swap_mixed(sum_rows(half, (near, half), (second, half)), way)

        def sum_over(value, bits):
            if len(bits) == 2:
                got = [swap(value, *way) for way in (bits[:1], bits[1:], bits)]
                return value + got[0] + (got[1] + got[2])
            for bit in bits:
                value = value + swap(value, bit)
            return value

        u_x = w_x(up_weight)
        n_own, c_own = norm_forward()
        seg = jnp.stack(
            [segments, swap(segments, ZL_BIT), swap(segments, X_BIT), swap(segments, X_BIT, ZL_BIT)]
        )
        u_x, c_own, seg, qkv_weight, out_weight, down_weight = sync(
            u_x, c_own, seg, qkv_weight, out_weight, down_weight
        )
        uu = w_place(w_zl(ordered(x_mine, *u_x, 0)))
        n_got = swap(n_own, ZL_BIT)
        qkv_piece = qkv_weight.reshape(share, 3, 4, att).swapaxes(1, 2).reshape(share, 4, 3 * att)
        out_piece = out_weight.T.reshape(share, 4, att)
        a_x = w_x(jnp.concatenate([qkv_piece, out_piece], axis=2).reshape(share, 16 * att))
        d_x = w_x(down_weight.T)
        uu, n_own, n_got, a_x, d_x, c_own, seg = sync(uu, n_own, n_got, a_x, d_x, c_own, seg)
        u_rest = w_top(uu)
        u_far = swap(uu, Y_BIT)
        n_pair = jnp.concatenate([n_own, n_got])
        n_second = swap(n_pair, X_BIT)
        n_got_pair = swap_core(n_pair)
        aa = w_place(w_zl(ordered(x_mine, *a_x, 0)))
        dd = ordered(x_mine, *d_x, 0)
        u_rest, u_far, n_second, n_got_pair, aa, dd, c_own, seg = sync(
            u_rest, u_far, n_second, n_got_pair, aa, dd, c_own, seg
        )
        a_rest = w_top(aa)
        a_far = swap(aa, Y_BIT)
        u_far_rest = g_swap_y(u_rest)
        n_got_second = swap_core(n_second)
        dd = w_place(w_zl(dd))
        c_got = swap_mixed(c_own, (ZL_BIT, X_BIT))
        order = jnp.broadcast_to(jnp.arange(rows, dtype=jnp.int32), (4, rows))
        begins = jnp.concatenate([jnp.ones((4, 1), bool), seg[:, 1:] != seg[:, :-1]], axis=1)
        opening = lax.cummax(jnp.where(begins, order, 0), axis=1)

        def halves(value):
            return jnp.where(core == 0, value, jnp.roll(value, half, axis=1))

        order, opening = halves(order), halves(opening)
        tables = rotary_lanes(
            (order - opening).reshape(4, 2, half).swapaxes(0, 1).reshape(4 * rows)
        )
        line = jnp.stack([order, opening], axis=2)
        line = jnp.pad(line, ((0, 0), (0, 0), (0, LANES - 2)))
        column = jnp.broadcast_to(order[:, None, :], (4, 8, rows))
        u_far_rest, a_rest, a_far, dd, c_own, c_got, n_got_second, tables, line, column = sync(
            u_far_rest, a_rest, a_far, dd, c_own, c_got, n_got_second, tables, line, column
        )
        d_rest = w_top(dd)
        d_far = swap(dd, Y_BIT)
        a_far_rest = g_swap_y(a_rest)
        c_pair = jnp.concatenate([c_own, c_got])
        c_second = swap_mixed(c_pair, (X_BIT, ZL_BIT))
        c_got_pair = swap_core(c_pair)
        normed = join(straight, n_pair, n_second, n_got_pair, n_got_second)
        my_up_bias = lax.dynamic_slice_in_dim(up_bias, block * hid, hid, 0).astype(F32)
        up_w = [w for w in (uu, u_rest, u_far, u_far_rest) if w is not None]
        act, slope = up_project(normed, my_up_bias, up_w)
        d_rest, d_far, a_far_rest, c_second, c_got_pair, normed, act, slope = sync(
            d_rest, d_far, a_far_rest, c_second, c_got_pair, normed, act, slope
        )
        d_far_rest = g_swap_y(d_rest)
        c_got_second = swap_core(c_second)
        cot = join(crossed, c_pair, c_second, c_got_pair, c_got_second)
        gd = weight_grads(unit, (0, 1, 2, 3), (cot, act))
        d_far_rest, cot, gd = sync(d_far_rest, cot, gd)
        d_a = g_swap_y(gd[0])
        my_qkv_bias = lax.dynamic_slice_in_dim(qkv_bias, block * att, att, 1).astype(F32)
        att_w = [w for w in (aa, a_rest, a_far, a_far_rest) if w is not None]
        attended, qkv_g, qkv_sums = attention(
            normed, cot, my_qkv_bias, tables, line, column, att_w
        )
        d_a, gd, attended, qkv_g, d_far_rest = sync(d_a, gd, attended, qkv_g, d_far_rest)
        d_z1, d_z2 = top_send(gd[2], d_a)
        d_z1 = g_top(d_z1)
        d_b = swap(gd[1], Y_BIT)
        ga = weight_grads(unit, (0, 1, 2), (normed, qkv_g), (cot, attended))
        gd_own = gd[3]
        down_w = [w for w in (dd, d_rest, d_far, d_far_rest) if w is not None]
        b_send = pair_dot(1, core, act, down_w, attended, att_w, 3 * att)
        d_z1, d_z2, d_b, ga, gd_own, b_send, cot, slope, act, attended = sync(
            d_z1, d_z2, d_b, ga, gd_own, b_send, cot, slope, act, attended
        )
        d_z2 = g_top(d_z2)
        a_a = g_swap_y(ga[0])
        b_got = swap_core(b_send)
        d_l = swap(g_far(gd_own, d_b, d_z1), ZL_BIT)
        up_g, up_sums = up_gradient(cot, slope, down_w)
        n_send = pair_dot(1, 1 - core, up_g, up_w, qkv_g, att_w, 0)
        b_far = pair_dot(0, 1 - core, act, down_w, attended, att_w, 3 * att, b_got, 2, 2)
        d_z2, a_a, ga, b_got, b_far, d_l, up_g, n_send, act, attended = sync(
            d_z2, a_a, ga, b_got, b_far, d_l, up_g, n_send, act, attended
        )
        a_z1, a_z2 = top_send(ga[2], a_a)
        a_z1 = g_top(a_z1)
        a_b = swap(ga[1], Y_BIT)
        n_got = swap_core(n_send)
        b_second = swap_mixed(b_far, first_way)
        (gu_a,) = weight_grads(unit, (0,), (normed, up_g))
        n_far = pair_dot(0, core, up_g, up_w, qkv_g, att_w, 0, n_got, 2, 2)
        b_near = pair_dot(0, 1 - core, act, down_w, attended, att_w, 3 * att, b_got, 0, 2)
        a_z1, a_z2, a_b, gu_a, n_got, n_far, b_near, b_second, up_g, qkv_g = sync(
            a_z1, a_z2, a_b, gu_a, n_got, n_far, b_near, b_second, up_g, qkv_g
        )
        a_z2 = g_top(a_z2)
        u_a = g_swap_y(gu_a)
        n_second = swap_mixed(n_far, second_way)
        gu = weight_grads(unit, (1, 2), (normed, up_g))
        n_near = pair_dot(0, core, up_g, up_w, qkv_g, att_w, 0, n_got, 0, 2)
        (ga_own,) = weight_grads(unit, (3,), (normed, qkv_g), (cot, attended))
        a_l = g_far(ga_own, a_b, a_z1)
        biases = jnp.concatenate([qkv_sums[0], up_sums[0]])
        spread = lax.dynamic_update_slice(
            jnp.zeros((4, biases.shape[0]), F32), biases[None], (block, 0)
        )
        a_z2, u_a, gu, ga_own, a_l, n_second, n_near, b_near, b_second, d_l, up_g, normed = sync(
            a_z2, u_a, gu, ga_own, a_l, n_second, n_near, b_near, b_second, d_l, up_g, normed
        )
        spread = sync(spread, a_z2)[0]
        u_z1, u_z2 = top_send(gu[1], u_a)
        u_z1 = g_top(u_z1)
        u_b = swap(gu[0], Y_BIT)
        n_first = near_side(n_near, n_second, first_way)
        b_first = near_side(b_near, b_second, second_way)
        a_l = swap(a_l, ZL_BIT)
        (gu_own,) = weight_grads(unit, (3,), (normed, up_g))
        d_x = g_cross(g_near(gd_own, d_b, d_z1, d_z2), d_l)
        a_near = g_near(ga_own, a_b, a_z1, a_z2)
        u_z1, u_z2, u_b, n_first, b_first, a_l, gu_own, d_x, a_near = sync(
            u_z1, u_z2, u_b, n_first, b_first, a_l, gu_own, d_x, a_near
        )
        u_z2 = g_top(u_z2)
        u_l = swap(g_far(gu_own, u_b, u_z1), ZL_BIT)
        d_x = g_x(d_x)
        a_x = g_x(g_cross(a_near, a_l))
        input_grad = norm_backward(n_near, n_second, n_first)
        result = finish(b_near, b_second, b_first)
        u_z2, u_l, d_x, a_x, input_grad, result, spread = sync(
            u_z2, u_l, d_x, a_x, input_grad, result, spread
        )
        gu = g_x(g_cross(g_near(gu_own, u_b, u_z1, u_z2), u_l))
        input_other = swap_core(input_grad)
        result_other = swap_core(result)
        result = place_halves(core, result, result_other, cost=8 * result.size)
        lines = input_grad[half : half + 3] + input_other[half : half + 3]
        lines = jnp.concatenate([lines.reshape(-1), spread.reshape(-1)])
        input_grad = place_halves(core, input_grad, input_other, rows=half, cost=16 * half * width)
        lines = sum_over(lines, [Y_BIT] + top_bits)
        lines, result, input_grad = sync(lines, result, input_grad)
        lines = sum_over(lines, [X_BIT, ZL_BIT])
        ga = ordered(x_mine, *a_x, 1)
        gd = ordered(x_mine, *d_x, 1)
        gu = ordered(x_mine, *gu, 1)

        gdown = gd.astype(F32).T
        gup = gu.astype(F32)
        ga = ga.reshape(share, 4, 4 * att)
        gqkv = ga[..., : 3 * att].astype(F32)
        gqkv = gqkv.reshape(share, 4, 3, att).swapaxes(1, 2).reshape(share, 3, 4 * att)
        gout = ga[..., 3 * att :].astype(F32).reshape(share, 4 * att).T
        biases = lines[3 * width :].reshape(4, 3 * att + hid)
        qkv_b = biases[:, : 3 * att].reshape(4, 3, att).swapaxes(0, 1).reshape(3, 4 * att)
        up_b = biases[:, 3 * att :].reshape(4 * hid)
        return (
            result,
            input_grad,
            lines[:width],
            lines[width : 2 * width],
            gqkv,
            qkv_b,
            gout,
            gup,
            up_b,
            gdown,
            lines[2 * width : 3 * width],
        )

    return local


def solution(mesh):
    return jax.shard_map(
        local_part(mesh.shape["dp"]),
        mesh=mesh,
        in_specs=(
            P("dp", None),
            P("dp"),
            P(),
            P(),
            P("dp", None, "tensor"),
            P(None, "tensor"),
            P("tensor", "dp"),
            P("dp", "tensor"),
            P("tensor"),
            P("tensor", "dp"),
            P(),
            P("dp", None),
        ),
        out_specs=(
            P("dp", None),
            P("dp", None),
            P(),
            P(),
            P("dp", None, "tensor"),
            P(None, "tensor"),
            P("tensor", "dp"),
            P("dp", "tensor"),
            P("tensor"),
            P("tensor", "dp"),
            P(),
        ),
        check_vma=False,
    )
```

```python
import functools

import jax
import jax.numpy as jnp
from jax import lax
from jax.experimental import pallas as pl
from jax.experimental.pallas import tpu as pltpu
from jax.sharding import PartitionSpec as P

HEAD_DIM = 64
ROT_DIM = 32
LANES = 128
NEGATIVE = -1e30
EPSILON = 1e-05
GELU_A = 0.7978845608028654
GELU_B = 0.044715
X_BIT, Y_BIT, ZL_BIT = 0, 1, 2
BF = jnp.bfloat16
F32 = jnp.float32


def dot_nn(a, b):
    return jnp.dot(a, b, preferred_element_type=F32)


def dot_nt(a, b):
    return lax.dot_general(a, b, (((1,), (1,)), ((), ())), preferred_element_type=F32)


def dot_tn(a, b):
    return lax.dot_general(a, b, (((0,), (0,)), ((), ())), preferred_element_type=F32)


def call(kernel, outs, grid, in_specs, out_specs, *operands, prefetch=0, cost=1000):
    return pl.pallas_call(
        kernel,
        out_shape=outs,
        grid_spec=pltpu.PrefetchScalarGridSpec(
            num_scalar_prefetch=prefetch, grid=grid, in_specs=in_specs, out_specs=out_specs
        ),
        compiler_params=pltpu.CompilerParams(vmem_limit_bytes=54 * 1024 * 1024),
        cost_estimate=pl.CostEstimate(flops=1000, bytes_accessed=cost, transcendentals=0),
    )(*operands)


def resident(value):
    return pl.BlockSpec(value.shape, lambda *_: (0,) * value.ndim)


def wide_dot(rows, refs, cols):
    total, low = None, 0
    for ref in refs:
        high = low + ref.shape[0]
        term = dot_nn(rows[:, low:high], ref[:, cols])
        total = term if total is None else total + term
        low = high
    return total


def sum_kernel(*refs):
    total = refs[0][...].astype(F32)
    for ref in refs[1:-1]:
        total = total + ref[...].astype(F32)
    refs[-1][...] = total.astype(BF)


def sum_rows(rows, *terms, tile=128):
    width = terms[0][0].shape[1]
    tile = min(tile, rows)

    def spec(start):
        return pl.BlockSpec((tile, width), lambda i: (start // tile + i, 0))

    return call(
        sum_kernel,
        jax.ShapeDtypeStruct((rows, width), BF),
        (rows // tile,),
        [spec(start) for _, start in terms],
        spec(0),
        *[value for value, _ in terms],
    )


def half_kernel(_, *refs):
    sum_kernel(*refs)


def half_sum(which, wholes, halves=(), steps=2):
    rows, cols = wholes[0].shape[0] // 2, wholes[0].shape[1]
    tile = rows // steps
    plain = pl.BlockSpec((tile, cols), lambda i, f: (i, 0))
    picked = pl.BlockSpec((tile, cols), lambda i, f: (f[0] * steps + i, 0))
    return call(
        half_kernel,
        jax.ShapeDtypeStruct((rows, cols), BF),
        (steps,),
        [picked] * len(wholes) + [plain] * len(halves),
        plain,
        which.reshape(1).astype(jnp.int32),
        *wholes,
        *halves,
        prefetch=1,
    )


def cross_kernel(flags_ref, own_ref, got_ref, send_ref, kept_ref):
    cols = own_ref.shape[1]
    for n, out_ref in enumerate((send_ref, kept_ref)):

        @pl.when(pl.program_id(0) == n)
        def _(out_ref=out_ref):
            for ref, place in ((own_ref, flags_ref[0]), (got_ref, 1 - flags_ref[0])):
                out_ref[:, pl.ds(pl.multiple_of(place * cols, cols), cols)] = ref[...]


def cross(zl, x, own, got):
    rows, cols = own.shape[0] // 2, own.shape[1]
    out = jax.ShapeDtypeStruct((rows, 2 * cols), BF)
    picked = pl.BlockSpec((rows, cols), lambda i, f: (jnp.where(i == 0, 1 - f[1], f[1]), 0))
    return call(
        cross_kernel,
        [out, out],
        (2,),
        [picked, picked],
        [pl.BlockSpec((rows, 2 * cols), lambda i, f: (0, 0))] * 2,
        jnp.stack([zl, x]).astype(jnp.int32),
        own,
        got,
        prefetch=1,
    )


def join_kernel(flags_ref, *refs):
    i = pl.program_id(0)
    place = lax.rem(i, 4)
    for own in range(2):
        swapped = (flags_ref[own] == 1) & (place > 0) & (place < 3)
        block = jnp.where(swapped, 3 - place, place)
        for n in range(4):
            ref = refs[2 * own + n // 2]
            half = ref.shape[0] // 2

            @pl.when((i // 4 == own) & (block == n))
            def _(ref=ref, low=(n % 2) * half, half=half):
                refs[-1][...] = ref[low : low + half, :]


def join(flags, pair, second, got_pair, got_second):
    half, width = pair.shape[0] // 2, pair.shape[1]
    arrays = (pair, second, got_pair, got_second)
    return call(
        join_kernel,
        jax.ShapeDtypeStruct((8 * half, width), pair.dtype),
        (8,),
        [resident(value) for value in arrays],
        pl.BlockSpec((half, width), lambda i, f: (i, 0)),
        flags,
        *arrays,
        prefetch=1,
    )


def stack_kernel(*refs):
    for n, ref in enumerate(refs[:-1]):

        @pl.when(pl.program_id(0) == n)
        def _(ref=ref):
            refs[-1][...] = ref[...]


def stack_rows(*blocks):
    rows, width = blocks[0].shape
    return call(
        stack_kernel,
        jax.ShapeDtypeStruct((len(blocks) * rows, width), blocks[0].dtype),
        (len(blocks),),
        [resident(value) for value in blocks],
        pl.BlockSpec((rows, width), lambda i: (i, 0)),
        *blocks,
    )


def place_kernel(core_ref, own_ref, other_ref, out_ref):
    steps = pl.num_programs(0) // 2

    @pl.when(pl.program_id(0) < steps)
    def _():
        out_ref[...] = own_ref[...]

    @pl.when(pl.program_id(0) >= steps)
    def _():
        out_ref[...] = other_ref[...]


def place_halves(core, own, other, steps=2, rows=None, cost=1000):
    rows, width = rows or own.shape[0], own.shape[1]
    tile = rows // steps
    return call(
        place_kernel,
        jax.ShapeDtypeStruct((2 * rows, width), own.dtype),
        (2 * steps,),
        [
            pl.BlockSpec((tile, width), lambda i, c: (jnp.minimum(i, steps - 1), 0)),
            pl.BlockSpec((tile, width), lambda i, c: (jnp.maximum(i - steps, 0), 0)),
        ],
        pl.BlockSpec((tile, width), lambda i, c: (lax.rem(i + steps * c[0], 2 * steps), 0)),
        core.reshape(1).astype(jnp.int32),
        own,
        other,
        prefetch=1,
        cost=cost,
    )


def up_kernel(rows_ref, bias_ref, *refs, chunk):
    weights, act_ref, slope_ref = refs[:-2], refs[-2], refs[-1]
    rows = rows_ref[...]
    for low in range(0, act_ref.shape[1], chunk):
        cols = slice(low, low + chunk)
        u = wide_dot(rows, weights, cols) + bias_ref[:, cols]
        squared = u * u
        gate = 0.5 + 0.5 * jnp.tanh(u * (GELU_A + GELU_A * GELU_B * squared))
        act = u * gate
        act_ref[:, cols] = act.astype(BF)
        slope = gate + act * (1.0 - gate) * (2.0 * GELU_A + 6.0 * GELU_A * GELU_B * squared)
        slope_ref[:, cols] = slope.astype(BF)


def up_project(rows, bias, weights, tile=256):
    count, hid = rows.shape[0], weights[0].shape[1]
    out = jax.ShapeDtypeStruct((count, hid), BF)
    block = pl.BlockSpec((tile, hid), lambda i: (i, 0))
    return call(
        functools.partial(up_kernel, chunk=256),
        [out, out],
        (count // tile,),
        [pl.BlockSpec((tile, rows.shape[1]), lambda i: (i, 0)), pl.BlockSpec((1, hid), lambda i: (0, 0))]
        + [resident(w) for w in weights],
        [block, block],
        rows,
        bias.reshape(1, hid),
        *weights,
    )


def add_row_sum(sum_ref, value):
    @pl.when(pl.program_id(0) == 0)
    def _():
        sum_ref[...] = jnp.zeros_like(sum_ref)

    sum_ref[0:1, :] += jnp.sum(value.astype(F32), axis=0, keepdims=True)


def up_grad_kernel(rows_ref, slope_ref, *refs):
    weights, grad_ref, sum_ref = refs[:-2], refs[-2], refs[-1]
    grad = wide_dot(rows_ref[...], weights, slice(None)) * slope_ref[...].astype(F32)
    grad = grad.astype(BF)
    grad_ref[...] = grad
    add_row_sum(sum_ref, grad)


def up_gradient(rows, slope, weights, tile=256):
    count, hid = slope.shape
    block = pl.BlockSpec((tile, hid), lambda i: (i, 0))
    return call(
        up_grad_kernel,
        [jax.ShapeDtypeStruct((count, hid), BF), jax.ShapeDtypeStruct((8, hid), F32)],
        (count // tile,),
        [pl.BlockSpec((tile, rows.shape[1]), lambda i: (i, 0)), block]
        + [resident(w) for w in weights],
        [block, pl.BlockSpec((8, hid), lambda i: (0, 0))],
        rows,
        slope,
        *weights,
    )


def weight_grad_kernel(terms, starts, *refs):
    outs = refs[2 * terms :]
    for n, out_ref in enumerate(outs):

        @pl.when((pl.program_id(0) >= starts[n]) & (pl.program_id(0) < starts[n + 1]))
        def _(out_ref=out_ref):
            low = 0
            for t in range(terms):
                value = dot_tn(refs[2 * t][...], refs[2 * t + 1][...])
                out_ref[:, low : low + value.shape[1]] = value.astype(BF)
                low = low + value.shape[1]


def weight_grads(unit, parts, *pairs):
    width = pairs[0][0].shape[1]
    cols = sum(right.shape[1] for _, right in pairs)
    tops = width // unit // 2
    every = ((tops + 1, tops - 1), (tops, 1), (1, tops - 1), (0, 1))
    sizes = [every[part][1] for part in parts]
    starts = [sum(sizes[:n]) for n in range(len(sizes) + 1)]

    def left_block(i):
        place = i
        for n, part in enumerate(parts):
            place = jnp.where(i >= starts[n], i - starts[n] + every[part][0], place)
        return 0, place

    in_specs, operands = [], []
    for left, right in pairs:
        in_specs.append(pl.BlockSpec((left.shape[0], unit), left_block))
        in_specs.append(resident(right))
        operands += [left, right]

    def out_block(n):
        return lambda i: (jnp.clip(i - starts[n], 0, sizes[n] - 1), 0)

    return call(
        functools.partial(weight_grad_kernel, len(pairs), starts),
        [jax.ShapeDtypeStruct((size * unit, cols), BF) for size in sizes],
        (starts[-1],),
        in_specs,
        [pl.BlockSpec((unit, cols), out_block(n)) for n in range(len(sizes))],
        *operands,
    )


def pair_kernel(pieces, adding, _, a_ref, c_ref, *refs):
    a, c, out_ref = a_ref[...], c_ref[...], refs[-1]
    low = 0
    for b_ref, d_ref in zip(refs[:pieces], refs[pieces : 2 * pieces]):
        high = low + b_ref.shape[0]
        total = dot_nt(a, b_ref[...]) + dot_nt(c, d_ref[...])
        if adding:
            total = total + refs[2 * pieces][:, low:high].astype(F32)
        out_ref[:, low:high] = total.astype(BF)
        low = high


def pair_dot(part, crossed, a, b, c, d, cut, got=None, begin=0, count=4):
    tile, width = a.shape[0] // 8, sum(piece.shape[0] for piece in b)
    extra = [] if got is None else [got]

    def row_block(i, f):
        i = i + begin
        return part * 4 + jnp.where((f[0] == 1) & (i > 0) & (i < 3), 3 - i, i), 0

    return call(
        functools.partial(pair_kernel, len(b), len(extra)),
        jax.ShapeDtypeStruct((count * tile, width), BF),
        (count,),
        [pl.BlockSpec((tile, a.shape[1]), row_block), pl.BlockSpec((tile, c.shape[1]), row_block)]
        + [resident(w) for w in b]
        + [pl.BlockSpec((w.shape[0], c.shape[1]), lambda i, f: (0, cut // c.shape[1])) for w in d]
        + [pl.BlockSpec((tile, width), lambda i, f: (i + begin, 0))] * len(extra),
        pl.BlockSpec((tile, width), lambda i, f: (i, 0)),
        crossed.reshape(1).astype(jnp.int32),
        a,
        c,
        *b,
        *d,
        *extra,
        prefetch=1,
    )


def attention_kernel(
    rows_ref, cot_ref, bias_ref, cos_ref, left_ref, right_ref, line_ref, column_ref, *refs
):
    weights, (out_ref, dpre_ref, sum_ref) = refs[:-3], refs[-3:]
    half, width = out_ref.shape[2:]
    rows = 2 * half
    scaling = HEAD_DIM ** (-0.5)

    def both(ref):
        return ref[:, 0].reshape(rows, ref.shape[3])

    cos, left, right = both(cos_ref), both(left_ref), both(right_ref)
    normed, cot = both(rows_ref), both(cot_ref)
    head_of = lax.broadcasted_iota(jnp.int32, (rows, LANES), 1) // HEAD_DIM

    def turn(v, sign):
        ahead = pltpu.roll(v, LANES - ROT_DIM // 2, 1)
        behind = pltpu.roll(v, ROT_DIM // 2, 1)
        return v * cos + sign * (ahead * left + behind * right)

    line, column = line_ref[0], column_ref[0]
    allowed = (line[:, 0:1] >= column[0:1]) & (line[:, 1:2] <= column[0:1])
    pre = wide_dot(normed, weights, slice(0, 3 * width)) + bias_ref[...]
    grads = wide_dot(cot, weights, slice(3 * width, 4 * width)).astype(BF)
    dpre_all = [None] * (3 * width // LANES)
    for pair in range(width // LANES):
        parts = [slice(b + pair * LANES, b + (pair + 1) * LANES) for b in (0, width, 2 * width)]
        q = turn(pre[:, parts[0]], 1.0).astype(BF)
        k = turn(pre[:, parts[1]], 1.0).astype(BF)
        v = pre[:, parts[2]].astype(BF)
        g = grads[:, parts[0]]
        att = dq = dk = dv = None
        for h in range(LANES // HEAD_DIM):
            mine = head_of == h
            qh = jnp.where(mine, q, 0).astype(BF)
            gh = jnp.where(mine, g, 0).astype(BF)
            s = jnp.where(allowed, dot_nt(qh, k) * scaling, NEGATIVE)
            e = jnp.exp(s - jnp.max(s, axis=-1, keepdims=True))
            p = e * (1.0 / jnp.sum(e, axis=-1, keepdims=True))
            low = p.astype(BF)
            att_h = dot_nn(low, v)
            dp = dot_nt(gh, v)
            inner = jnp.sum(p * dp, axis=-1, keepdims=True)
            ds = (p * (dp - inner)).astype(BF)
            dq_h = dot_nn(ds, k)
            dk_h = dot_tn(ds, qh)
            dv_h = dot_tn(low, gh)
            att = att_h if h == 0 else jnp.where(mine, att_h, att)
            dq = dq_h if h == 0 else jnp.where(mine, dq_h, dq)
            dk = dk_h if h == 0 else dk + dk_h
            dv = dv_h if h == 0 else dv + dv_h
        out_ref[:, 0, :, parts[0]] = att.astype(BF).reshape(2, half, LANES)
        for n, value in enumerate((turn(dq * scaling, -1.0), turn(dk * scaling, -1.0), dv)):
            value = value.astype(BF)
            dpre_ref[:, 0, :, parts[n]] = value.reshape(2, half, LANES)
            dpre_all[parts[n].start // LANES] = value
    add_row_sum(sum_ref, jnp.concatenate(dpre_all, axis=1))


def attention(normed, cot, bias, tables, line, column, weights):
    count, rows = column.shape[0], column.shape[2]
    half, width = rows // 2, weights[0].shape[1] // 4

    def split(value):
        return value.reshape(2, count, half, value.shape[1])

    def block(cols):
        return pl.BlockSpec((2, 1, half, cols), lambda s: (0, s, 0, 0))

    attended, dpre, sums = call(
        attention_kernel,
        [
            jax.ShapeDtypeStruct((2, count, half, width), BF),
            jax.ShapeDtypeStruct((2, count, half, 3 * width), BF),
            jax.ShapeDtypeStruct((8, 3 * width), F32),
        ],
        (count,),
        [
            block(normed.shape[1]),
            block(cot.shape[1]),
            pl.BlockSpec((1, 3 * width), lambda s: (0, 0)),
            block(LANES),
            block(LANES),
            block(LANES),
            pl.BlockSpec((1, rows, LANES), lambda s: (s, 0, 0)),
            pl.BlockSpec((1, 8, rows), lambda s: (s, 0, 0)),
        ]
        + [resident(w) for w in weights],
        [block(width), block(3 * width), pl.BlockSpec((8, 3 * width), lambda s: (0, 0))],
        split(normed),
        split(cot),
        bias.reshape(1, 3 * width),
        *[split(t) for t in tables],
        line,
        column,
        *weights,
    )
    tokens = 2 * count * half
    return attended.reshape(tokens, width), dpre.reshape(tokens, 3 * width), sums


def rotary_lanes(places):
    halfway = ROT_DIM // 2
    lane = jnp.arange(LANES, dtype=jnp.int32) % HEAD_DIM
    freqs = 10000.0 ** (-(lane % halfway).astype(F32) * 2.0 / ROT_DIM)
    angles = places.astype(F32)[:, None] * freqs[None, :]
    turned = lane < ROT_DIM
    cos = jnp.where(turned, jnp.cos(angles), 1.0)
    sin = jnp.where(turned, jnp.sin(angles), 0.0)
    return cos, jnp.where(lane < halfway, -sin, 0.0), jnp.where(lane >= halfway, sin, 0.0)


def standardize(inputs):
    average = jnp.mean(inputs, axis=-1, keepdims=True)
    centered = inputs - average
    inv_std = lax.rsqrt(jnp.mean(centered * centered, axis=-1, keepdims=True) + EPSILON)
    return centered * inv_std, inv_std


def input_gradient(normed_grad, cot, normal_x, inv_std, gain):
    scaled = normed_grad * gain
    return cot + inv_std * (
        scaled
        - jnp.mean(scaled, axis=-1, keepdims=True)
        - normal_x * jnp.mean(scaled * normal_x, axis=-1, keepdims=True)
    )


def norm_kernel(table_ref, tok_ref, cot_ref, gain_ref, shift_ref, normed_ref, mixed_ref, *, cols):
    normal_x, _ = standardize(tok_ref[...].astype(F32))
    normed = (normal_x * gain_ref[...].astype(F32) + shift_ref[...].astype(F32)).astype(BF)
    for n in range(tok_ref.shape[1] // cols):
        target = pl.ds(pl.multiple_of(table_ref[n], cols), cols)
        normed_ref[:, target] = normed[:, n * cols : (n + 1) * cols]
        mixed_ref[:, target] = cot_ref[:, n * cols : (n + 1) * cols]


def natural(table_ref, refs, cols):
    parts = []
    for n in range(refs[0].shape[1] // cols):
        source = pl.ds(pl.multiple_of(table_ref[n], cols), cols)
        total = refs[0][:, source].astype(F32)
        for ref in refs[1:]:
            total = total + ref[:, source].astype(F32)
        parts.append(total)
    return jnp.concatenate(parts, axis=1)


def norm_back_kernel(table_ref, tok_ref, cot_ref, gain_ref, *refs, cols):
    pieces, (grad_ref, lines_ref) = refs[:-2], refs[-2:]
    i, last_tile = pl.program_id(0), pl.num_programs(0) - 1

    @pl.when(i == 0)
    def _():
        lines_ref[...] = jnp.zeros_like(lines_ref)

    @pl.when(i == last_tile)
    def _():
        grad_ref[...] = jnp.zeros_like(grad_ref)
        grad_ref[0:8, :] = lines_ref[...]

    @pl.when(i < last_tile)
    def _():
        normal_x, inv_std = standardize(tok_ref[...].astype(F32))
        cot = cot_ref[...].astype(F32)
        normed_grad = natural(table_ref, pieces, cols)
        grad_ref[...] = input_gradient(
            normed_grad, cot, normal_x, inv_std, gain_ref[...].astype(F32)
        )
        for row, value in enumerate((normed_grad * normal_x, normed_grad, cot)):
            lines_ref[row : row + 1, :] += jnp.sum(value, axis=0, keepdims=True)


def result_kernel(table_ref, tok_ref, bias_ref, *refs, cols):
    pieces, out_ref = refs[:-1], refs[-1]
    branches = natural(table_ref, pieces, cols)
    out_ref[...] = (tok_ref[...].astype(F32) + branches + bias_ref[...].astype(F32)).astype(BF)


def on_half(kernel, table, cols, whole, lines, mine, outs, extra=0, scratch=(), tile=64):
    half, width = whole[0].shape[0] // 2, whole[0].shape[1]
    steps = half // tile
    last_entry = table.shape[0] - 1

    def row(i):
        return jnp.minimum(i, steps - 1)

    return pl.pallas_call(
        functools.partial(kernel, cols=cols),
        out_shape=outs,
        grid_spec=pltpu.PrefetchScalarGridSpec(
            num_scalar_prefetch=1,
            grid=(steps + extra,),
            in_specs=[pl.BlockSpec((tile, width), lambda i, t: (t[last_entry] * steps + row(i), 0))]
            * len(whole)
            + [pl.BlockSpec((1, width), lambda i, t: (0, 0))] * len(lines)
            + [pl.BlockSpec((tile, width), lambda i, t: (row(i), 0))] * len(mine),
            out_specs=[pl.BlockSpec((tile, width), lambda i, t: (i, 0))] * len(outs),
            scratch_shapes=list(scratch),
        ),
        compiler_params=pltpu.CompilerParams(vmem_limit_bytes=32 * 1024 * 1024),
        cost_estimate=pl.CostEstimate(flops=1000, bytes_accessed=1000, transcendentals=0),
    )(table, *whole, *[line.reshape(1, width) for line in lines], *mine)


def local_part(dp_size):
    top_bits = [b for b in range(3, dp_size.bit_length() - 1)]

    def swap(value, *bits):
        flip = sum(1 << bit for bit in bits)
        return lax.ppermute(value, "dp", [(i, i ^ flip) for i in range(dp_size)])

    def swap_core(value):
        return lax.ppermute(value, "tensor", [(0, 1), (1, 0)])

    def swap_mixed(value, bits):
        pairs = [(2 * i + c, 2 * (i ^ (1 << bits[c])) + c) for i in range(dp_size) for c in (0, 1)]
        return lax.ppermute(value, ("dp", "tensor"), pairs)

    def ordered(bit, own, other, axis):
        return jnp.where(
            bit == 0,
            jnp.concatenate([own, other], axis),
            jnp.concatenate([other, own], axis),
        )

    def part_of(value, index, axis):
        size = value.shape[axis] // 2
        return lax.dynamic_slice_in_dim(value, index * size, size, axis)

    def sync(*values):
        return lax.optimization_barrier(values)

    def local(
        tokens,
        segments,
        ln_gain,
        ln_shift,
        qkv_weight,
        qkv_bias,
        out_weight,
        up_weight,
        up_bias,
        down_weight,
        branch_bias,
        cotangent,
    ):
        rows, width = tokens.shape
        half = rows // 2
        wide = width // 2
        share = qkv_weight.shape[0]
        unit = 4 * share
        cols = 2 * share
        me = lax.axis_index("dp")
        core = lax.axis_index("tensor")
        x_mine, y_mine, zl_mine = (me >> X_BIT) & 1, (me >> Y_BIT) & 1, (me >> ZL_BIT) & 1
        block = 2 * x_mine + zl_mine
        att = qkv_weight.shape[2] // 4
        hid = up_weight.shape[1] // 4
        tops = 2 ** len(top_bits)

        n = jnp.arange(4 * tops, dtype=jnp.int32)
        table = ((((n & 1) ^ y_mine) * tops + ((n >> 2) ^ (me >> 3))) * 2 + ((n >> 1) & 1)) * cols
        table = jnp.concatenate([table, core.reshape(1)]).astype(jnp.int32)
        aligned = cols % LANES == 0

        def relative(split):
            for axis, bit in enumerate([Y_BIT] + top_bits[::-1]):
                split = jnp.where((me >> bit) & 1 == 1, jnp.flip(split, axis + 1), split)
            return split

        def to_mixed(value):
            count = value.shape[0]
            split = value.reshape(count, tops, 2, 2, cols).transpose(0, 3, 1, 2, 4)
            split = relative(split.reshape((count, 2) + (2,) * len(top_bits) + (unit,)))
            return split.reshape(count, width)

        def from_mixed(value):
            count = value.shape[0]
            split = relative(value.reshape((count, 2) + (2,) * len(top_bits) + (unit,)))
            split = split.reshape(count, 2, tops, 2, cols).transpose(0, 2, 3, 1, 4)
            return split.reshape(count, width)

        def my_rows(value):
            return lax.dynamic_slice_in_dim(value, core * half, half, 0)

        def norm_forward():
            shape = jax.ShapeDtypeStruct((half, width), BF)
            if aligned:
                return on_half(
                    norm_kernel,
                    table,
                    cols,
                    [tokens, cotangent],
                    [ln_gain, ln_shift],
                    [],
                    [shape, shape],
                )
            normal_x, _ = standardize(my_rows(tokens).astype(F32))
            normed = normal_x * ln_gain.astype(F32) + ln_shift.astype(F32)
            return to_mixed(normed.astype(BF)), to_mixed(my_rows(cotangent))

        def norm_backward(*pieces):
            if aligned:
                return on_half(
                    norm_back_kernel,
                    table,
                    cols,
                    [tokens, cotangent],
                    [ln_gain],
                    list(pieces),
                    [jax.ShapeDtypeStruct((half + 64, width), F32)],
                    extra=1,
                    scratch=[pltpu.VMEM((8, width), F32)],
                )[0]
            normal_x, inv_std = standardize(my_rows(tokens).astype(F32))
            cot = my_rows(cotangent).astype(F32)
            grad = from_mixed(add(*[piece[:half] for piece in pieces]))
            lines = [jnp.sum(v, axis=0, keepdims=True) for v in (grad * normal_x, grad, cot)]
            result = input_gradient(grad, cot, normal_x, inv_std, ln_gain.astype(F32))
            return jnp.concatenate([result] + lines + [jnp.zeros((61, width), F32)])

        def finish(*pieces):
            if aligned:
                return on_half(
                    result_kernel,
                    table,
                    cols,
                    [tokens],
                    [branch_bias],
                    list(pieces),
                    [jax.ShapeDtypeStruct((half, width), BF)],
                )[0]
            branches = from_mixed(add(*[piece[:half] for piece in pieces]))
            return (my_rows(tokens).astype(F32) + branches + branch_bias.astype(F32)).astype(BF)

        def w_x(piece):
            return part_of(piece, x_mine, 1), swap(part_of(piece, 1 - x_mine, 1), X_BIT)

        def w_zl(w):
            return part_of(w, zl_mine, 1), swap(part_of(w, 1 - zl_mine, 1), ZL_BIT)

        def w_place(pair):
            return place_halves(zl_mine, *pair, steps=1)

        def w_top(w):
            rest = None
            for bit in top_bits:
                mine = w if rest is None else jnp.concatenate([w, rest])
                got = swap(mine, bit)
                rest = got if rest is None else jnp.concatenate([rest, got])
            return rest

        def add(*values):
            total = values[0].astype(F32)
            for value in values[1:]:
                total = total + value.astype(F32)
            return total

        def top_send(kept, got):
            if tops > 2:
                return add(kept, got).astype(BF), None
            return half_sum(1 - zl_mine, (kept, got)), half_sum(zl_mine, (kept, got))

        def g_top(rest):
            if rest is None or tops == 2:
                return None if rest is None else swap(rest, top_bits[0])
            own = jnp.zeros((unit,) + rest.shape[1:], rest.dtype)
            grad = jnp.concatenate([own, rest])
            for bit in reversed(top_bits):
                cut = grad.shape[0] // 2
                grad = add(grad[:cut], swap(grad[cut:], bit)).astype(BF)
            return grad

        def g_far(kept, got, one):
            if tops > 2:
                return part_of(add(kept, got, one[:unit]).astype(BF), 1 - zl_mine, 0)
            return half_sum(1 - zl_mine, (kept, got), (one,))

        def g_near(kept, got, one, two):
            if tops > 2:
                return part_of(add(kept, got, one[:unit]).astype(BF), zl_mine, 0)
            return half_sum(zl_mine, (kept, got), (two,))

        def g_cross(own, got):
            return cross(zl_mine, x_mine, own, got)

        def g_x(split):
            return split[1], swap(split[0], X_BIT)

        def g_swap_y(value):
            return None if value is None else swap(value, Y_BIT)

        straight = jnp.zeros((2,), jnp.int32)
        crossed = jnp.stack([core, 1 - core]).astype(jnp.int32)

        first_way, second_way = (ZL_BIT, X_BIT), (X_BIT, ZL_BIT)

        def near_side(near, second, way):
            return swap_mixed(sum_rows(half, (near, half), (second, half)), way)

        def sum_over(value, bits):
            if len(bits) == 2:
                got = [swap(value, *way) for way in (bits[:1], bits[1:], bits)]
                return value + got[0] + (got[1] + got[2])
            for bit in bits:
                value = value + swap(value, bit)
            return value

        u_x = w_x(up_weight)
        n_own, c_own = norm_forward()
        seg = jnp.stack(
            [segments, swap(segments, ZL_BIT), swap(segments, X_BIT), swap(segments, X_BIT, ZL_BIT)]
        )
        u_x, c_own, seg, qkv_weight, out_weight, down_weight = sync(
            u_x, c_own, seg, qkv_weight, out_weight, down_weight
        )
        uu = w_place(w_zl(ordered(x_mine, *u_x, 0)))
        n_got = swap(n_own, ZL_BIT)
        qkv_piece = qkv_weight.reshape(share, 3, 4, att).swapaxes(1, 2).reshape(share, 4, 3 * att)
        out_piece = out_weight.T.reshape(share, 4, att)
        a_x = w_x(jnp.concatenate([qkv_piece, out_piece], axis=2).reshape(share, 16 * att))
        d_x = w_x(down_weight.T)
        uu, n_own, n_got, a_x, d_x, c_own, seg = sync(uu, n_own, n_got, a_x, d_x, c_own, seg)
        u_rest = w_top(uu)
        u_far = swap(uu, Y_BIT)
        n_pair = stack_rows(n_own, n_got)
        n_second = swap(n_pair, X_BIT)
        n_got_pair = swap_core(n_pair)
        aa = w_place(w_zl(ordered(x_mine, *a_x, 0)))
        dd = ordered(x_mine, *d_x, 0)
        u_rest, u_far, n_second, n_got_pair, aa, dd, c_own, seg = sync(
            u_rest, u_far, n_second, n_got_pair, aa, dd, c_own, seg
        )
        a_rest = w_top(aa)
        a_far = swap(aa, Y_BIT)
        u_far_rest = g_swap_y(u_rest)
        n_got_second = swap_core(n_second)
        dd = w_place(w_zl(dd))
        c_got = swap_mixed(c_own, (ZL_BIT, X_BIT))
        order = jnp.broadcast_to(jnp.arange(rows, dtype=jnp.int32), (4, rows))
        begins = jnp.concatenate([jnp.ones((4, 1), bool), seg[:, 1:] != seg[:, :-1]], axis=1)
        opening = lax.cummax(jnp.where(begins, order, 0), axis=1)

        def halves(value):
            return jnp.where(core == 0, value, jnp.roll(value, half, axis=1))

        order, opening = halves(order), halves(opening)
        tables = rotary_lanes(
            (order - opening).reshape(4, 2, half).swapaxes(0, 1).reshape(4 * rows)
        )
        line = jnp.stack([order, opening], axis=2)
        line = jnp.pad(line, ((0, 0), (0, 0), (0, LANES - 2)))
        column = jnp.broadcast_to(order[:, None, :], (4, 8, rows))
        u_far_rest, a_rest, a_far, dd, c_own, c_got, n_got_second, tables, line, column = sync(
            u_far_rest, a_rest, a_far, dd, c_own, c_got, n_got_second, tables, line, column
        )
        d_rest = w_top(dd)
        d_far = swap(dd, Y_BIT)
        a_far_rest = g_swap_y(a_rest)
        c_pair = stack_rows(c_own, c_got)
        c_second = swap_mixed(c_pair, (X_BIT, ZL_BIT))
        c_got_pair = swap_core(c_pair)
        normed = join(straight, n_pair, n_second, n_got_pair, n_got_second)
        my_up_bias = lax.dynamic_slice_in_dim(up_bias, block * hid, hid, 0).astype(F32)
        up_w = [w for w in (uu, u_rest, u_far, u_far_rest) if w is not None]
        act, slope = up_project(normed, my_up_bias, up_w)
        d_rest, d_far, a_far_rest, c_second, c_got_pair, normed, act, slope = sync(
            d_rest, d_far, a_far_rest, c_second, c_got_pair, normed, act, slope
        )
        d_far_rest = g_swap_y(d_rest)
        c_got_second = swap_core(c_second)
        cot = join(crossed, c_pair, c_second, c_got_pair, c_got_second)
        gd = weight_grads(unit, (0, 1, 2, 3), (cot, act))
        d_far_rest, cot, gd = sync(d_far_rest, cot, gd)
        d_a = g_swap_y(gd[0])
        my_qkv_bias = lax.dynamic_slice_in_dim(qkv_bias, block * att, att, 1).astype(F32)
        att_w = [w for w in (aa, a_rest, a_far, a_far_rest) if w is not None]
        attended, qkv_g, qkv_sums = attention(
            normed, cot, my_qkv_bias, tables, line, column, att_w
        )
        d_a, gd, attended, qkv_g, d_far_rest = sync(d_a, gd, attended, qkv_g, d_far_rest)
        d_z1, d_z2 = top_send(gd[2], d_a)
        d_z1 = g_top(d_z1)
        d_b = swap(gd[1], Y_BIT)
        ga = weight_grads(unit, (0, 1, 2), (normed, qkv_g), (cot, attended))
        gd_own = gd[3]
        down_w = [w for w in (dd, d_rest, d_far, d_far_rest) if w is not None]
        b_send = pair_dot(1, core, act, down_w, attended, att_w, 3 * att)
        d_z1, d_z2, d_b, ga, gd_own, b_send, cot, slope, act, attended = sync(
            d_z1, d_z2, d_b, ga, gd_own, b_send, cot, slope, act, attended
        )
        d_z2 = g_top(d_z2)
        a_a = g_swap_y(ga[0])
        b_got = swap_core(b_send)
        d_l = swap(g_far(gd_own, d_b, d_z1), ZL_BIT)
        up_g, up_sums = up_gradient(cot, slope, down_w)
        n_send = pair_dot(1, 1 - core, up_g, up_w, qkv_g, att_w, 0)
        b_far = pair_dot(0, 1 - core, act, down_w, attended, att_w, 3 * att, b_got, 2, 2)
        d_z2, a_a, ga, b_got, b_far, d_l, up_g, n_send, act, attended = sync(
            d_z2, a_a, ga, b_got, b_far, d_l, up_g, n_send, act, attended
        )
        a_z1, a_z2 = top_send(ga[2], a_a)
        a_z1 = g_top(a_z1)
        a_b = swap(ga[1], Y_BIT)
        n_got = swap_core(n_send)
        b_second = swap_mixed(b_far, first_way)
        (gu_a,) = weight_grads(unit, (0,), (normed, up_g))
        n_far = pair_dot(0, core, up_g, up_w, qkv_g, att_w, 0, n_got, 2, 2)
        b_near = pair_dot(0, 1 - core, act, down_w, attended, att_w, 3 * att, b_got, 0, 2)
        a_z1, a_z2, a_b, gu_a, n_got, n_far, b_near, b_second, up_g, qkv_g = sync(
            a_z1, a_z2, a_b, gu_a, n_got, n_far, b_near, b_second, up_g, qkv_g
        )
        a_z2 = g_top(a_z2)
        u_a = g_swap_y(gu_a)
        n_second = swap_mixed(n_far, second_way)
        gu = weight_grads(unit, (1, 2), (normed, up_g))
        n_near = pair_dot(0, core, up_g, up_w, qkv_g, att_w, 0, n_got, 0, 2)
        (ga_own,) = weight_grads(unit, (3,), (normed, qkv_g), (cot, attended))
        a_l = g_far(ga_own, a_b, a_z1)
        biases = jnp.concatenate([qkv_sums[0], up_sums[0]])
        spread = lax.dynamic_update_slice(
            jnp.zeros((4, biases.shape[0]), F32), biases[None], (block, 0)
        )
        a_z2, u_a, gu, ga_own, a_l, n_second, n_near, b_near, b_second, d_l, up_g, normed = sync(
            a_z2, u_a, gu, ga_own, a_l, n_second, n_near, b_near, b_second, d_l, up_g, normed
        )
        spread = sync(spread, a_z2)[0]
        u_z1, u_z2 = top_send(gu[1], u_a)
        u_z1 = g_top(u_z1)
        u_b = swap(gu[0], Y_BIT)
        n_first = near_side(n_near, n_second, first_way)
        b_first = near_side(b_near, b_second, second_way)
        a_l = swap(a_l, ZL_BIT)
        (gu_own,) = weight_grads(unit, (3,), (normed, up_g))
        d_x = g_cross(g_near(gd_own, d_b, d_z1, d_z2), d_l)
        a_near = g_near(ga_own, a_b, a_z1, a_z2)
        u_z1, u_z2, u_b, n_first, b_first, a_l, gu_own, d_x, a_near = sync(
            u_z1, u_z2, u_b, n_first, b_first, a_l, gu_own, d_x, a_near
        )
        u_z2 = g_top(u_z2)
        u_l = swap(g_far(gu_own, u_b, u_z1), ZL_BIT)
        d_x = g_x(d_x)
        a_x = g_x(g_cross(a_near, a_l))
        input_grad = norm_backward(n_near, n_second, n_first)
        result = finish(b_near, b_second, b_first)
        u_z2, u_l, d_x, a_x, input_grad, result, spread = sync(
            u_z2, u_l, d_x, a_x, input_grad, result, spread
        )
        gu = g_x(g_cross(g_near(gu_own, u_b, u_z1, u_z2), u_l))
        input_other = swap_core(input_grad)
        result_other = swap_core(result)
        result = place_halves(core, result, result_other, cost=8 * result.size)
        lines = input_grad[half : half + 3] + input_other[half : half + 3]
        lines = jnp.concatenate([lines.reshape(-1), spread.reshape(-1)])
        input_grad = place_halves(core, input_grad, input_other, rows=half, cost=16 * half * width)
        lines = sum_over(lines, [Y_BIT] + top_bits)
        lines, result, input_grad = sync(lines, result, input_grad)
        lines = sum_over(lines, [X_BIT, ZL_BIT])
        ga = ordered(x_mine, *a_x, 1)
        gd = ordered(x_mine, *d_x, 1)
        gu = ordered(x_mine, *gu, 1)

        gdown = gd.astype(F32).T
        gup = gu.astype(F32)
        ga = ga.reshape(share, 4, 4 * att)
        gqkv = ga[..., : 3 * att].astype(F32)
        gqkv = gqkv.reshape(share, 4, 3, att).swapaxes(1, 2).reshape(share, 3, 4 * att)
        gout = ga[..., 3 * att :].astype(F32).reshape(share, 4 * att).T
        biases = lines[3 * width :].reshape(4, 3 * att + hid)
        qkv_b = biases[:, : 3 * att].reshape(4, 3, att).swapaxes(0, 1).reshape(3, 4 * att)
        up_b = biases[:, 3 * att :].reshape(4 * hid)
        return (
            result,
            input_grad,
            lines[:width],
            lines[width : 2 * width],
            gqkv,
            qkv_b,
            gout,
            gup,
            up_b,
            gdown,
            lines[2 * width : 3 * width],
        )

    return local


def solution(mesh):
    return jax.shard_map(
        local_part(mesh.shape["dp"]),
        mesh=mesh,
        in_specs=(
            P("dp", None),
            P("dp"),
            P(),
            P(),
            P("dp", None, "tensor"),
            P(None, "tensor"),
            P("tensor", "dp"),
            P("dp", "tensor"),
            P("tensor"),
            P("tensor", "dp"),
            P(),
            P("dp", None),
        ),
        out_specs=(
            P("dp", None),
            P("dp", None),
            P(),
            P(),
            P("dp", None, "tensor"),
            P(None, "tensor"),
            P("tensor", "dp"),
            P("dp", "tensor"),
            P("tensor"),
            P("tensor", "dp"),
            P(),
        ),
        check_vma=False,
    )
```
